32 devices in a mesh: dp: 8 (over z, core), expert: 4 (over y, x).
Axes of the slice: x: 2, y: 2, z: 4, core: 2. Of those that a mesh axis runs over, the one named last changes fastest.
Arguments:
- tokens: bfloat16 [2, 8, 256, 2048], P(None, 'dp', 'expert'), may hold values from -6 to 6
- lengths: int32 [2, 8], P(None, 'dp'), may hold values from 193 to 256, as said below
- attention_routes: int32 [2, 8, 256, 2], P(None, 'dp', 'expert'), may hold values from 0 to 7, all different within a row; in each aligned block of 64 rows (0 to 63, 64 to 127, ..., all dimensions but the last counted through in order) at most 24 rows name the same one
- feedforward_routes: int32 [2, 8, 256, 2], P(None, 'dp', 'expert'), may hold values from 0 to 7, all different within a row; in each aligned block of 64 rows (0 to 63, 64 to 127, ..., all dimensions but the last counted through in order) at most 24 rows name the same one
- norm_gains: bfloat16 [2048, 2], P(('dp', 'expert')), may hold values from 0.5 to 1.5
- router_weight: bfloat16 [2048, 16], P(('dp', 'expert')), may hold values from -0.09375 to 0.09375
- key_value_weight: bfloat16 [2048, 4096], P(('dp', 'expert')), may hold values from -0.125 to 0.125
- query_weight: bfloat16 [8, 2048, 2048], P('expert', 'dp'), may hold values from -0.125 to 0.125
- output_weight: bfloat16 [8, 2048, 2048], P('expert', 'dp'), may hold values from -0.75 to 0.75
- input_weight: bfloat16 [8, 2048, 11264], P('expert', 'dp'), may hold values from -0.125 to 0.125
- down_weight: bfloat16 [8, 5632, 2048], P('expert', 'dp'), may hold values from -0.15625 to 0.15625
- cotangent: bfloat16 [2, 8, 256, 2048], P(None, 'dp', 'expert'), may hold values from -6 to 6
Outputs:
- result: bfloat16 [2, 8, 256, 2048], P(None, 'dp', 'expert')
- grad_tokens: bfloat16 [2, 8, 256, 2048], P(None, 'dp', 'expert')
- grad_norm_gains: float32 [2048, 2], P(('dp', 'expert'))
- grad_router_weight: float32 [2048, 16], P(('dp', 'expert'))
- grad_key_value_weight: float32 [2048, 4096], P(('dp', 'expert'))
- grad_query_weight: float32 [8, 2048, 2048], P('expert', 'dp')
- grad_output_weight: float32 [8, 2048, 2048], P('expert', 'dp')
- grad_input_weight: float32 [8, 2048, 11264], P('expert', 'dp')
- grad_down_weight: float32 [8, 5632, 2048], P('expert', 'dp')
The draws below stay inside these ranges and needn't reach their ends.
Inputs may be any that keep to these rules, and one draw needn't show every extreme that they name: `lengths`: each row fills more than 192 slots; in every draw some row fills all 256. `attention_routes`: A slot's 2 experts differ. Among the 64 slots of one device in one micro-batch no expert is named more than 24 times, a bound that some block reaches. `feedforward_routes`: A slot's 2 experts differ. Among the 64 slots of one device in one micro-batch no expert is named more than 24 times, a bound that some block reaches.
All inputs are finite; a program needn't handle non-finite values.
Results may differ from the reference program's by a relative error of at most 0.02.
Values may be sent and summed in bfloat16 or wider, within the bound.
A program may use at most 704 MiB of HBM per device.

```python
import math
import jax
import jax.numpy as jnp
import numpy as np
from jax import lax

D = 2048
KVH = 16
HD = 128
FF = 5632
NEXP = 8
TOPK = 2
MB = 2
TOK_MB = 64
ATT = 2048
ROW = 256
CAP = 24
N_DP = 8
N_EXPERT = 4


def draw_lengths(key, part):
    key = jax.random.fold_in(key, 11)
    draw_key, pick_key = jax.random.split(key)
    lengths_drawn = jax.random.randint(draw_key, (MB * N_DP,), ROW - TOK_MB + 1, ROW + 1)
    chosen = jax.random.randint(pick_key, (), 0, MB * N_DP)
    flattened = jnp.where(jnp.arange(MB * N_DP) == chosen, ROW, lengths_drawn)
    return flattened.reshape(MB, N_DP).astype(jnp.int32)


def level_of(rng, dims, cuts, low, largest):
    def one(dim, blocks):
        draws = jax.random.uniform(jax.random.fold_in(jax.random.fold_in(rng, 6), dim), (blocks,), jnp.float32, low / len(cuts), largest / len(cuts))
        return jnp.repeat(jnp.exp(draws), dims[dim] // blocks).reshape((-1,) + (1,) * (len(dims) - dim - 1))

    level = one(*cuts[0])
    for cut in cuts[1:]:
        level = level * one(*cut)
    return level


def deal_out(rng, own, number, rows, amount, top, most, skew):
    ranking = jax.random.permutation(rng, amount)
    crowded, ordinary = portions_of(amount, rows * top, most, skew, True), portions_of(amount, rows * top, most, skew, False)
    places = jnp.arange(amount)

    def named(sizes, turn):
        used = int((sizes > 0).sum())
        fixed = max(1, used // 4)
        moved = fixed + (places - fixed + turn * (used - fixed)) % max(1, amount - fixed)
        return jnp.zeros((amount,), jnp.int32).at[ranking[jnp.where(places < fixed, places, moved)]].set(jnp.asarray(sizes, jnp.int32))

    sizes = jnp.where(number % 4 == 0, named(crowded, number // 4), named(ordinary, number - number // 4 - 1))
    mixed = jax.random.permutation(jax.random.fold_in(own, 3), amount)
    source_of, taker = mixed[0:amount // 2 * 2:2], mixed[1:amount // 2 * 2:2]
    room = jnp.minimum(sizes[source_of] - 1, most - sizes[taker]) // 2
    room = jnp.where((source_of == ranking[0]) | (taker == ranking[0]) | (sizes[taker] == 0), 0, jnp.maximum(room, 0))
    moved = jax.random.randint(jax.random.fold_in(own, 4), (amount // 2,), 0, 1 << 20) % (room + 1)
    sizes = sizes.at[source_of].add(-moved).at[taker].add(moved)
    items = jnp.searchsorted(jnp.cumsum(sizes), jnp.arange(rows * top), side="right").astype(jnp.int32)
    listing = items.reshape(top, rows).T
    listing = listing[jax.random.permutation(jax.random.fold_in(own, 1), rows)]
    turn = jax.random.randint(jax.random.fold_in(own, 2), (rows, 1), 0, top)
    return jnp.take_along_axis(listing, (jnp.arange(top)[None, :] + turn) % top, axis=1)


def portions_of(amount, total, limit, lean, full):
    weights = [(1 << 20) // math.isqrt(standing ** lean) + 1 for standing in range(1, amount + 1)]
    largest = limit if full else min(limit, max(-(-total // amount), total * weights[0] // sum(weights)))
    least = 1 if total - largest >= amount - 1 else 0
    counts, surplus = [largest] + [least] * (amount - 1), total - largest - least * (amount - 1)
    while surplus > 0:
        free = [i for i in range(1, amount) if counts[i] < largest] or [i for i in range(1, amount) if counts[i] < limit]
        pool, remaining = sum([weights[i] for i in free]), surplus
        for i in free:
            more = min(limit - counts[i], max(1, remaining * weights[i] // pool), surplus)
            counts[i] = counts[i] + more
            surplus = surplus - more
    return np.array(counts)


def bell_draw(own_key, shape, spread, bound, shards=(), kind=jnp.bfloat16):
    factor_of = level_of(own_key, shape, shards, -0.22, 0.18) if shards else 1.0
    values = jax.random.normal(own_key, shape, jnp.float32) * spread * factor_of
    return jnp.minimum(jnp.maximum(values, -bound), bound).astype(kind)


def setup_inputs(seed: int = 0) -> dict:
    key_list = jax.random.split(jax.random.key(seed), 13)
    tokens = bell_draw(key_list[0], (MB, N_DP, ROW, D), 1.0, 6.0, ((1, 8), (2, 4)))
    lengths = draw_lengths(jax.random.fold_in(key_list[12], 71), 0)
    attention_routes_keys = jax.random.split(jax.random.fold_in(key_list[2], 1), MB * N_DP * ROW // TOK_MB)
    attention_routes_turns = jax.random.permutation(jax.random.fold_in(key_list[2], 3), MB * N_DP * ROW // TOK_MB)
    attention_routes = jax.vmap(lambda own, number: deal_out(jax.random.fold_in(key_list[2], 2), own, number, TOK_MB, NEXP, TOPK, CAP, 2))(attention_routes_keys, attention_routes_turns).reshape((MB, N_DP, ROW, TOPK))
    feedforward_routes_keys = jax.random.split(jax.random.fold_in(key_list[3], 1), MB * N_DP * ROW // TOK_MB)
    feedforward_routes_turns = jax.random.permutation(jax.random.fold_in(key_list[3], 3), MB * N_DP * ROW // TOK_MB)
    feedforward_routes = jax.vmap(lambda own, number: deal_out(jax.random.fold_in(key_list[3], 2), own, number, TOK_MB, NEXP, TOPK, CAP, 2))(feedforward_routes_keys, feedforward_routes_turns).reshape((MB, N_DP, ROW, TOPK))
    norm_gains = jnp.clip(1.0 + 0.1 * jax.random.normal(key_list[4], (D, 2), jnp.float32), 0.5, 1.5).astype(jnp.bfloat16)
    router_weight = bell_draw(key_list[5], (D, 2 * NEXP), (2 * D) ** -0.5, 0.09375, ((0, 32),))
    key_value_weight = bell_draw(key_list[6], (D, 2 * ATT), D ** -0.5, 0.125, ((0, 32),))
    query_weight = bell_draw(key_list[7], (NEXP, D, ATT), D ** -0.5, 0.125, ((0, 4), (1, 8)))
    output_weight = bell_draw(key_list[8], (NEXP, ATT, D), (ATT // 32) ** -0.5, 0.75, ((0, 4), (1, 8)))
    input_weight = bell_draw(key_list[9], (NEXP, D, 2 * FF), D ** -0.5, 0.125, ((0, 4), (1, 8)))
    down_weight = bell_draw(key_list[10], (NEXP, FF, D), (FF // 4) ** -0.5, 0.15625, ((0, 4), (1, 8)))
    cotangent = bell_draw(key_list[11], (MB, N_DP, ROW, D), 1.0, 6.0, ((1, 8), (2, 4)))
    return {"tokens": tokens, "lengths": lengths, "attention_routes": attention_routes, "feedforward_routes": feedforward_routes, "norm_gains": norm_gains, "router_weight": router_weight, "key_value_weight": key_value_weight, "query_weight": query_weight, "output_weight": output_weight, "input_weight": input_weight, "down_weight": down_weight, "cotangent": cotangent}


EPSILON = 1e-06
HIGHEST = lax.Precision.HIGHEST

@jax.custom_vjp
def low(v):
    return lax.optimization_barrier(v.astype(jnp.bfloat16)).astype(jnp.float32)

@jax.custom_vjp
def low_back(v):
    return v

def low_keep(v):
    return (low(v), None)

def low_pass(kept, grad):
    return (grad,)

def back_keep(v):
    return (v, None)

def back_low(kept, grad):
    return (low(grad),)
low.defvjp(low_keep, low_pass)
low_back.defvjp(back_keep, back_low)

def matmul(operand, factor):
    return jnp.dot(operand, factor, precision=HIGHEST)

def rms_norm(values, norm_gain):
    inverse = lax.rsqrt(lax.optimization_barrier(jnp.mean(values * values, axis=-1, keepdims=True)) + EPSILON)
    return values * inverse * norm_gain

def rotate(values, places):
    half_size = HD // 2
    frequency = 10000.0 ** (-(jnp.arange(half_size, dtype=jnp.float32) * (2.0 / HD)))
    angles = places.astype(jnp.float32)[..., None] * frequency
    cosine = jnp.cos(angles)[..., None, :]
    sine_part = jnp.sin(angles)[..., None, :]
    shaped = values.reshape(values.shape[:-1] + (KVH, HD))
    former = shaped[..., :half_size]
    latter = shaped[..., half_size:]
    turned = jnp.concatenate([former * cosine - latter * sine_part, latter * cosine + former * sine_part], axis=-1)
    return turned.reshape(values.shape)

def pick_gates(logits, routes):
    picked = jnp.take_along_axis(logits, routes, axis=1)
    return jax.nn.softmax(picked, axis=-1)

def slots_of(routes):
    flattened = routes.reshape(-1)
    onehot = (flattened[:, None] == jnp.arange(NEXP, dtype=jnp.int32)[None, :]).astype(jnp.int32)
    earlier = lax.optimization_barrier(jnp.sum((jnp.cumsum(onehot, axis=0) - onehot) * onehot, axis=1))
    target = (flattened * (N_EXPERT * CAP) + earlier).astype(jnp.int32)
    anchor = jnp.arange(flattened.shape[0], dtype=jnp.int32) // TOPK
    source = jnp.zeros((NEXP * N_EXPERT * CAP,), jnp.int32).at[target].set(anchor)
    return (target.reshape(routes.shape), source)

def attend(expert_rows, query_places, key_rows, value_rows, length, query_matrix, output_matrix):
    key_places = jnp.arange(key_rows.shape[0], dtype=jnp.int32)
    query_pre = low_back(matmul(expert_rows, query_matrix))
    queries = low(rotate(query_pre, query_places) * HD ** (-0.5))
    query_heads = queries.reshape(-1, KVH, HD)
    key_heads = key_rows.reshape(-1, KVH, HD)
    value_heads = value_rows.reshape(-1, KVH, HD)
    scores = low_back(jnp.einsum('qhd,khd->hqk', query_heads, key_heads, precision=HIGHEST))
    allowed = (key_places[None, :] <= query_places[:, None]) & (key_places[None, :] < length)
    scores = jnp.where(allowed[None], scores, -1e+30)
    attn_probs = low(jax.nn.softmax(scores, axis=-1))
    mixture = jnp.einsum('hqk,khd->qhd', attn_probs, value_heads, precision=HIGHEST).reshape(-1, KVH * HD)
    mixture = low(low_back(mixture))
    return low(low_back(matmul(mixture, output_matrix)))

def expert_feed(expert_rows, input_matrix, down_matrix):
    hidden = low_back(matmul(expert_rows, input_matrix))
    active = low(jax.nn.silu(hidden[:, :FF]) * hidden[:, FF:])
    return low(low_back(matmul(active, down_matrix)))

def layer_row(params, row_tokens, mixer_route, feed_route, length):
    norm_gains, router_weight, key_value_weight, query_weight, output_weight, input_weight, down_weight = params
    att_width = KVH * HD
    places = jnp.arange(row_tokens.shape[0], dtype=jnp.int32)
    normed_mixer = low(rms_norm(row_tokens, norm_gains[:, 0]))
    gates_mixer = pick_gates(matmul(normed_mixer, router_weight[:, :NEXP]), mixer_route)
    key_value = low_back(matmul(normed_mixer, key_value_weight))
    key_rows = low(rotate(key_value[:, :att_width], places))
    value_rows = low(key_value[:, att_width:])
    target_mixer, source_mixer = slots_of(mixer_route)
    buffer_mixer = low_back(normed_mixer[source_mixer]).reshape(NEXP, -1, D)
    places_mixer = source_mixer.reshape(NEXP, -1)
    checked_attend = jax.checkpoint(attend)

    def attend_item(packed):
        return checked_attend(packed[0], packed[1], key_rows, value_rows, length, packed[2], packed[3])
    outputs_mixer = lax.map(attend_item, (buffer_mixer, places_mixer, query_weight, output_weight))
    combined_mixer = outputs_mixer.reshape(-1, D)[target_mixer]
    second = row_tokens + lax.optimization_barrier(jnp.sum(gates_mixer[:, :, None] * combined_mixer, axis=1))
    normed_feed = low(rms_norm(second, norm_gains[:, 1]))
    gates_feed = pick_gates(matmul(normed_feed, router_weight[:, NEXP:]), feed_route)
    target_feed, source_feed = slots_of(feed_route)
    buffer_feed = low_back(normed_feed[source_feed]).reshape(NEXP, -1, D)
    checked_feed = jax.checkpoint(expert_feed)

    def feed_item(packed):
        return checked_feed(packed[0], packed[1], packed[2])
    outputs_feed = lax.map(feed_item, (buffer_feed, input_weight, down_weight))
    combined_feed = outputs_feed.reshape(-1, D)[target_feed]
    return second + lax.optimization_barrier(jnp.sum(gates_feed[:, :, None] * combined_feed, axis=1))

def reference(tokens, lengths, attention_routes, feedforward_routes, norm_gains, router_weight, key_value_weight, query_weight, output_weight, input_weight, down_weight, cotangent):
    params = tuple((weight.astype(jnp.float32) for weight in (norm_gains, router_weight, key_value_weight, query_weight, output_weight, input_weight, down_weight)))
    row_count = MB * N_DP
    rows_in = tokens.astype(jnp.float32).reshape(row_count, -1, D)
    routes_mixer = attention_routes.reshape(row_count, -1, TOPK)
    routes_feed = feedforward_routes.reshape(row_count, -1, TOPK)
    row_lengths = lengths.reshape(row_count)
    checked_row = jax.checkpoint(layer_row)

    def forward(inputs_all, weights_all):

        def one_row(carried, packed):
            return (carried, checked_row(weights_all, packed[0], packed[1], packed[2], packed[3]))
        return lax.scan(one_row, None, (inputs_all, routes_mixer, routes_feed, row_lengths))[1]
    outputs, pullback = jax.vjp(forward, rows_in, params)
    places = jnp.arange(rows_in.shape[1], dtype=jnp.int32)
    valid_mask = (places[None, :] < row_lengths[:, None]).astype(jnp.float32)
    masked = cotangent.astype(jnp.float32).reshape(outputs.shape) * valid_mask[:, :, None]
    grad_rows, weight_grads = pullback(masked)
    token_shape = tokens.shape
    return (outputs.reshape(token_shape).astype(jnp.bfloat16), grad_rows.reshape(token_shape).astype(jnp.bfloat16), weight_grads[0], weight_grads[1], weight_grads[2], weight_grads[3], weight_grads[4], weight_grads[5], weight_grads[6])
```

```python
import functools
import jax
import jax.numpy as jnp
from jax import lax
from jax.experimental import pallas as pl
from jax.experimental.pallas import tpu as pltpu
from jax.sharding import PartitionSpec as P

MESH = pl.DeviceIdType.MESH
BF16 = jnp.bfloat16
F32 = jnp.float32


def expert_factors(owners):
    return (2, owners // 2) if owners % 2 == 0 and owners > 2 else (1, owners)


class Place:
    def __init__(self, chips, first, second):
        dp = lax.axis_index("dp")
        ex = lax.axis_index("expert")
        self.chips, self.first, self.second = chips, first, second
        self.dp, self.ex = dp, ex
        self.z, self.k = dp // 2, dp % 2
        self.a, self.b = ex // second, ex % second

    def at(self, z=None, k=None, a=None, b=None):
        z = self.z if z is None else z
        k = self.k if k is None else k
        a = self.a if a is None else a
        b = self.b if b is None else b
        return (z * 2 + k, a * self.second + b)

    def greet(self):
        barrier = pltpu.get_barrier_semaphore()

        def hello(target):
            pl.semaphore_signal(barrier, inc=1, device_id=target, device_id_type=MESH)

        hello(self.at(k=1 - self.k))
        for i in range(1, self.first):
            hello(self.at(a=(self.a + i) % self.first))
        for i in range(1, self.second):
            hello(self.at(b=(self.b + i) % self.second))
        pl.when(self.z > 0)(lambda: hello(self.at(z=self.z - 1)))
        pl.when(self.z < self.chips - 1)(lambda: hello(self.at(z=self.z + 1)))
        along = (self.z > 0).astype(jnp.int32) + (self.z < self.chips - 1).astype(jnp.int32)
        pl.semaphore_wait(barrier, self.first + self.second - 1 + along)


def gather_kernel(chips, first, second, by_row, x_ref, out_ref, own_sem, recv, sends):
    me = Place(chips, first, second)
    owners = first * second
    me.greet()

    def index(z, k, a, b):
        return (z * 2 + k) * owners + a * second + b

    def piece(blk, h):
        return out_ref.at[h, blk] if by_row else out_ref.at[blk, h]

    pending = []

    def push(src, blk, h, target, when=None):
        copy = pltpu.make_async_remote_copy(
            src_ref=src,
            dst_ref=piece(blk, h),
            send_sem=sends.at[len(pending)],
            recv_sem=recv.at[blk, h],
            device_id=target,
            device_id_type=MESH,
        )
        pending.append((copy, when))
        copy.start() if when is None else pl.when(when)(copy.start)

    def landed(blk, h, when=None):
        copy = pltpu.make_async_remote_copy(
            src_ref=piece(blk, h),
            dst_ref=piece(blk, h),
            send_sem=sends.at[0],
            recv_sem=recv.at[blk, h],
            device_id=me.at(),
            device_id_type=MESH,
        )
        copy.wait_recv() if when is None else pl.when(when)(copy.wait_recv)

    own = index(me.z, me.k, me.a, me.b)
    stays = [pltpu.make_async_copy(x_ref.at[h], piece(own, h), own_sem.at[h]) for h in range(2)]
    for stay in stays:
        stay.start()

    def spread(z, blk, source, when=None):
        for h in range(2):
            for i in range(1, second):
                push(source(h), blk, h, me.at(b=(me.b + i) % second), when)
            for i in range(1, first):
                push(source(h), blk, h, me.at(a=(me.a + i) % first), when)
        for h in range(2):
            push(source(h), blk, h, me.at(k=1 - me.k), when)

    def relay(z, when=None):
        for h in range(2):
            if h == 0:
                froms = [(me.a, (me.b + i) % second) for i in range(1, second)]
                onward = [dict(a=(me.a + i) % first) for i in range(1, first)]
            else:
                froms = [((me.a + i) % first, me.b) for i in range(1, first)]
                onward = [dict(b=(me.b + i) % second) for i in range(1, second)]
            for a, b in froms:
                blk = index(z, me.k, a, b)
                landed(blk, h, when)
                for target in onward:
                    push(piece(blk, h), blk, h, me.at(**target), when)
                push(piece(blk, h), blk, h, me.at(k=1 - me.k), when)

    def finish(z, when=None):
        for h in range(2):
            for i in range(1, second if h else first):
                if h == 0:
                    a, bs = (me.a + i) % first, [(me.b + j) % second for j in range(second)]
                    spots = [(a, b) for b in bs]
                else:
                    b = (me.b + i) % second
                    spots = [((me.a + j) % first, b) for j in range(first)]
                for a, b in spots:
                    blk = index(z, me.k, a, b)
                    landed(blk, h, when)
                    push(piece(blk, h), blk, h, me.at(k=1 - me.k), when)

    def own_half(h):
        return x_ref.at[h]

    for h in range(2):
        push(own_half(h), own, h, me.at(z=me.z + 1), me.z < chips - 1)
        push(own_half(h), own, h, me.at(z=me.z - 1), me.z > 0)
    spread(me.z, own, own_half)
    queue = [(me.z, None)]
    for t in range(1, chips):
        fresh = []
        for sign in (-1, 1):
            z = me.z + sign * t
            there = (z >= 0) if sign < 0 else (z < chips)
            blk = index(z, me.k, me.a, me.b)
            further = (me.z < chips - 1) if sign < 0 else (me.z > 0)
            for h in range(2):
                landed(blk, h, there)
                push(piece(blk, h), blk, h, me.at(z=me.z - sign), there & further)
            spread(z, blk, lambda h, blk=blk: piece(blk, h), there)
            fresh.append((z, there))
        for z, there in queue:
            relay(z, there)
        for z, there in queue:
            finish(z, there)
        queue = fresh
    for z, there in queue:
        relay(z, there)
    for z, there in queue:
        finish(z, there)
    for stay in stays:
        stay.wait()
    for z in range(chips):
        for e in range(owners):
            for h in range(2):
                landed((z * 2 + 1 - me.k) * owners + e, h)
    for copy, when in pending:
        copy.wait_send() if when is None else pl.when(when)(copy.wait_send)


def gather_all(x, chips, owners, by_row, collective_id):
    first, second = expert_factors(owners)
    _, rows, width = x.shape
    blocks = chips * 2 * owners
    sends = 4 + (2 * chips - 1) * (
        2 + 2 * (first + second - 1) + 2 * (second - 1) * first + 2 * (first - 1) * second
    )
    shape = (2, blocks, rows, width) if by_row else (blocks, 2, rows, width)
    return pl.pallas_call(
        functools.partial(gather_kernel, chips, first, second, by_row),
        out_shape=jax.ShapeDtypeStruct(shape, x.dtype),
        in_specs=[pl.BlockSpec(memory_space=pl.ANY)],
        out_specs=pl.BlockSpec(memory_space=pl.ANY),
        scratch_shapes=[
            pltpu.SemaphoreType.DMA((2,)),
            pltpu.SemaphoreType.DMA((blocks, 2)),
            pltpu.SemaphoreType.DMA((sends,)),
        ],
        compiler_params=pltpu.CompilerParams(collective_id=collective_id, has_side_effects=True),
    )(x)


def scatter_kernel(
    chips, first, second, by_row, column, width, p_ref, out_ref,
    mine, fromk, a0, b0, b1, a1, fromz, total, load_sem, ks, a0s, b0s, b1s, a1s, zs, sends,
):
    me = Place(chips, first, second)
    owners = first * second
    me.greet()
    pending = []

    def push(src, dst, sem, target, when=None):
        copy = pltpu.make_async_remote_copy(
            src_ref=src, dst_ref=dst, send_sem=sends.at[len(pending)], recv_sem=sem,
            device_id=target, device_id_type=MESH,
        )
        pending.append((copy, when))
        copy.start() if when is None else pl.when(when)(copy.start)

    def landed(dst, sem):
        pltpu.make_async_remote_copy(
            src_ref=dst, dst_ref=dst, send_sem=sends.at[0], recv_sem=sem,
            device_id=me.at(), device_id_type=MESH,
        ).wait_recv()

    low = me.z < chips // 2

    def line(t):
        return jnp.where(
            low,
            jnp.where(t < chips - 1 - me.z, chips - 1 - t, t - (chips - 1 - me.z)),
            jnp.where(t < me.z, t, chips - 1 - (t - me.z)),
        )

    cut = pl.ds(column, width)

    def block(z, k, e):
        blk = (z * 2 + k) * owners + e
        return p_ref.at[:, blk, :, cut] if by_row else p_ref.at[blk, :, :, cut]

    loads = {}
    for t in range(chips):
        z = line(t)
        for e in range(owners):
            load = pltpu.make_async_copy(
                block(z, me.k, e), mine.at[t, e], load_sem.at[t, e]
            )
            load.start()
            loads[t, e] = load
            push(
                block(z, 1 - me.k, e),
                fromk.at[t, e], ks.at[t, e], me.at(k=1 - me.k),
            )

    def add(*terms):
        value = terms[0].astype(F32)
        for term in terms[1:]:
            value = value + term.astype(F32)
        return value

    def step_one(t):
        for i in range(first):
            for j in range(second):
                a, b = (me.a + 1 + i) % first, (me.b + 1 + j) % second
                e = a * second + b
                loads_sem = load_sem.at[t, e]
                pltpu.make_async_copy(mine.at[t, e], mine.at[t, e], loads_sem).wait()
                landed(fromk.at[t, e], ks.at[t, e])
                mine[t, e] = add(mine[t, e], fromk[t, e]).astype(BF16)
                if i < first - 1:
                    push(
                        mine.at[t, e, 0], a0.at[t, first - 2 - i, b],
                        a0s.at[t, first - 2 - i, b], me.at(a=a),
                    )
                if j < second - 1:
                    push(
                        mine.at[t, e, 1], b1.at[t, second - 2 - j, a],
                        b1s.at[t, second - 2 - j, a], me.at(b=b),
                    )

    def step_two(t):
        for j in range(second - 1):
            b = (me.b + 1 + j) % second
            e = me.a * second + b
            for i in range(first - 1):
                landed(a0.at[t, i, b], a0s.at[t, i, b])
            mine[t, e, 0] = add(
                mine[t, e, 0], *[a0[t, i, b] for i in range(first - 1)]
            ).astype(BF16)
            push(
                mine.at[t, e, 0], b0.at[t, second - 2 - j],
                b0s.at[t, second - 2 - j], me.at(b=b),
            )
        for i in range(first - 1):
            a = (me.a + 1 + i) % first
            e = a * second + me.b
            for j in range(second - 1):
                landed(b1.at[t, j, a], b1s.at[t, j, a])
            mine[t, e, 1] = add(
                mine[t, e, 1], *[b1[t, j, a] for j in range(second - 1)]
            ).astype(BF16)
            push(
                mine.at[t, e, 1], a1.at[t, first - 2 - i],
                a1s.at[t, first - 2 - i], me.at(a=a),
            )

    def step_three(t):
        z = line(t)
        e = me.ex
        for i in range(first - 1):
            landed(a0.at[t, i, me.b], a0s.at[t, i, me.b])
            landed(a1.at[t, i], a1s.at[t, i])
        for j in range(second - 1):
            landed(b1.at[t, j, me.a], b1s.at[t, j, me.a])
            landed(b0.at[t, j], b0s.at[t, j])
        total[t, 0] = add(
            mine[t, e, 0], *[a0[t, i, me.b] for i in range(first - 1)],
            *[b0[t, j] for j in range(second - 1)],
        )
        total[t, 1] = add(
            mine[t, e, 1], *[b1[t, j, me.a] for j in range(second - 1)],
            *[a1[t, i] for i in range(first - 1)],
        )
        if t < chips - 1:
            up = z > me.z
            from_beyond = jnp.where(up, me.z > 0, me.z < chips - 1)

            @pl.when(from_beyond)
            def _():
                landed(fromz.at[z], zs.at[z])
                total[t] = total[t] + fromz[z].astype(F32)

            mine[t, e] = total[t].astype(BF16)
            push(mine.at[t, e], fromz.at[z], zs.at[z], me.at(z=me.z + 1), up)
            slot = jnp.where(z == me.z - 1, chips, z)
            push(mine.at[t, e], fromz.at[slot], zs.at[slot], me.at(z=me.z - 1), jnp.logical_not(up))
        else:

            @pl.when(me.z > 0)
            def _():
                landed(fromz.at[me.z], zs.at[me.z])
                total[t] = total[t] + fromz[me.z].astype(F32)

            @pl.when(me.z < chips - 1)
            def _():
                landed(fromz.at[chips], zs.at[chips])
                total[t] = total[t] + fromz[chips].astype(F32)

            out_ref[...] = total[t]

    for t in range(chips + 2):
        if t < chips:
            step_one(t)
        if 0 <= t - 1 < chips:
            step_two(t - 1)
        if 0 <= t - 2 < chips:
            step_three(t - 2)
    for copy, when in pending:
        copy.wait_send() if when is None else pl.when(when)(copy.wait_send)


def scatter_sum(p, chips, owners, by_row, collective_id):
    first, second = expert_factors(owners)
    half, full = p.shape[2:]
    parts = 1
    while chips * owners * half * (full // parts) * 8 > 20 * 2**20:
        parts *= 2
    width = full // parts
    one = max(first - 1, 1), max(second - 1, 1)
    sends = chips * (owners + 2 + 2 * (first - 1) * second + 2 * (second - 1) * first)
    sends += chips * (first + second)

    def call(part):
        sem = pltpu.SemaphoreType.DMA
        return pl.pallas_call(
            functools.partial(scatter_kernel, chips, first, second, by_row, part * width, width),
            out_shape=jax.ShapeDtypeStruct((2, half, width), F32),
            in_specs=[pl.BlockSpec(memory_space=pl.ANY)],
            out_specs=pl.BlockSpec(memory_space=pltpu.VMEM),
            scratch_shapes=[
                pltpu.VMEM((chips, owners, 2, half, width), BF16),
                pltpu.VMEM((chips, owners, 2, half, width), BF16),
                pltpu.VMEM((chips, one[0], second, half, width), BF16),
                pltpu.VMEM((chips, one[1], half, width), BF16),
                pltpu.VMEM((chips, one[1], first, half, width), BF16),
                pltpu.VMEM((chips, one[0], half, width), BF16),
                pltpu.VMEM((chips + 1, 2, half, width), BF16),
                pltpu.VMEM((chips, 2, half, width), F32),
                sem((chips, owners)),
                sem((chips, owners)),
                sem((chips, one[0], second)),
                sem((chips, one[1])),
                sem((chips, one[1], first)),
                sem((chips, one[0])),
                sem((chips + 1,)),
                sem((sends,)),
            ],
            compiler_params=pltpu.CompilerParams(
                collective_id=collective_id + part, has_side_effects=True,
                vmem_limit_bytes=60 * 2**20,
            ),
        )(p)

    parts_out = [call(part) for part in range(parts)]
    return parts_out[0] if parts == 1 else jnp.concatenate(parts_out, axis=-1)


def exchange_kernel(devices, owners, same, x_ref, out_ref, own_sem, recv, sends):
    dp = lax.axis_index("dp")
    ex = lax.axis_index("expert")
    me = dp * owners + ex
    barrier = pltpu.get_barrier_semaphore()

    def target(i):
        other = (me + i) % devices
        return other, (other // owners, other % owners)

    def hello(i, _):
        pl.semaphore_signal(barrier, inc=1, device_id=target(i)[1], device_id_type=MESH)
        return 0

    lax.fori_loop(1, devices, hello, 0)
    stay = pltpu.make_async_copy(x_ref.at[0 if same else me], out_ref.at[me], own_sem)
    stay.start()
    pl.semaphore_wait(barrier, devices - 1)

    def copy(i):
        other, where = target(i)
        return pltpu.make_async_remote_copy(
            src_ref=x_ref.at[0 if same else other], dst_ref=out_ref.at[me],
            send_sem=sends.at[i], recv_sem=recv.at[me], device_id=where, device_id_type=MESH,
        )

    def send(i, _):
        copy(i).start()
        return 0

    def landed(i, _):
        other, where = target(i)
        pltpu.make_async_remote_copy(
            src_ref=out_ref.at[other], dst_ref=out_ref.at[other], send_sem=sends.at[i],
            recv_sem=recv.at[other], device_id=where, device_id_type=MESH,
        ).wait_recv()
        copy(i).wait_send()
        return 0

    lax.fori_loop(1, devices, send, 0)
    lax.fori_loop(1, devices, landed, 0)
    stay.wait()


def exchange(x, devices, owners, collective_id):
    same = x.shape[0] == 1
    return pl.pallas_call(
        functools.partial(exchange_kernel, devices, owners, same),
        out_shape=jax.ShapeDtypeStruct((devices,) + x.shape[1:], x.dtype),
        in_specs=[pl.BlockSpec(memory_space=pl.ANY)],
        out_specs=pl.BlockSpec(memory_space=pl.ANY),
        scratch_shapes=[
            pltpu.SemaphoreType.DMA,
            pltpu.SemaphoreType.DMA((devices,)),
            pltpu.SemaphoreType.DMA((devices,)),
        ],
        compiler_params=pltpu.CompilerParams(collective_id=collective_id, has_side_effects=True),
    )(x)


D = 2048
KVH = 16
HD = 128
FF = 5632
NEXP = 8
TOK_MB = 64
CAP = 24
LANES = 128
EPSILON = 1e-06


def product(pattern, operand, factor):
    return jnp.einsum(pattern, operand, factor, preferred_element_type=F32)


def turn(values, cosine, sine):
    shaped = values.reshape(values.shape[:-1] + (-1, 2, HD // 2))
    former, latter = shaped[..., 0, :], shaped[..., 1, :]
    cosine, sine = cosine[..., None, :], sine[..., None, :]
    turned = jnp.stack([former * cosine - latter * sine, latter * cosine + former * sine], axis=-2)
    return turned.reshape(values.shape)


def angles_of(places):
    frequency = 10000.0 ** (-(jnp.arange(HD // 2, dtype=F32) * (2.0 / HD)))
    angles = places.astype(F32)[..., None] * frequency
    return jnp.cos(angles), jnp.sin(angles)


def norm_forward(values, norm_gain):
    inverse = lax.rsqrt(jnp.mean(values * values, axis=-1, keepdims=True) + EPSILON)
    return (values * inverse * norm_gain, inverse)


def norm_backward(values, inverse, norm_gain, grad_normed):
    scaled = grad_normed * norm_gain
    grad_gain = jnp.sum(grad_normed * values * inverse, axis=(0, 1))
    grad_values = inverse * scaled - values * inverse**3 * jnp.mean(
        scaled * values, axis=-1, keepdims=True
    )
    return (grad_values, grad_gain)


def choices(routes):
    return (routes[..., None] == jnp.arange(NEXP, dtype=jnp.int32)).astype(F32)


def gate_values(logits, choose):
    picked = jnp.sum(choose * logits[..., None, :], axis=-1)
    highest = jnp.max(picked, axis=-1, keepdims=True)
    exponent = jnp.exp(picked - highest)
    return exponent / jnp.sum(exponent, axis=-1, keepdims=True)


def gate_grads(gate_probs, grad_gate_probs, choose):
    weighted = jnp.sum(gate_probs * grad_gate_probs, axis=-1, keepdims=True)
    grad_picked = gate_probs * (grad_gate_probs - weighted)
    return jnp.sum(grad_picked[..., None] * choose, axis=-2)


def seats(routes, first_expert, local_count, groups):
    experts = first_expert + jnp.arange(local_count, dtype=jnp.int32)
    hit = jnp.any(routes[:, :, :, None] == experts, axis=2).astype(jnp.int32)
    rank = jnp.cumsum(hit, axis=1) - hit
    blocks = routes.shape[0]
    per = blocks // groups
    hit = hit.reshape(groups, per, TOK_MB, local_count)
    seat = rank.reshape(hit.shape) + (jnp.arange(per, dtype=jnp.int32) * CAP)[:, None, None]
    seat = jnp.where(hit > 0, seat, -1).reshape(groups, per * TOK_MB, local_count)
    seat = jnp.swapaxes(seat, 1, 2)
    return seat[:, :, None, :] == jnp.arange(per * CAP, dtype=jnp.int32)[:, None]


def tile_starts(shards):
    share = FF // shards
    most = max(share * d % LANES for d in range(shards))
    tiles = -(-(share + most) // LANES)
    starts = [min(share * d // LANES, FF // LANES - tiles) for d in range(shards)]
    return tiles, starts, [share * d - LANES * starts[d] for d in range(shards)]


def shards(
    tokens, lengths, attention_routes, feedforward_routes, norm_gains, router_weight,
    key_value_weight, query_weight, output_weight, input_weight, down_weight, cotangent,
):
    n_dp = lax.axis_size("dp")
    owners = lax.axis_size("expert")
    chips = n_dp // 2
    devices = n_dp * owners
    dp = lax.axis_index("dp")
    ex = lax.axis_index("expert")
    me = dp * owners + ex
    mb = tokens.shape[0]
    local_count = NEXP // owners
    seqs = mb * n_dp
    row_length = owners * TOK_MB
    heads = KVH // n_dp
    hc = heads * HD
    att = KVH * HD
    depth = D // n_dp
    slice_rows = D // devices
    tiles, starts, offsets = tile_starts(n_dp)
    share, wide = FF // n_dp, tiles * LANES
    offset = jnp.array(offsets, jnp.int32)[dp]
    scaling = HD ** (-0.5)

    query_parts = jnp.transpose(
        query_weight.reshape(local_count, depth, n_dp, hc), (2, 0, 1, 3)
    )
    query_full = lax.all_to_all(query_parts, "dp", 0, 0, tiled=True)
    query_full = jnp.swapaxes(query_full, 0, 1).reshape(local_count, D, hc)
    key_value_parts = jnp.transpose(
        key_value_weight.reshape(slice_rows, 2, n_dp, hc), (2, 0, 1, 3)
    )
    key_value_full = lax.all_to_all(key_value_parts, "dp", 0, 0, tiled=True)
    key_value_full = lax.all_gather(
        key_value_full.reshape(n_dp, slice_rows, 2 * hc), "expert", axis=1
    ).reshape(D, 2 * hc)
    input_parts = jnp.stack(
        [
            jnp.stack(
                [
                    lax.slice_in_dim(input_weight, g * FF + LANES * s, g * FF + LANES * s + wide, axis=2)
                    for g in range(2)
                ]
            )
            for s in starts
        ]
    )
    input_full = lax.all_to_all(input_parts, "dp", 0, 0, tiled=True)
    input_full = jnp.transpose(input_full, (2, 1, 0, 3, 4)).reshape(local_count, 2, D, wide)
    gate_full, up_full = input_full[:, 0], input_full[:, 1]
    down_full = lax.dynamic_update_slice(
        jnp.zeros((local_count, wide, D), BF16), down_weight, (0, offset, 0)
    )

    shared = jnp.concatenate([norm_gains, router_weight], axis=1).astype(F32)
    small = jnp.concatenate(
        [
            attention_routes.reshape(-1).astype(F32),
            feedforward_routes.reshape(-1).astype(F32),
            shared.reshape(-1),
            lengths.reshape(-1).astype(F32),
        ]
    )
    count = small.shape[0]
    small = jnp.pad(small, (0, -count % (8 * LANES))).reshape(1, -1, LANES)
    small = exchange(small, devices, owners, 1).reshape(devices, -1)
    route_count = mb * TOK_MB * 2
    routes_all = small[:, : 2 * route_count].astype(jnp.int32)
    mixer_routes = routes_all[:, :route_count].reshape(n_dp, owners, mb, TOK_MB, 2)
    mixer_routes = jnp.transpose(mixer_routes, (2, 0, 1, 3, 4)).reshape(-1, TOK_MB, 2)
    feed_routes = routes_all[:, route_count:].reshape(-1, TOK_MB, 2)
    shared_all = small[:, 2 * route_count : 2 * route_count + slice_rows * 18].reshape(D, 18)
    gain_mixer, gain_feed = shared_all[:, 0], shared_all[:, 1]
    router_mixer = shared_all[:, 2 : 2 + NEXP]
    router_feed = shared_all[:, 2 + NEXP :]
    lengths_all = small[:, count - mb : count].astype(jnp.int32)
    row_lengths = lengths_all.reshape(n_dp, owners, mb)[:, 0].T.reshape(seqs)

    own_tokens = tokens[:, 0].astype(F32)
    home_places = ex * TOK_MB + jnp.arange(TOK_MB, dtype=jnp.int32)
    own_valid = (home_places[None, :] < lengths[:, :1]).astype(F32)
    own_cotangent = cotangent[:, 0].astype(F32) * own_valid[..., None]

    normed_mixer, inverse_mixer = norm_forward(own_tokens, gain_mixer)
    normed_mixer = normed_mixer.astype(BF16)
    mixer_all = gather_all(normed_mixer, chips, owners, True, 2).reshape(seqs, row_length, D)
    onehot_mixer = seats(mixer_routes, ex * local_count, local_count, seqs)
    seat_places = jnp.sum(
        jnp.where(onehot_mixer, jnp.arange(row_length, dtype=jnp.int32), 0), axis=-1
    )
    choose_mixer = choices(mixer_routes.reshape(seqs, row_length, 2))
    logits_mixer = product("std,de->ste", mixer_all, router_mixer.astype(BF16))
    gates_mixer = gate_values(logits_mixer, choose_mixer)
    experts_here = ex * local_count + jnp.arange(local_count, dtype=jnp.int32)
    here_mixer = mixer_routes.reshape(seqs, row_length, 2)[..., None] == experts_here
    slot_gates_mixer = jnp.sum(jnp.where(here_mixer, gates_mixer[..., None], 0.0), axis=2)
    seat_gates_mixer = jnp.sum(
        jnp.where(onehot_mixer, jnp.swapaxes(slot_gates_mixer, 1, 2)[:, :, None, :], 0.0), axis=-1
    )
    onehot_mixer_low = onehot_mixer.astype(BF16)

    key_places = jnp.arange(row_length, dtype=jnp.int32)
    key_cos, key_sin = angles_of(key_places)
    key_value = product("std,dc->stc", mixer_all, key_value_full)
    keys = turn(key_value[..., :hc], key_cos, key_sin).astype(BF16)
    values = key_value[..., hc:].astype(BF16)
    rows_mixer = product("slrt,std->lsrd", onehot_mixer_low, mixer_all).astype(BF16)
    seat_cos, seat_sin = angles_of(jnp.swapaxes(seat_places, 0, 1))
    queries = product("lsrd,ldc->lsrc", rows_mixer, query_full)
    queries = (turn(queries, seat_cos, seat_sin) * scaling).astype(BF16)
    query_heads = queries.reshape(local_count, seqs, -1, heads, HD)
    key_heads = keys.reshape(seqs, row_length, heads, HD)
    value_heads = values.reshape(seqs, row_length, heads, HD)
    allowed = (key_places <= seat_places[..., None]) & (
        key_places < row_lengths[:, None, None, None]
    )
    allowed = jnp.swapaxes(allowed, 0, 1)[:, :, None]
    scores = product("lsrhd,skhd->lshrk", query_heads, key_heads)
    scores = jnp.where(allowed, scores, -1e30)
    highest = jnp.max(scores, axis=-1, keepdims=True)
    exponent = jnp.exp(scores - highest)
    attn_probs = exponent / jnp.sum(exponent, axis=-1, keepdims=True)
    attn_low = attn_probs.astype(BF16)
    mixture = product("lshrk,skhd->lsrhd", attn_low, value_heads).reshape(queries.shape)
    seat_gates_mixer = jnp.swapaxes(seat_gates_mixer, 0, 1)[..., None]
    mixture_gated = (mixture * seat_gates_mixer).astype(BF16)
    mixer_rows = product("lsrc,lcd->lsrd", mixture_gated, output_weight).astype(BF16)
    mixer_part = product("slrt,lsrd->std", onehot_mixer_low, mixer_rows).astype(BF16)
    mixer_sum = scatter_sum(
        mixer_part.reshape(mb, devices, TOK_MB, D), chips, owners, True, 10
    )

    second = own_tokens + mixer_sum
    normed_feed, inverse_feed = norm_forward(second, gain_feed)
    normed_feed = normed_feed.astype(BF16)
    groups = seqs
    feed_all = gather_all(normed_feed, chips, owners, False, 3).reshape(groups, -1, D)
    cot_all = lax.all_gather(
        own_cotangent.astype(BF16), ("dp", "expert"), axis=0
    ).reshape(groups, -1, D)
    group_size = feed_all.shape[1]
    onehot_feed = seats(feed_routes, ex * local_count, local_count, groups)
    grouped_routes = feed_routes.reshape(groups, group_size, 2)
    choose_feed = choices(grouped_routes)
    logits_feed = product("std,de->ste", feed_all, router_feed.astype(BF16))
    gates_feed = gate_values(logits_feed, choose_feed)
    here_feed = grouped_routes[..., None] == experts_here
    slot_gates_feed = jnp.sum(jnp.where(here_feed, gates_feed[..., None], 0.0), axis=2)
    seat_gates_feed = jnp.sum(
        jnp.where(onehot_feed, jnp.swapaxes(slot_gates_feed, 1, 2)[:, :, None, :], 0.0), axis=-1
    )
    seat_gates_feed = jnp.swapaxes(seat_gates_feed, 0, 1)[..., None]
    onehot_feed_low = onehot_feed.astype(BF16)
    rows_feed = product("slrt,std->lsrd", onehot_feed_low, feed_all).astype(BF16)
    cot_rows = product("slrt,std->lsrd", onehot_feed_low, cot_all).astype(BF16)
    gate_part = product("lsrd,ldf->lsrf", rows_feed, gate_full)
    up_part = product("lsrd,ldf->lsrf", rows_feed, up_full)
    sigmoid = jax.nn.sigmoid(gate_part)
    silu = gate_part * sigmoid
    active = silu * up_part
    active_gated = (active * seat_gates_feed).astype(BF16)
    feed_rows = product("lsrf,lfd->lsrd", active_gated, down_full).astype(BF16)
    feed_part = product("slrt,lsrd->std", onehot_feed_low, feed_rows).astype(BF16)
    grad_plain = product("lsrd,lfd->lsrf", cot_rows, down_full)
    gate_terms_feed = jnp.sum(active * grad_plain, axis=-1)
    grad_active = grad_plain * seat_gates_feed
    grad_gate = (grad_active * up_part * sigmoid * (1.0 + gate_part * (1.0 - sigmoid))).astype(BF16)
    grad_up = (grad_active * silu).astype(BF16)
    grad_gate_w = product("lsrd,lsrf->ldf", rows_feed, grad_gate).astype(BF16)
    grad_up_w = product("lsrd,lsrf->ldf", rows_feed, grad_up).astype(BF16)
    grad_input_parts = jnp.stack([grad_gate_w, grad_up_w], axis=1).reshape(
        local_count, 2, n_dp, depth, wide
    )
    grad_input_parts = jnp.transpose(grad_input_parts, (2, 0, 1, 3, 4))
    grad_input_parts = lax.all_to_all(grad_input_parts, "dp", 0, 0, tiled=True)
    grad_rows_feed = (
        product("lsrf,ldf->lsrd", grad_gate, gate_full) + product("lsrf,ldf->lsrd", grad_up, up_full)
    ).astype(BF16)
    grad_feed_part = product("slrt,lsrd->std", onehot_feed_low, grad_rows_feed).astype(BF16)
    grad_down = product("lsrf,lsrd->lfd", active_gated, cot_rows)
    grad_down = lax.dynamic_slice_in_dim(grad_down, offset, share, axis=1)

    def gate_home(terms, onehot, here, by_row, collective_id):
        slot = jnp.sum(
            jnp.where(onehot, jnp.swapaxes(terms, 0, 1)[..., None], 0.0), axis=2
        )
        slot = jnp.sum(jnp.where(here, jnp.swapaxes(slot, 1, 2)[:, :, None, :], 0.0), axis=-1)
        if by_row:
            slot = jnp.swapaxes(slot.reshape(mb, devices, TOK_MB, 2), 0, 1)
        slot = slot.reshape(devices, -1, LANES)
        slot = jnp.pad(slot, ((0, 0), (0, -slot.shape[1] % 8), (0, 0)))
        slot = jnp.sum(exchange(slot, devices, owners, collective_id), axis=0)
        return slot.reshape(-1)[: mb * TOK_MB * 2].reshape(mb, TOK_MB, 2)

    def own_of(by_group, by_row):
        if by_row:
            return lax.dynamic_index_in_dim(
                by_group.reshape((mb, devices, TOK_MB) + by_group.shape[2:]), me, 1, keepdims=False
            )
        return lax.dynamic_index_in_dim(
            by_group.reshape((devices, mb, TOK_MB) + by_group.shape[2:]), me, 0, keepdims=False
        )

    grad_normed_feed = scatter_sum(
        grad_feed_part.reshape(devices, mb, TOK_MB, D), chips, owners, False, 20
    )
    grad_gates_feed = gate_home(gate_terms_feed, onehot_feed, here_feed, False, 4)
    grad_logits_feed = gate_grads(
        own_of(gates_feed, False), grad_gates_feed, own_of(choose_feed, False)
    )
    grad_normed_feed = grad_normed_feed + product(
        "mte,de->mtd", grad_logits_feed, router_feed
    )
    grad_second, grad_gain_feed = norm_backward(second, inverse_feed, gain_feed, grad_normed_feed)
    grad_second = grad_second + own_cotangent

    grad_all = gather_all(grad_second.astype(BF16), chips, owners, True, 5).reshape(
        seqs, row_length, D
    )
    feed_sum = scatter_sum(feed_part.reshape(devices, mb, TOK_MB, D), chips, owners, False, 30)
    result = (second + feed_sum).astype(BF16)[:, None]
    grad_rows = product("slrt,std->lsrd", onehot_mixer_low, grad_all).astype(BF16)
    grad_mixture = product("lsrd,lcd->lsrc", grad_rows, output_weight)
    gate_terms_mixer = jnp.sum(grad_mixture * mixture, axis=-1)
    grad_output = product("lsrc,lsrd->lcd", mixture_gated, grad_rows)
    grad_mixture_heads = (
        (grad_mixture * seat_gates_mixer).astype(BF16).reshape(query_heads.shape)
    )
    grad_probs = product("lsrhd,skhd->lshrk", grad_mixture_heads, value_heads)
    grad_values = product("lshrk,lsrhd->skhd", attn_low, grad_mixture_heads)
    row_dot = jnp.sum(attn_probs * grad_probs, axis=-1, keepdims=True)
    grad_scores = (attn_probs * (grad_probs - row_dot)).astype(BF16)
    grad_queries = product("lshrk,skhd->lsrhd", grad_scores, key_heads).reshape(queries.shape)
    grad_keys = product("lshrk,lsrhd->skhd", grad_scores, query_heads)
    grad_query_pre = (turn(grad_queries, seat_cos, -seat_sin) * scaling).astype(BF16)
    grad_key_value = jnp.concatenate(
        [
            turn(grad_keys.reshape(seqs, row_length, hc), key_cos, -key_sin),
            grad_values.reshape(seqs, row_length, hc),
        ],
        axis=-1,
    ).astype(BF16)
    grad_query = product("lsrd,lsrc->ldc", rows_mixer, grad_query_pre).astype(BF16)
    grad_query = jnp.swapaxes(grad_query.reshape(local_count, n_dp, depth, hc), 0, 1)
    grad_query = lax.all_to_all(grad_query, "dp", 0, 0, tiled=True)
    grad_rows_mixer = product("lsrc,ldc->lsrd", grad_query_pre, query_full).astype(BF16)
    grad_mixer_part = (
        product("slrt,lsrd->std", onehot_mixer_low, grad_rows_mixer)
        + product("stc,dc->std", grad_key_value, key_value_full)
    ).astype(BF16)
    grad_key_value_w = product("std,stc->dc", mixer_all, grad_key_value).astype(BF16)
    grad_normed_mixer = scatter_sum(
        grad_mixer_part.reshape(mb, devices, TOK_MB, D), chips, owners, True, 40
    )
    grad_key_value_w = exchange(
        grad_key_value_w.reshape(devices, slice_rows, 2 * hc), devices, owners, 6
    )
    grad_key_value_w = jnp.sum(
        grad_key_value_w.astype(F32).reshape(n_dp, owners, slice_rows, 2, hc), axis=1
    )
    grad_key_value_w = jnp.transpose(grad_key_value_w, (1, 2, 0, 3)).reshape(slice_rows, 2 * att)
    grad_gates_mixer = gate_home(gate_terms_mixer, onehot_mixer, here_mixer, True, 7)
    grad_logits_mixer = gate_grads(
        own_of(gates_mixer, True), grad_gates_mixer, own_of(choose_mixer, True)
    )
    grad_normed_mixer = grad_normed_mixer + product(
        "mte,de->mtd", grad_logits_mixer, router_mixer
    )
    grad_tokens, grad_gain_mixer = norm_backward(
        own_tokens, inverse_mixer, gain_mixer, grad_normed_mixer
    )
    grad_tokens = (grad_tokens + grad_second).astype(BF16)[:, None]

    gains = jnp.stack([grad_gain_mixer, grad_gain_feed], axis=1).reshape(devices, slice_rows * 2)
    logits = jnp.concatenate(
        [grad_logits_mixer.reshape(-1), grad_logits_feed.reshape(-1)]
    )
    last = jnp.concatenate(
        [gains, jnp.broadcast_to(logits, (devices,) + logits.shape)], axis=1
    )
    last = jnp.pad(last, ((0, 0), (0, -last.shape[1] % (8 * LANES)))).reshape(devices, -1, LANES)
    last = exchange(last, devices, owners, 8).reshape(devices, -1)
    grad_gains = jnp.sum(last[:, : slice_rows * 2], axis=0).reshape(slice_rows, 2)
    logits = last[:, slice_rows * 2 : slice_rows * 2 + 2 * mb * TOK_MB * NEXP].astype(BF16)
    logits = logits.reshape(devices, 2, mb * TOK_MB, NEXP)
    logits_m = jnp.swapaxes(
        logits[:, 0].reshape(devices, mb, TOK_MB, NEXP), 0, 1
    ).reshape(seqs, row_length, NEXP)
    router_m = product("std,ste->de", mixer_all, logits_m)
    router_f = product(
        "std,ste->de", feed_all, logits[:, 1].reshape(groups, group_size, NEXP)
    )
    grad_router = lax.dynamic_slice_in_dim(
        jnp.concatenate([router_m, router_f], axis=1), me * slice_rows, slice_rows, axis=0
    )

    grad_query = jnp.transpose(grad_query.astype(F32), (1, 2, 0, 3)).reshape(
        local_count, depth, att
    )
    pieces = []
    for g in range(2):
        edges = sorted(set(starts) | {s + tiles for s in starts})
        for low, high in zip(edges[:-1], edges[1:]):
            cover = [d for d in range(n_dp) if starts[d] <= low and high <= starts[d] + tiles]
            terms = [
                grad_input_parts[
                    d, :, g, :, (low - starts[d]) * LANES : (high - starts[d]) * LANES
                ].astype(F32)
                for d in cover
            ]
            pieces.append(functools.reduce(jnp.add, terms))
    grad_input = jnp.concatenate(pieces, axis=-1)
    return (
        result, grad_tokens, grad_gains, grad_router, grad_key_value_w, grad_query,
        grad_output, grad_input, grad_down,
    )


def solution(mesh):
    shared = P(("dp", "expert"), None)
    slots = P(None, "dp", "expert", None)
    owned = P("expert", "dp", None)
    return jax.shard_map(
        shards,
        mesh=mesh,
        in_specs=(slots, P(None, "dp"), slots, slots, shared, shared, shared) + (owned,) * 4 + (slots,),
        out_specs=(slots, slots, shared, shared, shared) + (owned,) * 4,
        check_vma=False,
    )
```

```python
import functools

import jax
import jax.numpy as jnp
from jax import lax
from jax.experimental import pallas as pl
from jax.experimental.pallas import tpu as pltpu
from jax.sharding import PartitionSpec as P

MESH = pl.DeviceIdType.MESH
BF16 = jnp.bfloat16
START = 1
F32 = jnp.float32
ANY = pl.BlockSpec(memory_space=pl.ANY)


def expert_factors(owners):
    return (2, owners // 2) if owners % 2 == 0 and owners > 2 else (1, owners)


class Place:
    def __init__(self, chips, first, second):
        dp = lax.axis_index("dp")
        ex = lax.axis_index("expert")
        self.chips, self.first, self.second = chips, first, second
        self.owners, self.n_dp = first * second, chips * 2
        self.dp, self.ex = dp, ex
        self.z, self.k = dp // 2, dp % 2
        self.a, self.b = ex // second, ex % second

    def at(self, z=None, k=None, a=None, b=None):
        z = self.z if z is None else z
        k = self.k if k is None else k
        a = self.a if a is None else a
        b = self.b if b is None else b
        return (z * 2 + k, a * self.second + b)

    def other(self, i):
        number = (self.dp * self.owners + self.ex + i) % (self.n_dp * self.owners)
        return number, (number // self.owners, number % self.owners)

    def greet(self, reach):
        barrier = pltpu.get_barrier_semaphore()

        def hello(target):
            pl.semaphore_signal(barrier, inc=1, device_id=target, device_id_type=MESH)

        if reach == "all":
            count = self.n_dp * self.owners - 1

            def one(i, carried):
                hello(self.other(i)[1])
                return carried

            lax.fori_loop(1, count + 1, one, 0)
            pl.semaphore_wait(barrier, count)
            return
        if reach in ("column", "dp"):
            for i in range(1, self.n_dp):
                hello(((self.dp + i) % self.n_dp, self.ex))
        if reach == "column":
            pl.semaphore_wait(barrier, self.n_dp - 1)
            return
        for i in range(1, self.first):
            hello(self.at(a=(self.a + i) % self.first))
        for i in range(1, self.second):
            hello(self.at(b=(self.b + i) % self.second))
        if reach == "dp":
            pl.semaphore_wait(barrier, self.first + self.second + self.n_dp - 3)
            return
        hello(self.at(k=1 - self.k))
        pl.when(self.z > 0)(lambda: hello(self.at(z=self.z - 1)))
        pl.when(self.z < self.chips - 1)(lambda: hello(self.at(z=self.z + 1)))
        along = (self.z > 0).astype(jnp.int32) + (self.z < self.chips - 1).astype(jnp.int32)
        pl.semaphore_wait(barrier, self.first + self.second - 1 + along)


def remote(src, dst, send, recv, target):
    return pltpu.make_async_remote_copy(
        src_ref=src, dst_ref=dst, send_sem=send, recv_sem=recv, device_id=target, device_id_type=MESH
    )


class Job:
    def __init__(self, src, out_shape, pick, put):
        self.src, self.out_shape, self.pick, self.put = src, out_shape, pick, put


class Load:
    def __init__(self, jobs, me, srcs, outs, sems):
        self.jobs, self.me, self.srcs, self.outs = jobs, me, srcs, outs
        self.own, self.send, self.recv = sems if jobs else (None,) * 3

    def peers(self):
        return [(i, (self.me.dp + i) % self.me.n_dp) for i in range(1, self.me.n_dp)]

    def copy(self, j, i, d):
        me, job = self.me, self.jobs[j]
        return remote(
            job.pick(self.srcs[j], d), job.put(self.outs[j], me.dp),
            self.send.at[j, i], self.recv.at[j, me.dp], (d, me.ex),
        )

    def stay(self, j):
        job, dp = self.jobs[j], self.me.dp
        return pltpu.make_async_copy(
            job.pick(self.srcs[j], dp), job.put(self.outs[j], dp), self.own.at[j]
        )

    def start(self):
        for j in range(len(self.jobs)):
            for i, d in self.peers():
                self.copy(j, i, d).start()
            self.stay(j).start()

    def landed(self, j):
        self.stay(j).wait()
        for i, d in self.peers():
            dst = self.jobs[j].put(self.outs[j], d)
            remote(dst, dst, self.send.at[j, i], self.recv.at[j, d], (d, self.me.ex)).wait_recv()

    def finish(self, skip=()):
        for j in range(len(self.jobs)):
            if j not in skip:
                self.landed(j)
            for i, d in self.peers():
                self.copy(j, i, d).wait_send()

    @staticmethod
    def scratch(jobs, n_dp):
        if not jobs:
            return []
        sem = pltpu.SemaphoreType.DMA
        return [sem((len(jobs),)), sem((len(jobs), n_dp)), sem((len(jobs), n_dp))]


class Carried:
    def __init__(self, jobs, chips, owners, refs, ins, outs):
        first, second = expert_factors(owners)
        n = len(jobs)
        refs = list(refs)
        srcs = refs[ins : ins + n]
        results = refs[ins + n + outs : ins + 2 * n + outs]
        sems = refs[len(refs) - 3 :] if n else []
        kept = refs[:ins] + refs[ins + n : ins + n + outs] + refs[ins + 2 * n + outs :]
        self.refs = kept[: len(kept) - 3] if n else kept
        self.jobs = jobs
        if n:
            self.me = Place(chips, first, second)
            self.load = Load(jobs, self.me, srcs, results, sems)

    def start(self):
        if self.jobs:

            @pl.when(pl.program_id(0) == 0)
            def _():
                self.me.greet("column")
                self.load.start()

    def finish(self):
        if self.jobs:
            pl.when(pl.program_id(0) == pl.num_programs(0) - 1)(self.load.finish)


class Mail:
    def __init__(self, arrays, me, srcs, outs, sems):
        self.arrays, self.me, self.srcs, self.outs = arrays, me, srcs, outs
        self.devices = me.n_dp * me.owners
        self.number = me.dp * me.owners + me.ex
        self.own, self.send, self.recv = sems if arrays else (None,) * 3

    def part(self, j, n):
        return self.srcs[j].at[0 if self.arrays[j].shape[0] == 1 else n]

    def copy(self, j, i):
        n, where = self.me.other(i)
        return remote(
            self.part(j, n), self.outs[j].at[self.number], self.send.at[j, i],
            self.recv.at[j, self.number], where,
        )

    def stay(self, j):
        return pltpu.make_async_copy(
            self.part(j, self.number), self.outs[j].at[self.number], self.own.at[j]
        )

    def start(self):
        for j in range(len(self.arrays)):

            def one(i, carried, j=j):
                self.copy(j, i).start()
                return carried

            self.stay(j).start()
            lax.fori_loop(1, self.devices, one, 0)

    def finish(self):
        for j in range(len(self.arrays)):

            def one(i, carried, j=j):
                n, where = self.me.other(i)
                there = self.outs[j].at[n]
                remote(there, there, self.send.at[j, i], self.recv.at[j, n], where).wait_recv()
                self.copy(j, i).wait_send()
                return carried

            self.stay(j).wait()
            lax.fori_loop(1, self.devices, one, 0)

    @staticmethod
    def scratch(arrays, devices):
        if not arrays:
            return []
        sem = pltpu.SemaphoreType.DMA
        return [sem((len(arrays),)), sem((len(arrays), devices)), sem((len(arrays), devices))]

    @staticmethod
    def shapes(arrays, devices):
        return [jax.ShapeDtypeStruct((devices,) + a.shape[1:], a.dtype) for a in arrays]


class Gather:
    def __init__(self, me, by_row, x_ref, out_ref, sems):
        self.me, self.by_row, self.x_ref, self.out_ref = me, by_row, x_ref, out_ref
        self.own_sem, self.recv, self.sends = sems
        self.pending = []
        self.own = self.index(me.z, me.a, me.b)

    @staticmethod
    def scratch(chips, first, second):
        sem = pltpu.SemaphoreType.DMA
        sends = 4 + (2 * chips - 1) * (
            2 + 2 * (first + second - 1) + 2 * (second - 1) * first + 2 * (first - 1) * second
        )
        return [sem((2,)), sem((chips * 2 * first * second, 2)), sem((sends,))]

    def index(self, z, a, b):
        return (z * 2 + self.me.k) * self.me.owners + a * self.me.second + b

    def piece(self, blk, h):
        return self.out_ref.at[h, blk] if self.by_row else self.out_ref.at[blk, h]

    def push(self, src, blk, h, target, when=None):
        copy = remote(
            src, self.piece(blk, h), self.sends.at[len(self.pending)], self.recv.at[blk, h], target
        )
        self.pending.append((copy, when))
        copy.start() if when is None else pl.when(when)(copy.start)

    def landed(self, blk, h, when=None):
        there = self.piece(blk, h)
        copy = remote(there, there, self.sends.at[0], self.recv.at[blk, h], self.me.at())
        copy.wait_recv() if when is None else pl.when(when)(copy.wait_recv)

    def spread(self, blk, source, when=None):
        me = self.me
        for h in range(2):
            for i in range(1, me.second):
                self.push(source(h), blk, h, me.at(b=(me.b + i) % me.second), when)
            for i in range(1, me.first):
                self.push(source(h), blk, h, me.at(a=(me.a + i) % me.first), when)
        for h in range(2):
            self.push(source(h), blk, h, me.at(k=1 - me.k), when)

    def relay(self, z, when):
        me = self.me
        for h in range(2):
            if h == 0:
                froms = [(me.a, (me.b + i) % me.second) for i in range(1, me.second)]
                onward = [dict(a=(me.a + i) % me.first) for i in range(1, me.first)]
            else:
                froms = [((me.a + i) % me.first, me.b) for i in range(1, me.first)]
                onward = [dict(b=(me.b + i) % me.second) for i in range(1, me.second)]
            for a, b in froms:
                blk = self.index(z, a, b)
                self.landed(blk, h, when)
                for target in onward:
                    self.push(self.piece(blk, h), blk, h, me.at(**target), when)
                self.push(self.piece(blk, h), blk, h, me.at(k=1 - me.k), when)

    def settle(self, z, when):
        me = self.me
        for h in range(2):
            for i in range(1, me.second if h else me.first):
                for j in range(me.first if h else me.second):
                    if h == 0:
                        a, b = (me.a + i) % me.first, (me.b + j) % me.second
                    else:
                        a, b = (me.a + j) % me.first, (me.b + i) % me.second
                    blk = self.index(z, a, b)
                    self.landed(blk, h, when)
                    self.push(self.piece(blk, h), blk, h, me.at(k=1 - me.k), when)

    def begin(self):
        me, x_ref, own = self.me, self.x_ref, self.own
        self.stays = [
            pltpu.make_async_copy(x_ref.at[h], self.piece(own, h), self.own_sem.at[h])
            for h in range(2)
        ]
        for stay in self.stays:
            stay.start()
        for h in range(2):
            self.push(x_ref.at[h], own, h, me.at(z=me.z + 1), me.z < me.chips - 1)
            self.push(x_ref.at[h], own, h, me.at(z=me.z - 1), me.z > 0)
        self.spread(own, lambda h: x_ref.at[h])
        self.queue = [(me.z, None)]

    def stage(self, t):
        me, fresh = self.me, []
        for sign in (-1, 1):
            z = me.z + sign * t
            there = (z >= 0) if sign < 0 else (z < me.chips)
            blk = self.index(z, me.a, me.b)
            further = (me.z < me.chips - 1) if sign < 0 else (me.z > 0)
            for h in range(2):
                self.landed(blk, h, there)
                self.push(self.piece(blk, h), blk, h, me.at(z=me.z - sign), there & further)
            self.spread(blk, lambda h, blk=blk: self.piece(blk, h), there)
            fresh.append((z, there))
        self.drain()
        self.queue = fresh

    def drain(self):
        for z, there in self.queue:
            self.relay(z, there)
        for z, there in self.queue:
            self.settle(z, there)

    def finish(self):
        me = self.me
        for stay in self.stays:
            stay.wait()
        for z in range(me.chips):
            for e in range(me.owners):
                for h in range(2):
                    self.landed((z * 2 + 1 - me.k) * me.owners + e, h)
        for copy, when in self.pending:
            copy.wait_send() if when is None else pl.when(when)(copy.wait_send)


def taken(refs, number):
    return [refs.pop(0) for _ in range(number)]


def gather_kernel(chips, first, second, orders, jobs, mails, *refs):
    me = Place(chips, first, second)
    refs = list(refs)
    x_refs = taken(refs, len(orders))
    mail_srcs = taken(refs, len(mails))
    srcs = taken(refs, len(jobs))
    out_refs = taken(refs, len(orders))
    mail_outs = taken(refs, len(mails))
    outs = taken(refs, len(jobs))
    gathers = [
        Gather(me, by_row, x_ref, out_ref, taken(refs, 3))
        for by_row, x_ref, out_ref in zip(orders, x_refs, out_refs)
    ]
    if mails:
        spread_send, spread_recv = taken(refs, 2)
        mail = Mail(mails, me, mail_srcs, mail_outs, taken(refs, 3))
    load = Load(jobs, me, srcs, outs, refs)
    me.greet("all" if mails else "dp" if jobs else "near")
    for gather in gathers:
        gather.begin()
    if mails:
        mail.start()
    for t in range(1, chips):
        for gather in gathers:
            gather.stage(t)
        if t == min(START, chips - 1):
            load.start()
    for gather in gathers:
        gather.drain()
    if mails:
        j = len(jobs) - 1
        load.landed(j)
        column = outs[j].at[:, me.ex]
        spreads = [
            remote(
                column, column, spread_send.at[i], spread_recv.at[me.ex],
                (me.dp, (me.ex + i) % me.owners),
            )
            for i in range(1, me.owners)
        ]
        for copy in spreads:
            copy.start()
        mail.finish()
        for i in range(1, me.owners):
            e = (me.ex + i) % me.owners
            there = outs[j].at[:, e]
            remote(there, there, spread_send.at[i], spread_recv.at[e], (me.dp, e)).wait_recv()
        for copy in spreads:
            copy.wait_send()
    for gather in gathers:
        gather.finish()
    load.finish(skip=(len(jobs) - 1,) if mails else ())


def gather_all(xs, orders, chips, owners, collective_id, jobs=(), mails=()):
    first, second = expert_factors(owners)
    blocks = chips * 2 * owners
    sem = pltpu.SemaphoreType.DMA
    shapes = []
    for x, by_row in zip(xs, orders):
        rest = x.shape[1:]
        shape = (2, blocks) + rest if by_row else (blocks, 2) + rest
        shapes.append(jax.ShapeDtypeStruct(shape, x.dtype))
    shapes += Mail.shapes(mails, blocks) + [job.out_shape for job in jobs]
    ins = list(xs) + list(mails) + [job.src for job in jobs]
    scratch = Gather.scratch(chips, first, second) * len(xs)
    if mails:
        scratch += [sem((owners,)), sem((owners,))] + Mail.scratch(mails, blocks)
    return pl.pallas_call(
        functools.partial(
            gather_kernel, chips, first, second, orders, jobs,
            [jax.ShapeDtypeStruct(a.shape, a.dtype) for a in mails],
        ),
        out_shape=shapes,
        in_specs=[ANY] * len(ins),
        out_specs=[ANY] * len(shapes),
        scratch_shapes=scratch + Load.scratch(jobs, chips * 2),
        compiler_params=pltpu.CompilerParams(collective_id=collective_id, has_side_effects=True),
    )(*ins)


def scatter_kernel(
    chips, first, second, by_row, column, width, jobs, mails, *refs
):
    me = Place(chips, first, second)
    owners = first * second
    n, m = len(jobs), len(mails)
    p_ref, srcs, mail_srcs = refs[0], refs[1 : n + 1], refs[n + 1 : n + m + 1]
    refs = refs[n + m + 1 :]
    out_ref, outs, mail_outs = refs[0], refs[1 : n + 1], refs[n + 1 : n + m + 1]
    refs = refs[n + m + 1 :]
    mine, fromk, a0, b0, b1, a1, fromz, total = refs[:8]
    load_sem, ks, a0s, b0s, b1s, a1s, zs, sends = refs[8:16]
    refs = refs[16:]
    mail = Mail(mails, me, mail_srcs, mail_outs, refs[:3])
    carried = Load(jobs, me, srcs, outs, refs[3:] if mails else refs)
    me.greet("all" if mails else "dp" if jobs else "near")
    pending = []

    def push(src, dst, sem, target, when=None):
        copy = remote(src, dst, sends.at[len(pending)], sem, target)
        pending.append((copy, when))
        copy.start() if when is None else pl.when(when)(copy.start)

    def landed(dst, sem):
        remote(dst, dst, sends.at[0], sem, me.at()).wait_recv()

    low = me.z < chips // 2

    def line(t):
        return jnp.where(
            low,
            jnp.where(t < chips - 1 - me.z, chips - 1 - t, t - (chips - 1 - me.z)),
            jnp.where(t < me.z, t, chips - 1 - (t - me.z)),
        )

    cut = pl.ds(column, width)

    def block(z, k, e):
        blk = (z * 2 + k) * owners + e
        return p_ref.at[:, blk, :, cut] if by_row else p_ref.at[blk, :, :, cut]

    loads = {}
    for t in range(chips):
        z = line(t)
        for e in range(owners):
            load = pltpu.make_async_copy(
                block(z, me.k, e), mine.at[t, e], load_sem.at[t, e]
            )
            load.start()
            loads[t, e] = load
            push(
                block(z, 1 - me.k, e),
                fromk.at[t, e], ks.at[t, e], me.at(k=1 - me.k),
            )

    mail.start()
    carried.start()

    def add(*terms):
        value = terms[0].astype(F32)
        for term in terms[1:]:
            value = value + term.astype(F32)
        return value

    def step_one(t):
        for i in range(first):
            for j in range(second):
                a, b = (me.a + 1 + i) % first, (me.b + 1 + j) % second
                e = a * second + b
                loads_sem = load_sem.at[t, e]
                pltpu.make_async_copy(mine.at[t, e], mine.at[t, e], loads_sem).wait()
                landed(fromk.at[t, e], ks.at[t, e])
                mine[t, e] = add(mine[t, e], fromk[t, e]).astype(BF16)
                if i < first - 1:
                    push(
                        mine.at[t, e, 0], a0.at[t, first - 2 - i, b],
                        a0s.at[t, first - 2 - i, b], me.at(a=a),
                    )
                if j < second - 1:
                    push(
                        mine.at[t, e, 1], b1.at[t, second - 2 - j, a],
                        b1s.at[t, second - 2 - j, a], me.at(b=b),
                    )

    def step_two(t):
        for j in range(second - 1):
            b = (me.b + 1 + j) % second
            e = me.a * second + b
            for i in range(first - 1):
                landed(a0.at[t, i, b], a0s.at[t, i, b])
            mine[t, e, 0] = add(
                mine[t, e, 0], *[a0[t, i, b] for i in range(first - 1)]
            ).astype(BF16)
            push(
                mine.at[t, e, 0], b0.at[t, second - 2 - j],
                b0s.at[t, second - 2 - j], me.at(b=b),
            )
        for i in range(first - 1):
            a = (me.a + 1 + i) % first
            e = a * second + me.b
            for j in range(second - 1):
                landed(b1.at[t, j, a], b1s.at[t, j, a])
            mine[t, e, 1] = add(
                mine[t, e, 1], *[b1[t, j, a] for j in range(second - 1)]
            ).astype(BF16)
            push(
                mine.at[t, e, 1], a1.at[t, first - 2 - i],
                a1s.at[t, first - 2 - i], me.at(a=a),
            )

    def step_three(t):
        z = line(t)
        e = me.ex
        for i in range(first - 1):
            landed(a0.at[t, i, me.b], a0s.at[t, i, me.b])
            landed(a1.at[t, i], a1s.at[t, i])
        for j in range(second - 1):
            landed(b1.at[t, j, me.a], b1s.at[t, j, me.a])
            landed(b0.at[t, j], b0s.at[t, j])
        total[t, 0] = add(
            mine[t, e, 0], *[a0[t, i, me.b] for i in range(first - 1)],
            *[b0[t, j] for j in range(second - 1)],
        )
        total[t, 1] = add(
            mine[t, e, 1], *[b1[t, j, me.a] for j in range(second - 1)],
            *[a1[t, i] for i in range(first - 1)],
        )
        if t < chips - 1:
            up = z > me.z
            from_beyond = jnp.where(up, me.z > 0, me.z < chips - 1)

            @pl.when(from_beyond)
            def _():
                landed(fromz.at[z], zs.at[z])
                total[t] = total[t] + fromz[z].astype(F32)

            mine[t, e] = total[t].astype(BF16)
            push(mine.at[t, e], fromz.at[z], zs.at[z], me.at(z=me.z + 1), up)
            slot = jnp.where(z == me.z - 1, chips, z)
            push(mine.at[t, e], fromz.at[slot], zs.at[slot], me.at(z=me.z - 1), jnp.logical_not(up))
        else:

            @pl.when(me.z > 0)
            def _():
                landed(fromz.at[me.z], zs.at[me.z])
                total[t] = total[t] + fromz[me.z].astype(F32)

            @pl.when(me.z < chips - 1)
            def _():
                landed(fromz.at[chips], zs.at[chips])
                total[t] = total[t] + fromz[chips].astype(F32)

            out_ref[...] = total[t]

    for t in range(chips + 2):
        if t < chips:
            step_one(t)
        if 0 <= t - 1 < chips:
            step_two(t - 1)
        if 0 <= t - 2 < chips:
            step_three(t - 2)
    mail.finish()
    carried.finish()
    for copy, when in pending:
        copy.wait_send() if when is None else pl.when(when)(copy.wait_send)


def scatter_sum(p, chips, owners, by_row, collective_id, jobs=(), mails=()):
    first, second = expert_factors(owners)
    half, full = p.shape[2:]
    parts = 1
    while chips * owners * half * (full // parts) * 8 > 20 * 2**20:
        parts *= 2
    width = full // parts
    one = max(first - 1, 1), max(second - 1, 1)
    sends = chips * (owners + 2 + 2 * (first - 1) * second + 2 * (second - 1) * first)
    sends += chips * (first + second)

    def call(part, jobs, mails):
        sem = pltpu.SemaphoreType.DMA
        return pl.pallas_call(
            functools.partial(scatter_kernel, chips, first, second, by_row, part * width, width, jobs, mails),
            out_shape=[jax.ShapeDtypeStruct((2, half, width), F32)]
            + [job.out_shape for job in jobs]
            + Mail.shapes(mails, chips * 2 * owners),
            in_specs=[ANY] * (1 + len(jobs) + len(mails)),
            out_specs=[pl.BlockSpec(memory_space=pltpu.VMEM)] + [ANY] * (len(jobs) + len(mails)),
            scratch_shapes=[
                pltpu.VMEM((chips, owners, 2, half, width), BF16),
                pltpu.VMEM((chips, owners, 2, half, width), BF16),
                pltpu.VMEM((chips, one[0], second, half, width), BF16),
                pltpu.VMEM((chips, one[1], half, width), BF16),
                pltpu.VMEM((chips, one[1], first, half, width), BF16),
                pltpu.VMEM((chips, one[0], half, width), BF16),
                pltpu.VMEM((chips + 1, 2, half, width), BF16),
                pltpu.VMEM((chips, 2, half, width), F32),
                sem((chips, owners)),
                sem((chips, owners)),
                sem((chips, one[0], second)),
                sem((chips, one[1])),
                sem((chips, one[1], first)),
                sem((chips, one[0])),
                sem((chips + 1,)),
                sem((sends,)),
            ]
            + Mail.scratch(mails, chips * 2 * owners)
            + Load.scratch(jobs, chips * 2),
            compiler_params=pltpu.CompilerParams(
                collective_id=collective_id + part, has_side_effects=True,
                vmem_limit_bytes=60 * 2**20,
            ),
        )(p, *[job.src for job in jobs], *mails)

    calls = [
        call(part, () if part else jobs, () if part else mails) for part in range(parts)
    ]
    whole = calls[0][0] if parts == 1 else jnp.concatenate([c[0] for c in calls], axis=-1)
    return [whole] + list(calls[0][1:])


def exchange_kernel(chips, first, second, array, x_ref, out_ref, *sems):
    me = Place(chips, first, second)
    mail = Mail([array], me, [x_ref], [out_ref], sems)
    me.greet("all")
    mail.start()
    mail.finish()


def exchange(x, chips, owners, collective_id):
    first, second = expert_factors(owners)
    devices = chips * 2 * owners
    shape = jax.ShapeDtypeStruct(x.shape, x.dtype)
    return pl.pallas_call(
        functools.partial(exchange_kernel, chips, first, second, shape),
        out_shape=shape,
        in_specs=[ANY],
        out_specs=ANY,
        scratch_shapes=Mail.scratch([shape], devices),
        compiler_params=pltpu.CompilerParams(collective_id=collective_id, has_side_effects=True),
    )(x)


D = 2048
KVH = 16
HD = 128
FF = 5632
NEXP = 8
TOK_MB = 64
CAP = 24
LANES = 128
EPSILON = 1e-06


def dot(a, b):
    return jnp.dot(a, b, preferred_element_type=F32)


def dot_nt(a, b):
    return lax.dot_general(a, b, (((1,), (1,)), ((), ())), preferred_element_type=F32)


def dot_tn(a, b):
    return lax.dot_general(a, b, (((0,), (0,)), ((), ())), preferred_element_type=F32)


def counted(shape, axis):
    return lax.broadcasted_iota(jnp.int32, shape, axis).astype(F32)


def two_parts(value):
    upper = value.astype(BF16)
    return upper, (value - upper.astype(F32)).astype(BF16)


class Seats:
    def __init__(self, meta, first_expert, count, tri, eye):
        slots = meta.shape[1]
        per = slots // TOK_MB * CAP
        self.count, self.per, self.slots, self.first = count, per, slots, first_expert
        line = counted(meta.shape, 0)
        expert = first_expert + line
        hit = (meta[0:1] == expert) | (meta[1:2] == expert)
        hit = hit & (line < count)
        rank = dot(jnp.where(hit, 1.0, 0.0).astype(BF16), tri)
        block = lax.broadcasted_iota(jnp.int32, meta.shape, 1) // TOK_MB
        seat = jnp.where(hit, block.astype(F32) * CAP + rank + line * per, -1.0)
        self.routes = dot_nt(eye, meta.astype(BF16))
        column = dot_nt(eye, seat.astype(BF16))
        total = count * per
        row = counted((total, slots), 0)
        lane = counted((slots, total), 1)
        here, there = row == seat[0:1], lane == column[:, 0:1]
        for l in range(1, count):
            here = here | (row == seat[l : l + 1])
            there = there | (lane == column[:, l : l + 1])
        self.take = jnp.where(here, 1.0, 0.0).astype(BF16)
        self.put = jnp.where(there, 1.0, 0.0).astype(BF16)

    def gates(self, logits):
        lane = counted(logits.shape, 1)
        one = jnp.sum(jnp.where(lane == self.routes[:, 0:1], logits, 0.0), axis=1, keepdims=True)
        two = jnp.sum(jnp.where(lane == self.routes[:, 1:2], logits, 0.0), axis=1, keepdims=True)
        highest = jnp.maximum(one, two)
        one, two = jnp.exp(one - highest), jnp.exp(two - highest)
        total = one + two
        return one / total, two / total

    def seat_values(self, pairs, plain):
        lane = counted((self.slots, LANES), 1)
        per_expert = []
        for l in range(self.count):
            expert = self.first + l
            values = [
                jnp.where(self.routes[:, 0:1] == expert, a, 0.0)
                + jnp.where(self.routes[:, 1:2] == expert, b, 0.0)
                for a, b in pairs
            ] + list(plain)
            packed = jnp.zeros((self.slots, LANES), F32)
            for i, value in enumerate(values):
                upper, lower = two_parts(value)
                packed = jnp.where(lane == 2 * i, upper.astype(F32), packed)
                packed = jnp.where(lane == 2 * i + 1, lower.astype(F32), packed)
            part = dot(self.take[l * self.per : (l + 1) * self.per], packed.astype(BF16))
            per_expert.append(
                [part[:, 2 * i : 2 * i + 1] + part[:, 2 * i + 1 : 2 * i + 2] for i in range(len(values))]
            )
        return [
            jnp.concatenate(parts, axis=0) if self.count > 1 else parts[0]
            for parts in zip(*per_expert)
        ]

    def slot_values(self, value):
        total = self.count * self.per
        lane = counted((total, LANES), 1)
        row = counted((total, LANES), 0)
        upper, lower = two_parts(value)
        packed = jnp.zeros((total, LANES), F32)
        for l in range(self.count):
            mine = (row >= l * self.per) & (row < (l + 1) * self.per)
            packed = jnp.where(mine & (lane == 2 * l), upper.astype(F32), packed)
            packed = jnp.where(mine & (lane == 2 * l + 1), lower.astype(F32), packed)
        back = dot(self.put, packed.astype(BF16))
        out = jnp.zeros((self.slots, 8), F32)
        lane = counted((self.slots, 8), 1)
        for l in range(self.count):
            value = back[:, 2 * l : 2 * l + 1] + back[:, 2 * l + 1 : 2 * l + 2]
            for k in range(2):
                chosen = (self.routes[:, k : k + 1] == self.first + l) & (lane == k)
                out = jnp.where(chosen, value, out)
        return out


def first_expert(count):
    return (lax.axis_index("expert") * count).astype(F32)


def turned(values, cosine, sine):
    heads = []
    for h in range(values.shape[1] // HD):
        head = values[:, h * HD : (h + 1) * HD]
        heads.append(head * cosine + pltpu.roll(head, HD // 2, 1) * sine)
    return heads[0] if len(heads) == 1 else jnp.concatenate(heads, axis=1)


def mixer_forward_kernel(count, jobs, chips, owners, *refs):
    carried = Carried(jobs, chips, owners, refs, 12, 10)
    (
        length_ref, x_ref, meta_ref, gain_ref, router_ref, wq_ref, wkv_ref, wo_ref,
        tri_ref, eye_ref, upper_ref, lower_ref,
        normed_ref, part_ref, rows_ref, key_ref, value_ref, query_ref, mix_ref, gated_ref, info_ref, gates_ref,
    ) = carried.refs
    carried.start()
    hc = key_ref.shape[2]
    x = x_ref[0].astype(F32)
    inverse = lax.rsqrt(jnp.mean(x * x, axis=1, keepdims=True) + EPSILON)
    normed = (x * inverse * gain_ref[...]).astype(BF16)
    normed_ref[0] = normed
    seats = Seats(meta_ref[0], first_expert(count), count, tri_ref[...], eye_ref[...])
    one, two = seats.gates(dot(normed, router_ref[...]))
    lane = counted((seats.slots, 8), 1)
    gates_ref[0] = jnp.where(lane == 0, one, jnp.where(lane == 1, two, 0.0))
    gate, place = seats.seat_values([(one, two)], [counted((seats.slots, 1), 0)])
    lane = counted((gate.shape[0], 8), 1)
    info_ref[0] = jnp.where(lane == 0, gate, jnp.where(lane == 1, place, 0.0))

    key_value = dot(normed, wkv_ref[...])
    upper, lower = upper_ref[...], lower_ref[...]
    table = upper.astype(F32) + lower.astype(F32)
    key = turned(key_value[:, :hc], table[:, :HD], table[:, HD:]).astype(BF16)
    value = key_value[:, hc:].astype(BF16)
    key_ref[0], value_ref[0] = key, value

    rows = dot(seats.take, normed).astype(BF16)
    per = seats.per
    for l in range(count):
        rows_ref[l] = rows[l * per : (l + 1) * per]
    table = dot(seats.take, upper) + dot(seats.take, lower)
    query = [dot(rows[l * per : (l + 1) * per], wq_ref[l]) for l in range(count)]
    query = query[0] if count == 1 else jnp.concatenate(query, axis=0)
    query = (turned(query, table[:, :HD], table[:, HD:]) * HD ** (-0.5)).astype(BF16)
    query_ref[0] = query

    at = counted((seats.take.shape), 1)
    length = length_ref[pl.program_id(0)].astype(F32)
    allowed = (at <= place) & (at < length)
    mix = []
    for h in range(hc // HD):
        cut = slice(h * HD, (h + 1) * HD)
        scores = jnp.where(allowed, dot_nt(query[:, cut], key[:, cut]), -1e30)
        exponent = jnp.exp(scores - jnp.max(scores, axis=1, keepdims=True))
        probs = (exponent / jnp.sum(exponent, axis=1, keepdims=True)).astype(BF16)
        mix.append(dot(probs, value[:, cut]))
    mix = mix[0] if len(mix) == 1 else jnp.concatenate(mix, axis=1)
    mix_ref[0] = mix
    gated = (mix * gate).astype(BF16)
    for l in range(count):
        gated_ref[l] = gated[l * per : (l + 1) * per]
    out = [dot(gated[l * per : (l + 1) * per], wo_ref[l]).astype(BF16) for l in range(count)]
    out = out[0] if count == 1 else jnp.concatenate(out, axis=0)
    part_ref[0] = dot(seats.put, out).astype(BF16)
    carried.finish()


def mixer_backward_kernel(count, jobs, chips, owners, *refs):
    carried = Carried(jobs, chips, owners, refs, 15, 5)
    (
        length_ref, grad_ref, meta_ref, wq_ref, wkv_ref, wo_ref, tri_ref, eye_ref,
        upper_ref, lower_ref, key_ref, value_ref, query_ref, mix_ref, info_ref,
        part_ref, rows_ref, terms_ref, grad_query_ref, grad_key_value_ref,
    ) = carried.refs
    carried.start()
    hc = key_ref.shape[2]
    seats = Seats(meta_ref[0], first_expert(count), count, tri_ref[...], eye_ref[...])
    per = seats.per
    rows = dot(seats.take, grad_ref[0]).astype(BF16)
    for l in range(count):
        rows_ref[l] = rows[l * per : (l + 1) * per]
    grad_mix = [dot_nt(rows[l * per : (l + 1) * per], wo_ref[l]) for l in range(count)]
    grad_mix = grad_mix[0] if count == 1 else jnp.concatenate(grad_mix, axis=0)
    gate, place = info_ref[0, :, 0:1], info_ref[0, :, 1:2]
    terms_ref[0] = seats.slot_values(jnp.sum(grad_mix * mix_ref[0], axis=1, keepdims=True))
    grad_mix = (grad_mix * gate).astype(BF16)

    at = counted(seats.take.shape, 1)
    length = length_ref[pl.program_id(0)].astype(F32)
    allowed = (at <= place) & (at < length)
    key, value, query = key_ref[0], value_ref[0], query_ref[0]
    grad_query, grad_key, grad_value = [], [], []
    for h in range(hc // HD):
        cut = slice(h * HD, (h + 1) * HD)
        scores = jnp.where(allowed, dot_nt(query[:, cut], key[:, cut]), -1e30)
        exponent = jnp.exp(scores - jnp.max(scores, axis=1, keepdims=True))
        probs = exponent / jnp.sum(exponent, axis=1, keepdims=True)
        grad_probs = dot_nt(grad_mix[:, cut], value[:, cut])
        grad_value.append(dot_tn(probs.astype(BF16), grad_mix[:, cut]))
        row_dot = jnp.sum(probs * grad_probs, axis=1, keepdims=True)
        grad_scores = (probs * (grad_probs - row_dot)).astype(BF16)
        grad_query.append(dot(grad_scores, key[:, cut]))
        grad_key.append(dot_tn(grad_scores, query[:, cut]))

    def joined(parts):
        return parts[0] if len(parts) == 1 else jnp.concatenate(parts, axis=1)

    upper, lower = upper_ref[...], lower_ref[...]
    table = dot(seats.take, upper) + dot(seats.take, lower)
    grad_query = turned(joined(grad_query), table[:, :HD], -table[:, HD:]) * HD ** (-0.5)
    grad_query = grad_query.astype(BF16)
    for l in range(count):
        grad_query_ref[l] = grad_query[l * per : (l + 1) * per]
    table = upper.astype(F32) + lower.astype(F32)
    grad_key = turned(joined(grad_key), table[:, :HD], -table[:, HD:])
    grad_key_value = jnp.concatenate([grad_key, joined(grad_value)], axis=1).astype(BF16)
    grad_key_value_ref[0] = grad_key_value
    back = [
        dot_nt(grad_query[l * per : (l + 1) * per], wq_ref[l]).astype(BF16) for l in range(count)
    ]
    back = back[0] if count == 1 else jnp.concatenate(back, axis=0)
    part_ref[0] = (dot(seats.put, back) + dot_nt(grad_key_value, wkv_ref[...])).astype(BF16)
    carried.finish()


def feed_kernel(count, groups, offsets, offset_ref, x_ref, cot_ref, meta_ref, router_ref, wd_ref, tri_ref, eye_ref, *refs):
    wg_ref, wu_ref = refs[0 : 2 * count : 2], refs[1 : 2 * count : 2]
    (
        part_ref, back_ref, rows_ref, cot_rows_ref, active_ref, grad_gate_ref, grad_up_ref, terms_ref,
        gates_ref, out_ref, dx_ref, gate_ref, term_ref,
    ) = refs[2 * count :]
    kept = []
    for g in range(groups):
        seats = Seats(meta_ref[g], first_expert(count), count, tri_ref[...], eye_ref[...])
        kept.append(seats)
        per = seats.per
        one, two = seats.gates(dot(x_ref[g], router_ref[...]))
        lane = counted((seats.slots, 8), 1)
        gates_ref[g] = jnp.where(lane == 0, one, jnp.where(lane == 1, two, 0.0))
        (gate,) = seats.seat_values([(one, two)], [])
        rows = dot(seats.take, x_ref[g]).astype(BF16)
        valid = meta_ref[g][2:3] > 0.0
        cot_rows = dot(jnp.where(valid, seats.take, 0.0).astype(BF16), cot_ref[g]).astype(BF16)
        for l in range(count):
            rows_ref[l, g * per : (g + 1) * per] = rows[l * per : (l + 1) * per]
            cot_rows_ref[l, g * per : (g + 1) * per] = cot_rows[l * per : (l + 1) * per]
            gate_ref[l, g * per : (g + 1) * per] = jnp.broadcast_to(
                gate[l * per : (l + 1) * per], (per, LANES)
            )
    wide = wd_ref.shape[1]
    for l in range(count):
        rows, cot_rows, gate = rows_ref[l], cot_rows_ref[l], gate_ref[l][:, 0:1]
        gate_part = dot(rows, wg_ref[l][...])
        up_part = dot(rows, wu_ref[l][...])
        grad_plain = dot_nt(cot_rows, wd_ref[l])
        sigmoid = 1.0 / (1.0 + jnp.exp(-gate_part))
        silu = gate_part * sigmoid
        active = silu * up_part
        gated = active * gate
        front = gated
        for off in offsets:
            front = jnp.where(offset_ref[0] == off, pltpu.roll(gated, wide - off, 1), front)
        active_ref[l] = front.astype(BF16)
        gated = gated.astype(BF16)
        term = jnp.sum(active * grad_plain, axis=1, keepdims=True)
        grad_active = grad_plain * gate
        grad_up = (grad_active * silu).astype(BF16)
        grad_gate = (
            grad_active * up_part * sigmoid * (1.0 + gate_part * (1.0 - sigmoid))
        ).astype(BF16)
        grad_gate_ref[l], grad_up_ref[l] = grad_gate, grad_up
        out = dot(gated, wd_ref[l]).astype(BF16)
        back = (dot_nt(grad_gate, wg_ref[l][...]) + dot_nt(grad_up, wu_ref[l][...])).astype(BF16)
        for g in range(groups):
            out_ref[g, l * per : (l + 1) * per] = out[g * per : (g + 1) * per]
            dx_ref[g, l * per : (l + 1) * per] = back[g * per : (g + 1) * per]
            term_ref[g, l * per : (l + 1) * per] = jnp.broadcast_to(
                term[g * per : (g + 1) * per], (per, LANES)
            )
    for g in range(groups):
        part_ref[g] = dot(kept[g].put, out_ref[g]).astype(BF16)
        back_ref[g] = dot(kept[g].put, dx_ref[g]).astype(BF16)
        terms_ref[g] = kept[g].slot_values(term_ref[g][:, 0:1])


def whole_block(array):
    return pl.BlockSpec(array.shape, lambda i: (0,) * array.ndim)


def step_block(shape, first=1):
    return pl.BlockSpec((first,) + tuple(shape[1:]), lambda i: (i,) + (0,) * (len(shape) - 1))


SMEM = pl.BlockSpec(memory_space=pltpu.SMEM)


def constants(slots):
    at = jnp.arange(slots)
    earlier = (at[:, None] < at[None, :]) & (at[:, None] // TOK_MB == at[None, :] // TOK_MB)
    return earlier.astype(BF16), (at[:, None] == at[None, :]).astype(BF16)


def mixer_tables(slots):
    frequency = 10000.0 ** (-(jnp.arange(HD // 2, dtype=F32) * (2.0 / HD)))
    angles = jnp.arange(slots, dtype=F32)[:, None] * frequency
    cosine, sine = jnp.cos(angles), jnp.sin(angles)
    table = jnp.concatenate([cosine, cosine, -sine, sine], axis=1)
    upper = lax.reduce_precision(table, 8, 7)
    return upper.astype(BF16), (table - upper).astype(BF16)


def mixer_forward(x, meta, lengths, gain, router, wq, wkv, wo, fixed, jobs, chips, owners, collective_id):
    seqs, slots, _ = x.shape
    count, _, hc = wq.shape
    seats = slots // TOK_MB * CAP * count
    per = seats // count

    def by_expert(width):
        shape = (count, seqs * per, width)
        return shape, BF16, pl.BlockSpec((count, per, width), lambda i: (0, i, 0))

    def by_row(rows, width, dtype=BF16):
        shape = (seqs, rows, width)
        return shape, dtype, step_block(shape)

    outs = [
        by_row(slots, D), by_row(slots, D), by_expert(D), by_row(slots, hc), by_row(slots, hc),
        by_row(seats, hc), by_row(seats, hc, F32), by_expert(hc), by_row(seats, 8, F32), by_row(slots, 8, F32),
    ]
    fixed_in = [gain, router, wq, wkv, wo, *fixed]
    return pl.pallas_call(
        functools.partial(mixer_forward_kernel, count, jobs, chips, owners),
        grid=(seqs,),
        out_shape=[jax.ShapeDtypeStruct(shape, dtype) for shape, dtype, _ in outs]
        + [job.out_shape for job in jobs],
        in_specs=[SMEM, step_block(x.shape), step_block(meta.shape)]
        + [whole_block(a) for a in fixed_in]
        + [ANY] * len(jobs),
        out_specs=[spec for _, _, spec in outs] + [ANY] * len(jobs),
        scratch_shapes=Load.scratch(jobs, chips * 2),
        compiler_params=pltpu.CompilerParams(
            vmem_limit_bytes=60 * 2**20,
            collective_id=collective_id if jobs else None,
            has_side_effects=bool(jobs),
        ),
    )(lengths, x, meta, *fixed_in, *[job.src for job in jobs])


def mixer_backward(
    grad, meta, lengths, wq, wkv, wo, fixed, saved, jobs, chips, owners, collective_id
):
    seqs, slots, _ = grad.shape
    count, _, hc = wq.shape
    seats = slots // TOK_MB * CAP * count
    per = seats // count

    def by_expert(width):
        shape = (count, seqs * per, width)
        return shape, BF16, pl.BlockSpec((count, per, width), lambda i: (0, i, 0))

    def by_row(rows, width, dtype=BF16):
        shape = (seqs, rows, width)
        return shape, dtype, step_block(shape)

    outs = [
        by_row(slots, D), by_expert(D), by_row(slots, 8, F32), by_expert(hc), by_row(slots, 2 * hc)
    ]
    fixed_in = [wq, wkv, wo, *fixed]
    return pl.pallas_call(
        functools.partial(mixer_backward_kernel, count, jobs, chips, owners),
        grid=(seqs,),
        out_shape=[jax.ShapeDtypeStruct(shape, dtype) for shape, dtype, _ in outs]
        + [job.out_shape for job in jobs],
        in_specs=[SMEM, step_block(grad.shape), step_block(meta.shape)]
        + [whole_block(a) for a in fixed_in]
        + [step_block(a.shape) for a in saved]
        + [ANY] * len(jobs),
        out_specs=[spec for _, _, spec in outs] + [ANY] * len(jobs),
        scratch_shapes=Load.scratch(jobs, chips * 2),
        compiler_params=pltpu.CompilerParams(
            vmem_limit_bytes=60 * 2**20,
            collective_id=collective_id if jobs else None,
            has_side_effects=bool(jobs),
        ),
    )(lengths, grad, meta, *fixed_in, *saved, *[job.src for job in jobs])


def feed(x, cot, meta, router, wgu, wd, fixed, offset, offsets):
    groups, slots, _ = x.shape
    count, wide, _ = wd.shape
    per = slots // TOK_MB * CAP
    at_once = 2
    seats = groups * per
    shapes = [((groups, slots, D), BF16), ((groups, slots, D), BF16)]
    specs = [step_block(s, at_once) for s, _ in shapes]
    for width in (D, D, wide, wide, wide):
        shapes.append(((count, seats, width), BF16))
        specs.append(pl.BlockSpec((count, at_once * per, width), lambda i: (0, i, 0)))
    for _ in range(2):
        shapes.append(((groups, slots, 8), F32))
        specs.append(step_block(shapes[-1][0], at_once))
    fixed_in = [router, wd, *fixed, *wgu]
    turns = sorted({o for o in offsets if o})
    return pl.pallas_call(
        functools.partial(feed_kernel, count, at_once, turns),
        grid=(groups // at_once,),
        out_shape=[jax.ShapeDtypeStruct(*s) for s in shapes],
        in_specs=[SMEM]
        + [step_block(a.shape, at_once) for a in (x, cot, meta)]
        + [whole_block(a) for a in fixed_in],
        out_specs=specs,
        scratch_shapes=[
            pltpu.VMEM((at_once, count * per, D), BF16),
            pltpu.VMEM((at_once, count * per, D), BF16),
            pltpu.VMEM((count, at_once * per, LANES), F32),
            pltpu.VMEM((at_once, count * per, LANES), F32),
        ],
        compiler_params=pltpu.CompilerParams(vmem_limit_bytes=60 * 2**20),
    )(offset.reshape(1), x, cot, meta, *fixed_in)


def norm_forward(values, norm_gain):
    inverse = lax.rsqrt(jnp.mean(values * values, axis=-1, keepdims=True) + EPSILON)
    return (values * inverse * norm_gain, inverse)


def norm_backward(values, inverse, norm_gain, grad_normed):
    scaled = grad_normed * norm_gain
    grad_gain = jnp.sum(grad_normed * values * inverse, axis=(0, 1))
    grad_values = inverse * scaled - values * inverse**3 * jnp.mean(
        scaled * values, axis=-1, keepdims=True
    )
    return (grad_values, grad_gain)


def gate_grads(gate_probs, grad_gate_probs, routes):
    weighted = jnp.sum(gate_probs * grad_gate_probs, axis=-1, keepdims=True)
    grad_picked = gate_probs * (grad_gate_probs - weighted)
    choose = (routes[..., None] == jnp.arange(NEXP, dtype=jnp.int32)).astype(F32)
    return jnp.sum(grad_picked[..., None] * choose, axis=-2)


def tile_starts(shards):
    share = FF // shards
    most = max(share * d % LANES for d in range(shards))
    tiles = -(-(share + most) // LANES)
    starts = [min(share * d // LANES, FF // LANES - tiles) for d in range(shards)]
    return tiles, starts, [share * d - LANES * starts[d] for d in range(shards)]


def put_together_kernel(count, starts, tiles, *refs):
    out_ref = refs[-1]
    edges = sorted(set(starts) | {s + tiles for s in starts})
    for l in range(count):
        for g in range(2):
            part = refs[l * 2 + g]
            for low, high in zip(edges[:-1], edges[1:]):
                cover = [d for d in range(len(starts)) if starts[d] <= low and high <= starts[d] + tiles]
                value = None
                for d in cover:
                    cut = slice((low - starts[d]) * LANES, (high - starts[d]) * LANES)
                    term = part[d, :, cut].astype(F32)
                    value = term if value is None else value + term
                out_ref[l, :, g * FF + low * LANES : g * FF + high * LANES] = value


def put_together(parts, count, starts, tiles):
    n_dp, depth, wide = parts[0].shape
    rows = 32
    return pl.pallas_call(
        functools.partial(put_together_kernel, count, starts, tiles),
        grid=(depth // rows,),
        out_shape=jax.ShapeDtypeStruct((count, depth, 2 * FF), F32),
        in_specs=[pl.BlockSpec((n_dp, rows, wide), lambda i: (0, i, 0))] * len(parts),
        out_specs=pl.BlockSpec((count, rows, 2 * FF), lambda i: (0, i, 0)),
        compiler_params=pltpu.CompilerParams(vmem_limit_bytes=48 * 2**20),
    )(*parts)


def product(pattern, operand, factor):
    return jnp.einsum(pattern, operand, factor, preferred_element_type=F32)


def shards(
    tokens, lengths, attention_routes, feedforward_routes, norm_gains, router_weight,
    key_value_weight, query_weight, output_weight, input_weight, down_weight, cotangent,
):
    n_dp = lax.axis_size("dp")
    owners = lax.axis_size("expert")
    chips = n_dp // 2
    devices = n_dp * owners
    dp = lax.axis_index("dp")
    ex = lax.axis_index("expert")
    me = dp * owners + ex
    mb = tokens.shape[0]
    count = NEXP // owners
    seqs = mb * n_dp
    slots = owners * TOK_MB
    hc = KVH // n_dp * HD
    att = KVH * HD
    depth = D // n_dp
    slice_rows = D // devices
    tiles, starts, offsets = tile_starts(n_dp)
    share, wide = FF // n_dp, tiles * LANES
    offset = jnp.array(offsets, jnp.int32)[dp]

    def query_job(l):
        return Job(
            query_weight,
            jax.ShapeDtypeStruct((D, hc), BF16),
            lambda src, d: src.at[l, :, pl.ds(pl.multiple_of(d * hc, LANES), hc)],
            lambda out, d: out.at[pl.ds(pl.multiple_of(d * depth, depth), depth)],
        )

    key_value_job = Job(
        jnp.swapaxes(key_value_weight.reshape(slice_rows, 2, att), 0, 1),
        jax.ShapeDtypeStruct((n_dp, owners, 2, slice_rows, hc), BF16),
        lambda src, d: src.at[:, :, pl.ds(pl.multiple_of(d * hc, LANES), hc)],
        lambda out, d: out.at[d, lax.axis_index("expert")],
    )

    def start_of(d):
        start = (share * d) // LANES
        if max(share * i // LANES - starts[i] for i in range(n_dp)):
            start = jnp.minimum(start, FF // LANES - tiles)
        return start

    def input_job(l, g):
        return Job(
            input_weight,
            jax.ShapeDtypeStruct((D, wide), BF16),
            lambda src, d: src.at[
                l, :, pl.ds(pl.multiple_of(g * FF + start_of(d) * LANES, LANES), wide)
            ],
            lambda out, d: out.at[pl.ds(pl.multiple_of(d * depth, depth), depth)],
        )

    def back_job(grad):
        return Job(
            grad,
            jax.ShapeDtypeStruct((n_dp, depth, grad.shape[1]), BF16),
            lambda src, d: src.at[pl.ds(pl.multiple_of(d * depth, depth), depth)],
            lambda out, d: out.at[d],
        )

    def spread_jobs(jobs, places):
        lists = [[] for _ in range(places)]
        for i, job in enumerate(jobs):
            lists[i * places // len(jobs)].append(job)
        return lists

    input_lists = spread_jobs([input_job(l, g) for l in range(count) for g in range(2)], 4)
    input_lists[2] += input_lists.pop()
    down_full = lax.dynamic_update_slice(
        jnp.zeros((count, wide, D), BF16), down_weight, (0, offset, 0)
    )

    def route_lines(routes):
        return jnp.swapaxes(routes[:, 0], 1, 2).reshape(-1, LANES).astype(F32)

    shared = jnp.concatenate([norm_gains, router_weight], axis=1).astype(F32)
    tail = jnp.concatenate([shared.reshape(-1), lengths.reshape(-1).astype(F32)])
    tail = jnp.pad(tail, (0, -tail.shape[0] % LANES)).reshape(-1, LANES)
    small = jnp.concatenate(
        [route_lines(attention_routes), route_lines(feedforward_routes), tail]
    )
    small = jnp.pad(small, ((0, -small.shape[0] % 8), (0, 0)))[None]
    tokens_all, cot_all, small, *resharded = gather_all(
        [tokens[:, 0], cotangent[:, 0]], [True, False], chips, owners, 1,
        [query_job(l) for l in range(count)] + [key_value_job], [small],
    )
    tokens_all = tokens_all.reshape(seqs, slots, D)
    query_full = jnp.stack(resharded[:-1])
    key_value_full = jnp.transpose(resharded[-1], (0, 1, 3, 2, 4)).reshape(D, 2 * hc)
    group_slots = mb * TOK_MB * 2
    groups = devices // 2
    cot_all = cot_all.reshape(groups, group_slots, D)
    lines = mb * 2 * TOK_MB // LANES
    mixer_routes = small[:, :lines].reshape(n_dp, owners, mb, 2, TOK_MB)
    mixer_meta = jnp.transpose(mixer_routes, (2, 0, 3, 1, 4)).reshape(seqs, 2, slots)
    mixer_meta = jnp.pad(mixer_meta, ((0, 0), (0, 6), (0, 0)))
    feed_routes = small[:, lines : 2 * lines].reshape(groups, 2, mb, 2, TOK_MB)
    feed_meta = jnp.transpose(feed_routes, (0, 3, 1, 2, 4)).reshape(groups, 2, group_slots)
    tail = small[:, 2 * lines :].reshape(devices, -1)
    shared_all = tail[:, : slice_rows * 18].reshape(D, 18)
    all_lengths = tail[:, slice_rows * 18 : slice_rows * 18 + mb].reshape(n_dp, owners, mb)
    row_lengths = all_lengths[:, 0].T.reshape(seqs).astype(jnp.int32)
    places = (jnp.arange(owners)[:, None, None] * TOK_MB + jnp.arange(TOK_MB)).astype(F32)
    valid = (places[None] < all_lengths[..., None]).astype(F32).reshape(groups, 1, group_slots)
    feed_meta = jnp.concatenate([feed_meta, valid], axis=1)
    feed_meta = jnp.pad(feed_meta, ((0, 0), (0, 5), (0, 0)))
    gain_mixer, gain_feed = shared_all[:, 0], shared_all[:, 1]
    router_mixer, router_feed = shared_all[:, 2 : 2 + NEXP], shared_all[:, 2 + NEXP :]

    def routers(part):
        return jnp.pad(part.astype(BF16), ((0, 0), (0, LANES - NEXP)))

    own_tokens = tokens[:, 0].astype(F32)
    home_places = ex * TOK_MB + jnp.arange(TOK_MB, dtype=jnp.int32)
    own_valid = (home_places[None, :] < lengths[:, :1]).astype(F32)
    own_cotangent = cotangent[:, 0].astype(F32) * own_valid[..., None]

    normed_mixer, inverse_mixer = norm_forward(own_tokens, gain_mixer)
    fixed = constants(slots)
    tables = mixer_tables(slots)
    (
        mixer_all, mixer_part, rows_mixer, keys, values, queries, mixture, mixture_gated, info,
        gates_mixer, *input_parts,
    ) = mixer_forward(
        tokens_all, mixer_meta, row_lengths, gain_mixer[None], routers(router_mixer), query_full,
        key_value_full, output_weight, (*fixed, *tables), input_lists[0], chips, owners, 2,
    )
    mixer_sum, *more_parts = scatter_sum(
        mixer_part.reshape(mb, devices, TOK_MB, D), chips, owners, True, 10, input_lists[1]
    )
    input_parts += more_parts

    second = own_tokens + mixer_sum
    normed_feed, inverse_feed = norm_forward(second, gain_feed)
    feed_all, *more_parts = gather_all(
        [normed_feed.astype(BF16)], [False], chips, owners, 3, input_lists[2]
    )
    input_parts += more_parts
    feed_all = feed_all.reshape(groups, group_slots, D)
    (
        feed_part, grad_feed_part, rows_feed, cot_rows, active_gated, grad_gate, grad_up,
        gate_terms_feed, gates_feed,
    ) = feed(
        feed_all, cot_all, feed_meta, routers(router_feed), input_parts, down_full,
        constants(group_slots), offset, offsets,
    )
    back_lists = []
    for l in range(count):
        for grad in (grad_gate, grad_up):
            back_lists.append(product("rd,rf->df", rows_feed[l], grad[l]).astype(BF16))
    back_lists = spread_jobs([back_job(grad) for grad in back_lists], 4)
    grad_down = product("lrf,lrd->lfd", active_gated[..., :share], cot_rows)

    def home_parts(terms, by_row):
        terms = terms[..., :2]
        if by_row:
            terms = jnp.swapaxes(terms.reshape(mb, devices, TOK_MB * 2), 0, 1)
        terms = terms.reshape(devices, -1, LANES)
        return jnp.pad(terms, ((0, 0), (0, -terms.shape[1] % 8), (0, 0)))

    def at_home(parts):
        return jnp.sum(parts, axis=0).reshape(-1)[: mb * TOK_MB * 2].reshape(mb, TOK_MB, 2)

    def own_of(gates, by_row):
        gates = gates[..., :2]
        if by_row:
            return lax.dynamic_index_in_dim(
                gates.reshape(mb, devices, TOK_MB, 2), me, 1, keepdims=False
            )
        return lax.dynamic_index_in_dim(
            gates.reshape(devices, mb, TOK_MB, 2), me, 0, keepdims=False
        )

    grad_normed_feed, *grad_input_parts, terms = scatter_sum(
        grad_feed_part.reshape(devices, mb, TOK_MB, D), chips, owners, False, 20, back_lists[0],
        [home_parts(gate_terms_feed, False)],
    )
    grad_logits_feed = gate_grads(
        own_of(gates_feed, False), at_home(terms), feedforward_routes[:, 0]
    )
    grad_normed_feed = grad_normed_feed + product("mte,de->mtd", grad_logits_feed, router_feed)
    grad_second, grad_gain_feed = norm_backward(second, inverse_feed, gain_feed, grad_normed_feed)
    grad_second = grad_second + own_cotangent

    grad_all, *more_parts = gather_all(
        [grad_second.astype(BF16)], [True], chips, owners, 5, back_lists[1]
    )
    grad_input_parts += more_parts
    grad_all = grad_all.reshape(seqs, slots, D)
    feed_sum, *more_parts = scatter_sum(
        feed_part.reshape(devices, mb, TOK_MB, D), chips, owners, False, 30, back_lists[2]
    )
    grad_input_parts += more_parts
    result = (second + feed_sum).astype(BF16)[:, None]
    (
        grad_mixer_part, grad_rows, gate_terms_mixer, grad_query_pre, grad_key_value, *more_parts
    ) = mixer_backward(
        grad_all, mixer_meta, row_lengths, query_full, key_value_full, output_weight,
        (*fixed, *tables), (keys, values, queries, mixture, info), back_lists[3], chips, owners, 6,
    )
    grad_input_parts += more_parts
    grad_output = product("lrc,lrd->lcd", mixture_gated, grad_rows)
    grad_query = [
        product("rd,rc->dc", rows_mixer[l], grad_query_pre[l]).astype(BF16) for l in range(count)
    ]
    grad_key_value_w = product("std,stc->dc", mixer_all, grad_key_value).astype(BF16)
    grad_normed_mixer, *more_parts = scatter_sum(
        grad_mixer_part.reshape(mb, devices, TOK_MB, D), chips, owners, True, 40,
        [back_job(grad) for grad in grad_query],
        [
            home_parts(gate_terms_mixer, True),
            grad_key_value_w.reshape(devices, slice_rows, 2 * hc),
        ],
    )
    *more_parts, terms, grad_key_value_w = more_parts
    grad_query = jnp.stack(more_parts, axis=1)
    grad_key_value_w = jnp.sum(
        grad_key_value_w.astype(F32).reshape(n_dp, owners, slice_rows, 2, hc), axis=1
    )
    grad_key_value_w = jnp.transpose(grad_key_value_w, (1, 2, 0, 3)).reshape(slice_rows, 2 * att)
    grad_logits_mixer = gate_grads(
        own_of(gates_mixer, True), at_home(terms), attention_routes[:, 0]
    )
    grad_normed_mixer = grad_normed_mixer + product("mte,de->mtd", grad_logits_mixer, router_mixer)
    grad_tokens, grad_gain_mixer = norm_backward(
        own_tokens, inverse_mixer, gain_mixer, grad_normed_mixer
    )
    grad_tokens = (grad_tokens + grad_second).astype(BF16)[:, None]

    router_terms = [
        product("mtd,mte->de", normed.astype(BF16), logits.astype(BF16))
        for normed, logits in ((normed_mixer, grad_logits_mixer), (normed_feed, grad_logits_feed))
    ]
    last = jnp.concatenate([grad_gain_mixer[:, None], grad_gain_feed[:, None], *router_terms], axis=1)
    last = last.reshape(devices, slice_rows * 18)
    last = jnp.pad(last, ((0, 0), (0, -last.shape[1] % (8 * LANES)))).reshape(devices, -1, LANES)
    last = jnp.sum(exchange(last, chips, owners, 8), axis=0).reshape(-1)
    last = last[: slice_rows * 18].reshape(slice_rows, 18)
    grad_gains, grad_router = last[:, :2], last[:, 2:]

    grad_query = jnp.transpose(grad_query.astype(F32), (1, 2, 0, 3)).reshape(count, depth, att)
    grad_input = put_together(grad_input_parts, count, starts, tiles)
    return (
        result, grad_tokens, grad_gains, grad_router, grad_key_value_w, grad_query,
        grad_output, grad_input, grad_down,
    )


def solution(mesh):
    shared = P(("dp", "expert"), None)
    slots = P(None, "dp", "expert", None)
    owned = P("expert", "dp", None)
    return jax.shard_map(
        shards,
        mesh=mesh,
        in_specs=(slots, P(None, "dp"), slots, slots, shared, shared, shared) + (owned,) * 4 + (slots,),
        out_specs=(slots, slots, shared, shared, shared) + (owned,) * 4,
        check_vma=False,
    )
```

```python
import functools

import jax
import jax.numpy as jnp
from jax import lax
from jax.experimental import pallas as pl
from jax.experimental.pallas import tpu as pltpu
from jax.sharding import PartitionSpec as P

MESH = pl.DeviceIdType.MESH
BF16 = jnp.bfloat16
F32 = jnp.float32
ANY = pl.BlockSpec(memory_space=pl.ANY)


def expert_factors(owners):
    return (2, owners // 2) if owners % 2 == 0 and owners > 2 else (1, owners)


class Place:
    def __init__(self, chips, first, second):
        dp = lax.axis_index("dp")
        ex = lax.axis_index("expert")
        self.chips, self.first, self.second = chips, first, second
        self.owners, self.n_dp = first * second, chips * 2
        self.dp, self.ex = dp, ex
        self.z, self.k = dp // 2, dp % 2
        self.a, self.b = ex // second, ex % second

    def at(self, z=None, k=None, a=None, b=None):
        z = self.z if z is None else z
        k = self.k if k is None else k
        a = self.a if a is None else a
        b = self.b if b is None else b
        return (z * 2 + k, a * self.second + b)

    def other(self, i):
        number = (self.dp * self.owners + self.ex + i) % (self.n_dp * self.owners)
        return number, (number // self.owners, number % self.owners)

    def greet(self, reach):
        barrier = pltpu.get_barrier_semaphore()

        def hello(target):
            pl.semaphore_signal(barrier, inc=1, device_id=target, device_id_type=MESH)

        if reach == "all":
            count = self.n_dp * self.owners - 1

            def one(i, carried):
                hello(self.other(i)[1])
                return carried

            lax.fori_loop(1, count + 1, one, 0)
            pl.semaphore_wait(barrier, count)
            return
        if reach in ("column", "dp"):
            for i in range(1, self.n_dp):
                hello(((self.dp + i) % self.n_dp, self.ex))
        if reach == "column":
            pl.semaphore_wait(barrier, self.n_dp - 1)
            return
        for i in range(1, self.first):
            hello(self.at(a=(self.a + i) % self.first))
        for i in range(1, self.second):
            hello(self.at(b=(self.b + i) % self.second))
        if reach == "dp":
            pl.semaphore_wait(barrier, self.first + self.second + self.n_dp - 3)
            return
        hello(self.at(k=1 - self.k))
        pl.when(self.z > 0)(lambda: hello(self.at(z=self.z - 1)))
        pl.when(self.z < self.chips - 1)(lambda: hello(self.at(z=self.z + 1)))
        along = (self.z > 0).astype(jnp.int32) + (self.z < self.chips - 1).astype(jnp.int32)
        pl.semaphore_wait(barrier, self.first + self.second - 1 + along)


def remote(src, dst, send, recv, target):
    return pltpu.make_async_remote_copy(
        src_ref=src, dst_ref=dst, send_sem=send, recv_sem=recv, device_id=target, device_id_type=MESH
    )


class Job:
    def __init__(self, src, out_shape, pick, put):
        self.src, self.out_shape, self.pick, self.put = src, out_shape, pick, put


class Load:
    def __init__(self, jobs, me, srcs, outs, sems):
        self.jobs, self.me, self.srcs, self.outs = jobs, me, srcs, outs
        self.own, self.send, self.recv = sems if jobs else (None,) * 3

    def peers(self):
        return [(i, (self.me.dp + i) % self.me.n_dp) for i in range(1, self.me.n_dp)]

    def copy(self, j, i, d):
        me, job = self.me, self.jobs[j]
        return remote(
            job.pick(self.srcs[j], d), job.put(self.outs[j], me.dp),
            self.send.at[j, i], self.recv.at[j, me.dp], (d, me.ex),
        )

    def stay(self, j):
        job, dp = self.jobs[j], self.me.dp
        return pltpu.make_async_copy(
            job.pick(self.srcs[j], dp), job.put(self.outs[j], dp), self.own.at[j]
        )

    def start(self):
        for j in range(len(self.jobs)):
            for i, d in self.peers():
                self.copy(j, i, d).start()
            self.stay(j).start()

    def landed(self, j):
        self.stay(j).wait()
        for i, d in self.peers():
            dst = self.jobs[j].put(self.outs[j], d)
            remote(dst, dst, self.send.at[j, i], self.recv.at[j, d], (d, self.me.ex)).wait_recv()

    def finish(self, skip=()):
        for j in range(len(self.jobs)):
            if j not in skip:
                self.landed(j)
            for i, d in self.peers():
                self.copy(j, i, d).wait_send()

    @staticmethod
    def scratch(jobs, n_dp):
        if not jobs:
            return []
        sem = pltpu.SemaphoreType.DMA
        return [sem((len(jobs),)), sem((len(jobs), n_dp)), sem((len(jobs), n_dp))]


class Mail:
    def __init__(self, arrays, me, srcs, outs, sems):
        self.arrays, self.me, self.srcs, self.outs = arrays, me, srcs, outs
        self.devices = me.n_dp * me.owners
        self.number = me.dp * me.owners + me.ex
        self.own, self.send, self.recv = sems if arrays else (None,) * 3

    def part(self, j, n):
        return self.srcs[j].at[0 if self.arrays[j].shape[0] == 1 else n]

    def copy(self, j, i):
        n, where = self.me.other(i)
        return remote(
            self.part(j, n), self.outs[j].at[self.number], self.send.at[j, i],
            self.recv.at[j, self.number], where,
        )

    def stay(self, j):
        return pltpu.make_async_copy(
            self.part(j, self.number), self.outs[j].at[self.number], self.own.at[j]
        )

    def start(self):
        for j in range(len(self.arrays)):

            def one(i, carried, j=j):
                self.copy(j, i).start()
                return carried

            self.stay(j).start()
            lax.fori_loop(1, self.devices, one, 0)

    def finish(self):
        for j in range(len(self.arrays)):

            def one(i, carried, j=j):
                n, where = self.me.other(i)
                there = self.outs[j].at[n]
                remote(there, there, self.send.at[j, i], self.recv.at[j, n], where).wait_recv()
                self.copy(j, i).wait_send()
                return carried

            self.stay(j).wait()
            lax.fori_loop(1, self.devices, one, 0)

    @staticmethod
    def scratch(arrays, devices):
        if not arrays:
            return []
        sem = pltpu.SemaphoreType.DMA
        return [sem((len(arrays),)), sem((len(arrays), devices)), sem((len(arrays), devices))]

    @staticmethod
    def shapes(arrays, devices):
        return [jax.ShapeDtypeStruct((devices,) + a.shape[1:], a.dtype) for a in arrays]


class Gather:
    def __init__(self, me, by_row, x_ref, out_ref, sems):
        self.me, self.by_row, self.x_ref, self.out_ref = me, by_row, x_ref, out_ref
        self.own_sem, self.recv, self.sends = sems
        self.pending = []
        self.own = self.index(me.z, me.a, me.b)

    @staticmethod
    def scratch(chips, first, second):
        sem = pltpu.SemaphoreType.DMA
        sends = 4 + (2 * chips - 1) * (
            2 + 2 * (first + second - 1) + 2 * (second - 1) * first + 2 * (first - 1) * second
        )
        return [sem((2,)), sem((chips * 2 * first * second, 2)), sem((sends,))]

    def index(self, z, a, b):
        return (z * 2 + self.me.k) * self.me.owners + a * self.me.second + b

    def piece(self, blk, h):
        return self.out_ref.at[h, blk] if self.by_row else self.out_ref.at[blk, h]

    def push(self, src, blk, h, target, when=None):
        copy = remote(
            src, self.piece(blk, h), self.sends.at[len(self.pending)], self.recv.at[blk, h], target
        )
        self.pending.append(when)
        copy.start() if when is None else pl.when(when())(copy.start)

    def landed(self, blk, h, when=None):
        there = self.piece(blk, h)
        copy = remote(there, there, self.sends.at[0], self.recv.at[blk, h], self.me.at())
        copy.wait_recv() if when is None else pl.when(when())(copy.wait_recv)

    def there(self, shift):
        if shift == 0:
            return None
        me = self.me
        return lambda: (me.z + shift >= 0) if shift < 0 else (me.z + shift < me.chips)

    def spread(self, blk, source, when=None):
        me = self.me
        for h in range(2):
            for i in range(1, me.second):
                self.push(source(h), blk, h, me.at(b=(me.b + i) % me.second), when)
            for i in range(1, me.first):
                self.push(source(h), blk, h, me.at(a=(me.a + i) % me.first), when)
        for h in range(2):
            self.push(source(h), blk, h, me.at(k=1 - me.k), when)

    def relay(self, shift):
        me, when = self.me, self.there(shift)
        z = me.z + shift
        for h in range(2):
            if h == 0:
                froms = [(me.a, (me.b + i) % me.second) for i in range(1, me.second)]
                onward = [dict(a=(me.a + i) % me.first) for i in range(1, me.first)]
            else:
                froms = [((me.a + i) % me.first, me.b) for i in range(1, me.first)]
                onward = [dict(b=(me.b + i) % me.second) for i in range(1, me.second)]
            for a, b in froms:
                blk = self.index(z, a, b)
                self.landed(blk, h, when)
                for target in onward:
                    self.push(self.piece(blk, h), blk, h, me.at(**target), when)
                self.push(self.piece(blk, h), blk, h, me.at(k=1 - me.k), when)

    def settle(self, shift):
        me, when = self.me, self.there(shift)
        z = me.z + shift
        for h in range(2):
            for i in range(1, me.second if h else me.first):
                for j in range(me.first if h else me.second):
                    if h == 0:
                        a, b = (me.a + i) % me.first, (me.b + j) % me.second
                    else:
                        a, b = (me.a + j) % me.first, (me.b + i) % me.second
                    blk = self.index(z, a, b)
                    self.landed(blk, h, when)
                    self.push(self.piece(blk, h), blk, h, me.at(k=1 - me.k), when)

    def stay(self, h):
        return pltpu.make_async_copy(
            self.x_ref.at[h], self.piece(self.own, h), self.own_sem.at[h]
        )

    def begin(self):
        me, x_ref, own = self.me, self.x_ref, self.own
        for h in range(2):
            self.stay(h).start()
        for h in range(2):
            self.push(x_ref.at[h], own, h, me.at(z=me.z + 1), self.there(1))
            self.push(x_ref.at[h], own, h, me.at(z=me.z - 1), self.there(-1))
        self.spread(own, lambda h: x_ref.at[h])

    def stage(self, t):
        me = self.me
        for shift in (-t, t):
            there, onward = self.there(shift), self.there(1 if shift < 0 else -1)
            blk = self.index(me.z + shift, me.a, me.b)
            for h in range(2):
                self.landed(blk, h, there)
                self.push(
                    self.piece(blk, h), blk, h, me.at(z=me.z + (1 if shift < 0 else -1)),
                    lambda there=there, onward=onward: there() & onward(),
                )
            self.spread(blk, lambda h, blk=blk: self.piece(blk, h), there)

    def drain(self, t):
        shifts = (-t, t) if t else (0,)
        for shift in shifts:
            self.relay(shift)
        for shift in shifts:
            self.settle(shift)

    def along(self):
        return [functools.partial(self.stage, t) for t in range(1, self.me.chips)]

    def across(self):
        return [functools.partial(self.drain, t) for t in range(self.me.chips)]

    def finish(self):
        me = self.me
        for h in range(2):
            self.stay(h).wait()
        for z in range(me.chips):
            for e in range(me.owners):
                for h in range(2):
                    self.landed((z * 2 + 1 - me.k) * me.owners + e, h)
        for i, when in enumerate(self.pending):
            copy = remote(
                self.x_ref.at[0], self.x_ref.at[0], self.sends.at[i], self.recv.at[0, 0], me.at()
            )
            copy.wait_send() if when is None else pl.when(when())(copy.wait_send)


def taken(refs, number):
    return [refs.pop(0) for _ in range(number)]


def gather_kernel(chips, first, second, orders, jobs, mails, *refs):
    me = Place(chips, first, second)
    refs = list(refs)
    x_refs = taken(refs, len(orders))
    mail_srcs = taken(refs, len(mails))
    srcs = taken(refs, len(jobs))
    out_refs = taken(refs, len(orders))
    mail_outs = taken(refs, len(mails))
    outs = taken(refs, len(jobs))
    gathers = [
        Gather(me, by_row, x_ref, out_ref, taken(refs, 3))
        for by_row, x_ref, out_ref in zip(orders, x_refs, out_refs)
    ]
    if mails:
        spread_send, spread_recv = taken(refs, 2)
        mail = Mail(mails, me, mail_srcs, mail_outs, taken(refs, 3))
    load = Load(jobs, me, srcs, outs, refs)
    me.greet("all" if mails else "dp" if jobs else "near")
    for gather in gathers:
        gather.begin()
    if mails:
        mail.start()
    along = [stage for stages in zip(*[gather.along() for gather in gathers]) for stage in stages]
    for i, stage in enumerate(along):
        if i == len(along) - 1:
            load.start()
        stage()
    rest = [stage for stages in zip(*[gather.across() for gather in gathers]) for stage in stages]
    for stage in rest[:2]:
        stage()
    if mails:
        j = 0
        load.landed(j)
        column = outs[j].at[:, me.ex]
        spreads = [
            remote(
                column, column, spread_send.at[i], spread_recv.at[me.ex],
                (me.dp, (me.ex + i) % me.owners),
            )
            for i in range(1, me.owners)
        ]
        for copy in spreads:
            copy.start()
    for stage in rest[2:]:
        stage()
    if mails:
        mail.finish()
        for i in range(1, me.owners):
            e = (me.ex + i) % me.owners
            there = outs[j].at[:, e]
            remote(there, there, spread_send.at[i], spread_recv.at[e], (me.dp, e)).wait_recv()
        for copy in spreads:
            copy.wait_send()
    for gather in gathers:
        gather.finish()
    load.finish(skip=(0,) if mails else ())


def gather_all(xs, orders, chips, owners, collective_id, jobs=(), mails=()):
    first, second = expert_factors(owners)
    blocks = chips * 2 * owners
    sem = pltpu.SemaphoreType.DMA
    shapes = []
    for x, by_row in zip(xs, orders):
        rest = x.shape[1:]
        shape = (2, blocks) + rest if by_row else (blocks, 2) + rest
        shapes.append(jax.ShapeDtypeStruct(shape, x.dtype))
    shapes += Mail.shapes(mails, blocks) + [job.out_shape for job in jobs]
    ins = list(xs) + list(mails) + [job.src for job in jobs]
    scratch = Gather.scratch(chips, first, second) * len(xs)
    if mails:
        scratch += [sem((owners,)), sem((owners,))] + Mail.scratch(mails, blocks)
    return pl.pallas_call(
        functools.partial(
            gather_kernel, chips, first, second, orders, jobs,
            [jax.ShapeDtypeStruct(a.shape, a.dtype) for a in mails],
        ),
        out_shape=shapes,
        in_specs=[ANY] * len(ins),
        out_specs=[ANY] * len(shapes),
        scratch_shapes=scratch + Load.scratch(jobs, chips * 2),
        compiler_params=pltpu.CompilerParams(collective_id=collective_id, has_side_effects=True),
    )(*ins)


class Scatter:
    def __init__(self, me, by_row, column, width, p_ref, out_ref, refs):
        self.me, self.by_row, self.cut = me, by_row, pl.ds(column, width)
        self.p_ref, self.out_ref = p_ref, out_ref
        self.mine, self.fromk, self.a0, self.b0, self.b1, self.a1, self.fromz = refs[:7]
        self.load_sem, self.ks, self.a0s, self.b0s, self.b1s, self.a1s, self.zs, self.sends = refs[7:]
        self.pending = []

    @staticmethod
    def scratch(chips, first, second, half, width):
        sem, owners = pltpu.SemaphoreType.DMA, first * second
        one = max(first - 1, 1), max(second - 1, 1)
        sends = chips * (owners + 2 + 2 * (first - 1) * second + 2 * (second - 1) * first)
        return [
            pltpu.VMEM((chips, owners, 2, half, width), BF16),
            pltpu.VMEM((chips, owners, 2, half, width), BF16),
            pltpu.VMEM((chips, one[0], second, half, width), BF16),
            pltpu.VMEM((chips, one[1], half, width), BF16),
            pltpu.VMEM((chips, one[1], first, half, width), BF16),
            pltpu.VMEM((chips, one[0], half, width), BF16),
            pltpu.VMEM((chips + 1, 2, half, width), BF16),
            sem((chips, owners)),
            sem((chips, owners)),
            sem((chips, one[0], second)),
            sem((chips, one[1])),
            sem((chips, one[1], first)),
            sem((chips, one[0])),
            sem((chips + 1,)),
            sem((sends + chips * (first + second),)),
        ]

    def push(self, src, dst, sem, target, part, when=None):
        copy = remote(src, dst, self.sends.at[len(self.pending)], sem, target)
        self.pending.append((part, when))
        copy.start() if when is None else pl.when(when())(copy.start)

    def landed(self, dst, sem):
        remote(dst, dst, self.sends.at[0], sem, self.me.at()).wait_recv()

    def line(self, t):
        z, chips = self.me.z, self.me.chips
        return jnp.where(
            z < chips // 2,
            jnp.where(t < chips - 1 - z, chips - 1 - t, t - (chips - 1 - z)),
            jnp.where(t < z, t, chips - 1 - (t - z)),
        )

    def block(self, z, k, e):
        blk = (z * 2 + k) * self.me.owners + e
        if self.by_row:
            return self.p_ref.at[:, blk, :, self.cut]
        return self.p_ref.at[blk, :, :, self.cut]

    def begin(self):
        me = self.me
        for t in range(me.chips):
            z = self.line(t)
            for e in range(me.owners):
                pltpu.make_async_copy(
                    self.block(z, me.k, e), self.mine.at[t, e], self.load_sem.at[t, e]
                ).start()
                self.push(
                    self.block(z, 1 - me.k, e), self.fromk.at[t, e], self.ks.at[t, e],
                    me.at(k=1 - me.k), "block",
                )

    @staticmethod
    def add(*terms):
        value = terms[0].astype(F32)
        for term in terms[1:]:
            value = value + term.astype(F32)
        return value

    def step_one(self, t):
        me, mine = self.me, self.mine
        first, second = me.first, me.second
        for i in range(first):
            for j in range(second):
                a, b = (me.a + 1 + i) % first, (me.b + 1 + j) % second
                e = a * second + b
                pltpu.make_async_copy(mine.at[t, e], mine.at[t, e], self.load_sem.at[t, e]).wait()
                self.landed(self.fromk.at[t, e], self.ks.at[t, e])
                mine[t, e] = self.add(mine[t, e], self.fromk[t, e]).astype(BF16)
                if i < first - 1:
                    slot = first - 2 - i
                    self.push(
                        mine.at[t, e, 0], self.a0.at[t, slot, b], self.a0s.at[t, slot, b],
                        me.at(a=a), "half",
                    )
                if j < second - 1:
                    slot = second - 2 - j
                    self.push(
                        mine.at[t, e, 1], self.b1.at[t, slot, a], self.b1s.at[t, slot, a],
                        me.at(b=b), "half",
                    )

    def step_two(self, t):
        me, mine = self.me, self.mine
        first, second = me.first, me.second
        for j in range(second - 1):
            b = (me.b + 1 + j) % second
            e = me.a * second + b
            for i in range(first - 1):
                self.landed(self.a0.at[t, i, b], self.a0s.at[t, i, b])
            mine[t, e, 0] = self.add(
                mine[t, e, 0], *[self.a0[t, i, b] for i in range(first - 1)]
            ).astype(BF16)
            slot = second - 2 - j
            self.push(
                mine.at[t, e, 0], self.b0.at[t, slot], self.b0s.at[t, slot], me.at(b=b), "half"
            )
        for i in range(first - 1):
            a = (me.a + 1 + i) % first
            e = a * second + me.b
            for j in range(second - 1):
                self.landed(self.b1.at[t, j, a], self.b1s.at[t, j, a])
            mine[t, e, 1] = self.add(
                mine[t, e, 1], *[self.b1[t, j, a] for j in range(second - 1)]
            ).astype(BF16)
            slot = first - 2 - i
            self.push(
                mine.at[t, e, 1], self.a1.at[t, slot], self.a1s.at[t, slot], me.at(a=a), "half"
            )

    def step_three(self, t):
        me, mine, total, fromz, zs = self.me, self.mine, self.out_ref, self.fromz, self.zs
        first, second, chips = me.first, me.second, me.chips
        z, e = self.line(t), me.ex
        for i in range(first - 1):
            self.landed(self.a0.at[t, i, me.b], self.a0s.at[t, i, me.b])
            self.landed(self.a1.at[t, i], self.a1s.at[t, i])
        for j in range(second - 1):
            self.landed(self.b1.at[t, j, me.a], self.b1s.at[t, j, me.a])
            self.landed(self.b0.at[t, j], self.b0s.at[t, j])
        total[0] = self.add(
            mine[t, e, 0], *[self.a0[t, i, me.b] for i in range(first - 1)],
            *[self.b0[t, j] for j in range(second - 1)],
        )
        total[1] = self.add(
            mine[t, e, 1], *[self.b1[t, j, me.a] for j in range(second - 1)],
            *[self.a1[t, i] for i in range(first - 1)],
        )

        def also(when, slot):
            @pl.when(when)
            def _():
                self.landed(fromz.at[slot], zs.at[slot])
                total[...] = total[...] + fromz[slot].astype(F32)

        if t < chips - 1:
            up = z > me.z
            also(jnp.where(up, me.z > 0, me.z < chips - 1), z)
            mine[t, e] = total[...].astype(BF16)
            self.push(
                mine.at[t, e], fromz.at[z], zs.at[z], me.at(z=me.z + 1), "block",
                lambda: self.line(t) > me.z,
            )
            slot = jnp.where(z == me.z - 1, chips, z)
            self.push(
                mine.at[t, e], fromz.at[slot], zs.at[slot], me.at(z=me.z - 1), "block",
                lambda: self.line(t) < me.z,
            )
        else:
            also(me.z > 0, me.z)
            also(me.z < chips - 1, chips)

    def stage(self, t):
        if t < self.me.chips:
            self.step_one(t)
        if 0 <= t - 1 < self.me.chips:
            self.step_two(t - 1)
        if 0 <= t - 2 < self.me.chips:
            self.step_three(t - 2)

    def stages(self):
        return [functools.partial(self.stage, t) for t in range(self.me.chips + 2)]

    def finish(self):
        for i, (part, when) in enumerate(self.pending):
            ref = self.mine.at[0, 0] if part == "block" else self.mine.at[0, 0, 0]
            copy = remote(ref, ref, self.sends.at[i], self.zs.at[0], self.me.at())
            copy.wait_send() if when is None else pl.when(when())(copy.wait_send)


def scatter_parts(chips, owners, half, full):
    parts = 1
    while chips * owners * half * (full // parts) * 8 > 20 * 2**20:
        parts *= 2
    return parts


def scatter_kernel(chips, first, second, by_row, column, width, jobs, mails, *refs):
    me = Place(chips, first, second)
    refs = list(refs)
    (p_ref,) = taken(refs, 1)
    srcs, mail_srcs = taken(refs, len(jobs)), taken(refs, len(mails))
    (out_ref,) = taken(refs, 1)
    outs, mail_outs = taken(refs, len(jobs)), taken(refs, len(mails))
    scatter = Scatter(me, by_row, column, width, p_ref, out_ref, taken(refs, 15))
    mail = Mail(mails, me, mail_srcs, mail_outs, taken(refs, 3) if mails else ())
    load = Load(jobs, me, srcs, outs, refs)
    me.greet("all" if mails else "dp" if jobs else "near")
    scatter.begin()
    mail.start()
    load.start()
    for stage in scatter.stages():
        stage()
    mail.finish()
    load.finish()
    scatter.finish()


def scatter_sum(p, chips, owners, by_row, collective_id, jobs=(), mails=()):
    first, second = expert_factors(owners)
    half, full = p.shape[2:]
    parts = scatter_parts(chips, owners, half, full)
    width = full // parts

    def call(part, jobs, mails):
        return pl.pallas_call(
            functools.partial(
                scatter_kernel, chips, first, second, by_row, part * width, width, jobs,
                [jax.ShapeDtypeStruct(a.shape, a.dtype) for a in mails],
            ),
            out_shape=[jax.ShapeDtypeStruct((2, half, width), F32)]
            + [job.out_shape for job in jobs]
            + Mail.shapes(mails, chips * 2 * owners),
            in_specs=[ANY] * (1 + len(jobs) + len(mails)),
            out_specs=[pl.BlockSpec(memory_space=pltpu.VMEM)] + [ANY] * (len(jobs) + len(mails)),
            scratch_shapes=Scatter.scratch(chips, first, second, half, width)
            + Mail.scratch(mails, chips * 2 * owners)
            + Load.scratch(jobs, chips * 2),
            compiler_params=pltpu.CompilerParams(
                collective_id=collective_id + part, has_side_effects=True,
                vmem_limit_bytes=60 * 2**20,
            ),
        )(p, *[job.src for job in jobs], *mails)

    calls = [
        call(part, () if part else jobs, () if part else mails) for part in range(parts)
    ]
    whole = calls[0][0] if parts == 1 else jnp.concatenate([c[0] for c in calls], axis=-1)
    return [whole] + list(calls[0][1:])


class Riders:
    def __init__(self, chips, owners, jobs=(), gather=None, scatter=None):
        self.chips, self.owners, self.jobs = chips, owners, jobs
        self.factors = expert_factors(owners)
        self.orders = [order for pair in (gather, scatter) if pair for order in pair[1:]]
        self.has = gather is not None, scatter is not None
        self.ins = [pair[0] for pair in (gather, scatter) if pair] + [job.src for job in jobs]
        self.out_shapes, self.out_specs, self.scratch = [], [], []
        blocks = chips * 2 * owners
        if gather:
            x, by_row = gather
            rest = x.shape[1:]
            shape = (2, blocks) + rest if by_row else (blocks, 2) + rest
            self.out_shapes.append(jax.ShapeDtypeStruct(shape, x.dtype))
            self.out_specs.append(ANY)
            self.scratch += Gather.scratch(chips, *self.factors)
        if scatter:
            half, full = scatter[0].shape[2:]
            shape = jax.ShapeDtypeStruct((2, half, full), F32)
            self.out_shapes.append(shape)
            self.out_specs.append(pl.BlockSpec(shape.shape, lambda i: (0, 0, 0)))
            self.scratch += Scatter.scratch(chips, *self.factors, half, full)
            self.full = full
        self.out_shapes += [job.out_shape for job in jobs]
        self.out_specs += [ANY] * len(jobs)
        self.scratch += Load.scratch(jobs, chips * 2)
        self.ins_specs = [ANY] * len(self.ins)
        self.count = len(self.ins)

    def params(self, collective_id):
        if not self.count:
            return dict(vmem_limit_bytes=60 * 2**20)
        return dict(
            vmem_limit_bytes=60 * 2**20, collective_id=collective_id, has_side_effects=True
        )

    def board(self, refs, ins, outs, scratch=0):
        refs = list(refs)
        own = taken(refs, ins)
        given = taken(refs, self.count)
        own += taken(refs, outs)
        results = taken(refs, self.count)
        own += taken(refs, scratch)
        if not self.count:
            return own
        self.me = me = Place(self.chips, *self.factors)
        orders, staged, self.stages = list(self.orders), [], []
        if self.has[0]:
            rider = Gather(me, orders.pop(0), given.pop(0), results.pop(0), taken(refs, 3))
            staged.append(rider)
        if self.has[1]:
            rider = Scatter(
                me, orders.pop(0), 0, self.full, given.pop(0), results.pop(0), taken(refs, 15)
            )
            staged.append(rider)
        load = Load(self.jobs, me, given, results, refs)
        step, steps = pl.program_id(0), pl.num_programs(0)

        @pl.when(step == 0)
        def _():
            me.greet("column" if not staged else "dp" if self.jobs else "near")
            for rider in staged:
                rider.begin()
            if not self.has[0]:
                load.start()

        plan = []
        for rider in staged:
            if isinstance(rider, Gather):
                along, across = rider.along(), rider.across()
                along.insert(len(along) - 1, load.start)
                plan += [(1 + i // 2, stage) for i, stage in enumerate(along)]
                begin = 2 + len(along) // 2
                plan += [
                    (begin + i * (self.steps - 1 - begin) // len(across), stage)
                    for i, stage in enumerate(across)
                ]
            else:
                stages = rider.stages()
                plan += [
                    (1 + i * (self.steps - 2) // (len(stages) - 1), stage)
                    for i, stage in enumerate(stages)
                ]
        for at, stage in plan:
            pl.when(step == at)(stage)

        def finish():
            @pl.when(step == steps - 1)
            def _():
                for rider in staged:
                    rider.finish()
                load.finish()

        self.alight = finish
        return own

    def alight(self):
        pass


def exchange_kernel(chips, first, second, array, x_ref, out_ref, *sems):
    me = Place(chips, first, second)
    mail = Mail([array], me, [x_ref], [out_ref], sems)
    me.greet("all")
    mail.start()
    mail.finish()


def exchange(x, chips, owners, collective_id):
    first, second = expert_factors(owners)
    devices = chips * 2 * owners
    shape = jax.ShapeDtypeStruct(x.shape, x.dtype)
    return pl.pallas_call(
        functools.partial(exchange_kernel, chips, first, second, shape),
        out_shape=shape,
        in_specs=[ANY],
        out_specs=ANY,
        scratch_shapes=Mail.scratch([shape], devices),
        compiler_params=pltpu.CompilerParams(collective_id=collective_id, has_side_effects=True),
    )(x)


D = 2048
KVH = 16
HD = 128
FF = 5632
NEXP = 8
TOK_MB = 64
CAP = 24
LANES = 128
EPSILON = 1e-06


def dot(a, b):
    return jnp.dot(a, b, preferred_element_type=F32)


def dot_nt(a, b):
    return lax.dot_general(a, b, (((1,), (1,)), ((), ())), preferred_element_type=F32)


def dot_tn(a, b):
    return lax.dot_general(a, b, (((0,), (0,)), ((), ())), preferred_element_type=F32)


def counted(shape, axis):
    return lax.broadcasted_iota(jnp.int32, shape, axis).astype(F32)


def two_parts(value):
    upper = value.astype(BF16)
    return upper, (value - upper.astype(F32)).astype(BF16)


class Seats:
    def __init__(self, meta, first_expert, count, tri, eye):
        slots = meta.shape[1]
        per = slots // TOK_MB * CAP
        self.count, self.per, self.slots, self.first = count, per, slots, first_expert
        line = counted(meta.shape, 0)
        expert = first_expert + line
        hit = (meta[0:1] == expert) | (meta[1:2] == expert)
        hit = hit & (line < count)
        rank = dot(jnp.where(hit, 1.0, 0.0).astype(BF16), tri)
        block = lax.broadcasted_iota(jnp.int32, meta.shape, 1) // TOK_MB
        seat = jnp.where(hit, block.astype(F32) * CAP + rank + line * per, -1.0)
        self.routes = dot_nt(eye, meta.astype(BF16))
        column = dot_nt(eye, seat.astype(BF16))
        total = count * per
        row = counted((total, slots), 0)
        lane = counted((slots, total), 1)
        here, there = row == seat[0:1], lane == column[:, 0:1]
        for l in range(1, count):
            here = here | (row == seat[l : l + 1])
            there = there | (lane == column[:, l : l + 1])
        self.take = jnp.where(here, 1.0, 0.0).astype(BF16)
        self.put = jnp.where(there, 1.0, 0.0).astype(BF16)

    def gates(self, logits):
        lane = counted(logits.shape, 1)
        one = jnp.sum(jnp.where(lane == self.routes[:, 0:1], logits, 0.0), axis=1, keepdims=True)
        two = jnp.sum(jnp.where(lane == self.routes[:, 1:2], logits, 0.0), axis=1, keepdims=True)
        highest = jnp.maximum(one, two)
        one, two = jnp.exp(one - highest), jnp.exp(two - highest)
        total = one + two
        return one / total, two / total

    def seat_values(self, pairs, plain):
        lane = counted((self.slots, LANES), 1)
        per_expert = []
        for l in range(self.count):
            expert = self.first + l
            values = [
                jnp.where(self.routes[:, 0:1] == expert, a, 0.0)
                + jnp.where(self.routes[:, 1:2] == expert, b, 0.0)
                for a, b in pairs
            ] + list(plain)
            packed = jnp.zeros((self.slots, LANES), F32)
            for i, value in enumerate(values):
                upper, lower = two_parts(value)
                packed = jnp.where(lane == 2 * i, upper.astype(F32), packed)
                packed = jnp.where(lane == 2 * i + 1, lower.astype(F32), packed)
            part = dot(self.take[l * self.per : (l + 1) * self.per], packed.astype(BF16))
            per_expert.append(
                [part[:, 2 * i : 2 * i + 1] + part[:, 2 * i + 1 : 2 * i + 2] for i in range(len(values))]
            )
        return [
            jnp.concatenate(parts, axis=0) if self.count > 1 else parts[0]
            for parts in zip(*per_expert)
        ]

    def slot_values(self, value):
        total = self.count * self.per
        lane = counted((total, LANES), 1)
        row = counted((total, LANES), 0)
        upper, lower = two_parts(value)
        packed = jnp.zeros((total, LANES), F32)
        for l in range(self.count):
            mine = (row >= l * self.per) & (row < (l + 1) * self.per)
            packed = jnp.where(mine & (lane == 2 * l), upper.astype(F32), packed)
            packed = jnp.where(mine & (lane == 2 * l + 1), lower.astype(F32), packed)
        back = dot(self.put, packed.astype(BF16))
        out = jnp.zeros((self.slots, 8), F32)
        lane = counted((self.slots, 8), 1)
        for l in range(self.count):
            value = back[:, 2 * l : 2 * l + 1] + back[:, 2 * l + 1 : 2 * l + 2]
            for k in range(2):
                chosen = (self.routes[:, k : k + 1] == self.first + l) & (lane == k)
                out = jnp.where(chosen, value, out)
        return out


def first_expert(count):
    return (lax.axis_index("expert") * count).astype(F32)


def turned(values, cosine, sine):
    heads = []
    for h in range(values.shape[1] // HD):
        head = values[:, h * HD : (h + 1) * HD]
        heads.append(head * cosine + pltpu.roll(head, HD // 2, 1) * sine)
    return heads[0] if len(heads) == 1 else jnp.concatenate(heads, axis=1)


def mixer_forward_kernel(count, riders, *refs):
    (
        length_ref, x_ref, meta_ref, gain_ref, router_ref, wq_ref, wkv_ref, wo_ref,
        tri_ref, eye_ref, upper_ref, lower_ref,
        normed_ref, part_ref, rows_ref, key_ref, value_ref, query_ref, mix_ref, gated_ref, info_ref, gates_ref,
    ) = riders.board(refs, 12, 10)
    hc = key_ref.shape[2]
    x = x_ref[0].astype(F32)
    inverse = lax.rsqrt(jnp.mean(x * x, axis=1, keepdims=True) + EPSILON)
    normed = (x * inverse * gain_ref[...]).astype(BF16)
    normed_ref[0] = normed
    seats = Seats(meta_ref[0], first_expert(count), count, tri_ref[...], eye_ref[...])
    one, two = seats.gates(dot(normed, router_ref[...]))
    lane = counted((seats.slots, 8), 1)
    gates_ref[0] = jnp.where(lane == 0, one, jnp.where(lane == 1, two, 0.0))
    gate, place = seats.seat_values([(one, two)], [counted((seats.slots, 1), 0)])
    lane = counted((gate.shape[0], 8), 1)
    info_ref[0] = jnp.where(lane == 0, gate, jnp.where(lane == 1, place, 0.0))

    key_value = dot(normed, wkv_ref[...])
    upper, lower = upper_ref[...], lower_ref[...]
    table = upper.astype(F32) + lower.astype(F32)
    key = turned(key_value[:, :hc], table[:, :HD], table[:, HD:]).astype(BF16)
    value = key_value[:, hc:].astype(BF16)
    key_ref[0], value_ref[0] = key, value

    rows = dot(seats.take, normed).astype(BF16)
    per = seats.per
    for l in range(count):
        rows_ref[l] = rows[l * per : (l + 1) * per]
    table = dot(seats.take, upper) + dot(seats.take, lower)
    query = [dot(rows[l * per : (l + 1) * per], wq_ref[l]) for l in range(count)]
    query = query[0] if count == 1 else jnp.concatenate(query, axis=0)
    query = (turned(query, table[:, :HD], table[:, HD:]) * HD ** (-0.5)).astype(BF16)
    query_ref[0] = query

    at = counted((seats.take.shape), 1)
    length = length_ref[pl.program_id(0)].astype(F32)
    allowed = (at <= place) & (at < length)
    mix = []
    for h in range(hc // HD):
        cut = slice(h * HD, (h + 1) * HD)
        scores = jnp.where(allowed, dot_nt(query[:, cut], key[:, cut]), -1e30)
        exponent = jnp.exp(scores - jnp.max(scores, axis=1, keepdims=True))
        probs = (exponent / jnp.sum(exponent, axis=1, keepdims=True)).astype(BF16)
        mix.append(dot(probs, value[:, cut]))
    mix = mix[0] if len(mix) == 1 else jnp.concatenate(mix, axis=1)
    mix_ref[0] = mix
    gated = (mix * gate).astype(BF16)
    for l in range(count):
        gated_ref[l] = gated[l * per : (l + 1) * per]
    out = [dot(gated[l * per : (l + 1) * per], wo_ref[l]).astype(BF16) for l in range(count)]
    out = out[0] if count == 1 else jnp.concatenate(out, axis=0)
    part_ref[0] = dot(seats.put, out).astype(BF16)
    riders.alight()


def mixer_backward_kernel(count, riders, *refs):
    (
        length_ref, grad_ref, meta_ref, wq_ref, wkv_ref, wo_ref, tri_ref, eye_ref,
        upper_ref, lower_ref, key_ref, value_ref, query_ref, mix_ref, info_ref,
        part_ref, rows_ref, terms_ref, grad_query_ref, grad_key_value_ref,
    ) = riders.board(refs, 15, 5)
    hc = key_ref.shape[2]
    seats = Seats(meta_ref[0], first_expert(count), count, tri_ref[...], eye_ref[...])
    per = seats.per
    rows = dot(seats.take, grad_ref[0]).astype(BF16)
    for l in range(count):
        rows_ref[l] = rows[l * per : (l + 1) * per]
    grad_mix = [dot_nt(rows[l * per : (l + 1) * per], wo_ref[l]) for l in range(count)]
    grad_mix = grad_mix[0] if count == 1 else jnp.concatenate(grad_mix, axis=0)
    gate, place = info_ref[0, :, 0:1], info_ref[0, :, 1:2]
    terms_ref[0] = seats.slot_values(jnp.sum(grad_mix * mix_ref[0], axis=1, keepdims=True))
    grad_mix = (grad_mix * gate).astype(BF16)

    at = counted(seats.take.shape, 1)
    length = length_ref[pl.program_id(0)].astype(F32)
    allowed = (at <= place) & (at < length)
    key, value, query = key_ref[0], value_ref[0], query_ref[0]
    grad_query, grad_key, grad_value = [], [], []
    for h in range(hc // HD):
        cut = slice(h * HD, (h + 1) * HD)
        scores = jnp.where(allowed, dot_nt(query[:, cut], key[:, cut]), -1e30)
        exponent = jnp.exp(scores - jnp.max(scores, axis=1, keepdims=True))
        probs = exponent / jnp.sum(exponent, axis=1, keepdims=True)
        grad_probs = dot_nt(grad_mix[:, cut], value[:, cut])
        grad_value.append(dot_tn(probs.astype(BF16), grad_mix[:, cut]))
        row_dot = jnp.sum(probs * grad_probs, axis=1, keepdims=True)
        grad_scores = (probs * (grad_probs - row_dot)).astype(BF16)
        grad_query.append(dot(grad_scores, key[:, cut]))
        grad_key.append(dot_tn(grad_scores, query[:, cut]))

    def joined(parts):
        return parts[0] if len(parts) == 1 else jnp.concatenate(parts, axis=1)

    upper, lower = upper_ref[...], lower_ref[...]
    table = dot(seats.take, upper) + dot(seats.take, lower)
    grad_query = turned(joined(grad_query), table[:, :HD], -table[:, HD:]) * HD ** (-0.5)
    grad_query = grad_query.astype(BF16)
    for l in range(count):
        grad_query_ref[l] = grad_query[l * per : (l + 1) * per]
    table = upper.astype(F32) + lower.astype(F32)
    grad_key = turned(joined(grad_key), table[:, :HD], -table[:, HD:])
    grad_key_value = jnp.concatenate([grad_key, joined(grad_value)], axis=1).astype(BF16)
    grad_key_value_ref[0] = grad_key_value
    back = [
        dot_nt(grad_query[l * per : (l + 1) * per], wq_ref[l]).astype(BF16) for l in range(count)
    ]
    back = back[0] if count == 1 else jnp.concatenate(back, axis=0)
    part_ref[0] = (dot(seats.put, back) + dot_nt(grad_key_value, wkv_ref[...])).astype(BF16)
    riders.alight()


def feed_kernel(count, l, last, groups, turns, riders, *refs):
    prior = 2 * l if last else 0
    refs = riders.board(refs, 10 + prior, 9 if last else 9, 4 if last else 2)
    (
        offset_ref, x_ref, cot_ref, meta_ref, router_ref, wg_ref, wu_ref, wd_ref, tri_ref, eye_ref,
    ) = refs[:10]
    before, refs = refs[10 : 10 + prior], refs[10 + prior :]
    part_ref, back_ref, rows_ref, cot_rows_ref, active_ref, grad_gate_ref, grad_up_ref, terms_ref, gates_ref = refs[:9]
    gate_ref, term_ref = refs[9:11]
    kept = []
    for g in range(groups):
        seats = Seats(meta_ref[g], first_expert(count), count, tri_ref[...], eye_ref[...])
        kept.append(seats)
        per = seats.per
        mine = slice(l * per, (l + 1) * per)
        one, two = seats.gates(dot(x_ref[g], router_ref[...]))
        lane = counted((seats.slots, 8), 1)
        gates_ref[g] = jnp.where(lane == 0, one, jnp.where(lane == 1, two, 0.0))
        (gate,) = seats.seat_values([(one, two)], [])
        take = seats.take[mine]
        valid = meta_ref[g][2:3] > 0.0
        here = slice(g * per, (g + 1) * per)
        rows_ref[here] = dot(take, x_ref[g]).astype(BF16)
        cot_rows_ref[here] = dot(jnp.where(valid, take, 0.0).astype(BF16), cot_ref[g]).astype(BF16)
        gate_ref[here] = jnp.broadcast_to(gate[mine], (per, LANES))
    wide = wd_ref.shape[0]
    rows, cot_rows, gate = rows_ref[...], cot_rows_ref[...], gate_ref[...][:, 0:1]
    gate_part = dot(rows, wg_ref[...])
    up_part = dot(rows, wu_ref[...])
    grad_plain = dot_nt(cot_rows, wd_ref[...])
    sigmoid = 1.0 / (1.0 + jnp.exp(-gate_part))
    silu = gate_part * sigmoid
    active = silu * up_part
    gated = active * gate
    front = gated
    for off in turns:
        front = jnp.where(offset_ref[0] == off, pltpu.roll(gated, wide - off, 1), front)
    active_ref[...] = front.astype(BF16)
    gated = gated.astype(BF16)
    term = jnp.sum(active * grad_plain, axis=1, keepdims=True)
    term_ref[...] = jnp.broadcast_to(term, term_ref.shape)
    grad_active = grad_plain * gate
    grad_up = (grad_active * silu).astype(BF16)
    grad_gate = (
        grad_active * up_part * sigmoid * (1.0 + gate_part * (1.0 - sigmoid))
    ).astype(BF16)
    grad_gate_ref[...], grad_up_ref[...] = grad_gate, grad_up
    out = dot(gated, wd_ref[...]).astype(BF16)
    back = (dot_nt(grad_gate, wg_ref[...]) + dot_nt(grad_up, wu_ref[...])).astype(BF16)
    if last:
        out_ref, dx_ref = refs[11:]
        for g in range(groups):
            here = slice(g * per, (g + 1) * per)
            for e in range(l):
                out_ref[g, e * per : (e + 1) * per] = before[2 * e][here]
                dx_ref[g, e * per : (e + 1) * per] = before[2 * e + 1][here]
            out_ref[g, mine] = out[here]
            dx_ref[g, mine] = back[here]
        for g in range(groups):
            part_ref[g] = dot(kept[g].put, out_ref[g]).astype(BF16)
            back_ref[g] = dot(kept[g].put, dx_ref[g]).astype(BF16)
    else:
        part_ref[...], back_ref[...] = out, back
    for g in range(groups):
        value = term_ref[g * per : (g + 1) * per][:, 0:1]
        parts = [value if e == l else jnp.zeros_like(value) for e in range(count)]
        value = parts[0] if count == 1 else jnp.concatenate(parts, axis=0)
        terms_ref[g] = kept[g].slot_values(value)
    riders.alight()


def whole_block(array):
    return pl.BlockSpec(array.shape, lambda i: (0,) * array.ndim)


def step_block(shape, first=1):
    return pl.BlockSpec((first,) + tuple(shape[1:]), lambda i: (i,) + (0,) * (len(shape) - 1))


SMEM = pl.BlockSpec(memory_space=pltpu.SMEM)


def constants(slots):
    at = jnp.arange(slots)
    earlier = (at[:, None] < at[None, :]) & (at[:, None] // TOK_MB == at[None, :] // TOK_MB)
    return earlier.astype(BF16), (at[:, None] == at[None, :]).astype(BF16)


def mixer_tables(slots):
    frequency = 10000.0 ** (-(jnp.arange(HD // 2, dtype=F32) * (2.0 / HD)))
    angles = jnp.arange(slots, dtype=F32)[:, None] * frequency
    cosine, sine = jnp.cos(angles), jnp.sin(angles)
    table = jnp.concatenate([cosine, cosine, -sine, sine], axis=1)
    upper = lax.reduce_precision(table, 8, 7)
    return upper.astype(BF16), (table - upper).astype(BF16)


def mixer_forward(x, meta, lengths, gain, router, wq, wkv, wo, fixed, riders, collective_id):
    seqs, slots, _ = x.shape
    riders.steps = seqs
    count, _, hc = wq.shape
    seats = slots // TOK_MB * CAP * count
    per = seats // count

    def by_expert(width):
        shape = (count, seqs * per, width)
        return shape, BF16, pl.BlockSpec((count, per, width), lambda i: (0, i, 0))

    def by_row(rows, width, dtype=BF16):
        shape = (seqs, rows, width)
        return shape, dtype, step_block(shape)

    outs = [
        by_row(slots, D), by_row(slots, D), by_expert(D), by_row(slots, hc), by_row(slots, hc),
        by_row(seats, hc), by_row(seats, hc, F32), by_expert(hc), by_row(seats, 8, F32), by_row(slots, 8, F32),
    ]
    fixed_in = [gain, router, wq, wkv, wo, *fixed]
    return pl.pallas_call(
        functools.partial(mixer_forward_kernel, count, riders),
        grid=(seqs,),
        out_shape=[jax.ShapeDtypeStruct(shape, dtype) for shape, dtype, _ in outs]
        + riders.out_shapes,
        in_specs=[SMEM, step_block(x.shape), step_block(meta.shape)]
        + [whole_block(a) for a in fixed_in]
        + riders.ins_specs,
        out_specs=[spec for _, _, spec in outs] + riders.out_specs,
        scratch_shapes=riders.scratch,
        compiler_params=pltpu.CompilerParams(**riders.params(collective_id)),
    )(lengths, x, meta, *fixed_in, *riders.ins)


def mixer_backward(
    grad, meta, lengths, wq, wkv, wo, fixed, saved, riders, collective_id
):
    seqs, slots, _ = grad.shape
    riders.steps = seqs
    count, _, hc = wq.shape
    seats = slots // TOK_MB * CAP * count
    per = seats // count

    def by_expert(width):
        shape = (count, seqs * per, width)
        return shape, BF16, pl.BlockSpec((count, per, width), lambda i: (0, i, 0))

    def by_row(rows, width, dtype=BF16):
        shape = (seqs, rows, width)
        return shape, dtype, step_block(shape)

    outs = [
        by_row(slots, D), by_expert(D), by_row(slots, 8, F32), by_expert(hc), by_row(slots, 2 * hc)
    ]
    fixed_in = [wq, wkv, wo, *fixed]
    return pl.pallas_call(
        functools.partial(mixer_backward_kernel, count, riders),
        grid=(seqs,),
        out_shape=[jax.ShapeDtypeStruct(shape, dtype) for shape, dtype, _ in outs]
        + riders.out_shapes,
        in_specs=[SMEM, step_block(grad.shape), step_block(meta.shape)]
        + [whole_block(a) for a in fixed_in]
        + [step_block(a.shape) for a in saved]
        + riders.ins_specs,
        out_specs=[spec for _, _, spec in outs] + riders.out_specs,
        scratch_shapes=riders.scratch,
        compiler_params=pltpu.CompilerParams(**riders.params(collective_id)),
    )(lengths, grad, meta, *fixed_in, *saved, *riders.ins)


def feed(x, cot, meta, router, wg, wu, wd, fixed, offset, offsets, l, count, before, riders, collective_id):
    groups, slots, _ = x.shape
    wide, _ = wd.shape
    per = slots // TOK_MB * CAP
    last = l == count - 1
    at_once = 2 if last else 4
    riders.steps = groups // at_once
    seats = groups * per

    def of_rows(width):
        return ((seats, width), BF16), pl.BlockSpec((at_once * per, width), lambda i: (i, 0))

    def of_slots(width, dtype):
        return ((groups, slots, width), dtype), step_block((groups, slots, width), at_once)

    outs = [of_slots(D, BF16) if last else of_rows(D)] * 2
    outs += [of_rows(width) for width in (D, D, wide, wide, wide)] + [of_slots(8, F32)] * 2
    fixed_in = [router, wg, wu, wd, *fixed]
    turns = sorted({o for o in offsets if o})
    scratch = [pltpu.VMEM((at_once * per, LANES), F32)] * 2
    if last:
        scratch += [pltpu.VMEM((at_once, count * per, D), BF16)] * 2
    return pl.pallas_call(
        functools.partial(feed_kernel, count, l, last, at_once, turns, riders),
        grid=(groups // at_once,),
        out_shape=[jax.ShapeDtypeStruct(*shape) for shape, _ in outs] + riders.out_shapes,
        in_specs=[SMEM]
        + [step_block(a.shape, at_once) for a in (x, cot, meta)]
        + [
            pl.BlockSpec(a.shape, lambda i, n=a.ndim: (0,) * n, pipeline_mode=pl.Buffered(1))
            for a in fixed_in
        ]
        + [of_rows(D)[1]] * len(before)
        + riders.ins_specs,
        out_specs=[spec for _, spec in outs] + riders.out_specs,
        scratch_shapes=scratch + riders.scratch,
        compiler_params=pltpu.CompilerParams(**riders.params(collective_id)),
    )(offset.reshape(1), x, cot, meta, *fixed_in, *before, *riders.ins)


def rejoin_kernel(owners, *refs):
    *parts, key_value, query_out, key_value_out = refs
    for l, part in enumerate(parts):
        n_dp, _, hc = part.shape
        for d in range(n_dp):
            query_out[l, :, d * hc : (d + 1) * hc] = part[d].astype(F32)
    for d in range(n_dp):
        total = key_value[d * owners].astype(F32)
        for e in range(1, owners):
            total = total + key_value[d * owners + e].astype(F32)
        for half in range(2):
            at = (half * n_dp + d) * hc
            key_value_out[:, at : at + hc] = total[:, half * hc : (half + 1) * hc]


def rejoin(parts, key_value, owners):
    n_dp, depth, hc = parts[0].shape
    rows = key_value.shape[1]
    return pl.pallas_call(
        functools.partial(rejoin_kernel, owners),
        out_shape=[
            jax.ShapeDtypeStruct((len(parts), depth, n_dp * hc), F32),
            jax.ShapeDtypeStruct((rows, 2 * n_dp * hc), F32),
        ],
        compiler_params=pltpu.CompilerParams(vmem_limit_bytes=48 * 2**20),
    )(*parts, key_value)


def norm_forward(values, norm_gain):
    inverse = lax.rsqrt(jnp.mean(values * values, axis=-1, keepdims=True) + EPSILON)
    return (values * inverse * norm_gain, inverse)


def norm_backward(values, inverse, norm_gain, grad_normed):
    scaled = grad_normed * norm_gain
    grad_gain = jnp.sum(grad_normed * values * inverse, axis=(0, 1))
    grad_values = inverse * scaled - values * inverse**3 * jnp.mean(
        scaled * values, axis=-1, keepdims=True
    )
    return (grad_values, grad_gain)


def gate_grads(gate_probs, grad_gate_probs, routes):
    weighted = jnp.sum(gate_probs * grad_gate_probs, axis=-1, keepdims=True)
    grad_picked = gate_probs * (grad_gate_probs - weighted)
    choose = (routes[..., None] == jnp.arange(NEXP, dtype=jnp.int32)).astype(F32)
    return jnp.sum(grad_picked[..., None] * choose, axis=-2)


def tile_starts(shards):
    share = FF // shards
    most = max(share * d % LANES for d in range(shards))
    tiles = -(-(share + most) // LANES)
    starts = [min(share * d // LANES, FF // LANES - tiles) for d in range(shards)]
    return tiles, starts, [share * d - LANES * starts[d] for d in range(shards)]


def put_together_kernel(count, starts, tiles, *refs):
    out_ref = refs[-1]
    edges = sorted(set(starts) | {s + tiles for s in starts})
    for l in range(count):
        for g in range(2):
            part = refs[l * 2 + g]
            for low, high in zip(edges[:-1], edges[1:]):
                cover = [d for d in range(len(starts)) if starts[d] <= low and high <= starts[d] + tiles]
                value = None
                for d in cover:
                    cut = slice((low - starts[d]) * LANES, (high - starts[d]) * LANES)
                    term = part[d, :, cut].astype(F32)
                    value = term if value is None else value + term
                out_ref[l, :, g * FF + low * LANES : g * FF + high * LANES] = value


def put_together(parts, count, starts, tiles):
    n_dp, depth, wide = parts[0].shape
    rows = 32
    return pl.pallas_call(
        functools.partial(put_together_kernel, count, starts, tiles),
        grid=(depth // rows,),
        out_shape=jax.ShapeDtypeStruct((count, depth, 2 * FF), F32),
        in_specs=[pl.BlockSpec((n_dp, rows, wide), lambda i: (0, i, 0))] * len(parts),
        out_specs=pl.BlockSpec((count, rows, 2 * FF), lambda i: (0, i, 0)),
        compiler_params=pltpu.CompilerParams(vmem_limit_bytes=48 * 2**20),
    )(*parts)


def product(pattern, operand, factor):
    return jnp.einsum(pattern, operand, factor, preferred_element_type=F32)


def shards(
    tokens, lengths, attention_routes, feedforward_routes, norm_gains, router_weight,
    key_value_weight, query_weight, output_weight, input_weight, down_weight, cotangent,
):
    n_dp = lax.axis_size("dp")
    owners = lax.axis_size("expert")
    chips = n_dp // 2
    devices = n_dp * owners
    dp = lax.axis_index("dp")
    ex = lax.axis_index("expert")
    me = dp * owners + ex
    mb = tokens.shape[0]
    count = NEXP // owners
    seqs = mb * n_dp
    slots = owners * TOK_MB
    hc = KVH // n_dp * HD
    att = KVH * HD
    depth = D // n_dp
    slice_rows = D // devices
    tiles, starts, offsets = tile_starts(n_dp)
    share, wide = FF // n_dp, tiles * LANES
    offset = jnp.array(offsets, jnp.int32)[dp]

    def query_job(l):
        return Job(
            query_weight,
            jax.ShapeDtypeStruct((D, hc), BF16),
            lambda src, d: src.at[l, :, pl.ds(pl.multiple_of(d * hc, LANES), hc)],
            lambda out, d: out.at[pl.ds(pl.multiple_of(d * depth, depth), depth)],
        )

    key_value_job = Job(
        jnp.swapaxes(key_value_weight.reshape(slice_rows, 2, att), 0, 1),
        jax.ShapeDtypeStruct((n_dp, owners, 2, slice_rows, hc), BF16),
        lambda src, d: src.at[:, :, pl.ds(pl.multiple_of(d * hc, LANES), hc)],
        lambda out, d: out.at[d, lax.axis_index("expert")],
    )

    def start_of(d):
        start = (share * d) // LANES
        if max(share * i // LANES - starts[i] for i in range(n_dp)):
            start = jnp.minimum(start, FF // LANES - tiles)
        return start

    def input_job(l, g):
        return Job(
            input_weight,
            jax.ShapeDtypeStruct((D, wide), BF16),
            lambda src, d: src.at[
                l, :, pl.ds(pl.multiple_of(g * FF + start_of(d) * LANES, LANES), wide)
            ],
            lambda out, d: out.at[pl.ds(pl.multiple_of(d * depth, depth), depth)],
        )

    def back_job(grad):
        return Job(
            grad,
            jax.ShapeDtypeStruct((n_dp, depth, grad.shape[1]), BF16),
            lambda src, d: src.at[pl.ds(pl.multiple_of(d * depth, depth), depth)],
            lambda out, d: out.at[d],
        )

    input_jobs = [[input_job(l, g) for g in range(2)] for l in range(count)]
    down_full = lax.dynamic_update_slice(
        jnp.zeros((count, wide, D), BF16), down_weight, (0, offset, 0)
    )

    def route_lines(routes):
        return jnp.swapaxes(routes[:, 0], 1, 2).reshape(-1, LANES).astype(F32)

    shared = jnp.concatenate([norm_gains, router_weight], axis=1).astype(F32)
    tail = jnp.concatenate([shared.reshape(-1), lengths.reshape(-1).astype(F32)])
    tail = jnp.pad(tail, (0, -tail.shape[0] % LANES)).reshape(-1, LANES)
    small = jnp.concatenate(
        [route_lines(attention_routes), route_lines(feedforward_routes), tail]
    )
    small = jnp.pad(small, ((0, -small.shape[0] % 8), (0, 0)))[None]
    tokens_all, small, *resharded = gather_all(
        [tokens[:, 0]], [True], chips, owners, 1,
        [key_value_job] + [query_job(l) for l in range(count)], [small],
    )
    tokens_all = tokens_all.reshape(seqs, slots, D)
    query_full = jnp.stack(resharded[1:])
    key_value_full = jnp.transpose(resharded[0], (0, 1, 3, 2, 4)).reshape(D, 2 * hc)
    group_slots = mb * TOK_MB * 2
    groups = devices // 2
    lines = mb * 2 * TOK_MB // LANES
    mixer_routes = small[:, :lines].reshape(n_dp, owners, mb, 2, TOK_MB)
    mixer_meta = jnp.transpose(mixer_routes, (2, 0, 3, 1, 4)).reshape(seqs, 2, slots)
    mixer_meta = jnp.pad(mixer_meta, ((0, 0), (0, 6), (0, 0)))
    feed_routes = small[:, lines : 2 * lines].reshape(groups, 2, mb, 2, TOK_MB)
    feed_meta = jnp.transpose(feed_routes, (0, 3, 1, 2, 4)).reshape(groups, 2, group_slots)
    tail = small[:, 2 * lines :].reshape(devices, -1)
    shared_all = tail[:, : slice_rows * 18].reshape(D, 18)
    all_lengths = tail[:, slice_rows * 18 : slice_rows * 18 + mb].reshape(n_dp, owners, mb)
    row_lengths = all_lengths[:, 0].T.reshape(seqs).astype(jnp.int32)
    places = (jnp.arange(owners)[:, None, None] * TOK_MB + jnp.arange(TOK_MB)).astype(F32)
    valid = (places[None] < all_lengths[..., None]).astype(F32).reshape(groups, 1, group_slots)
    feed_meta = jnp.concatenate([feed_meta, valid], axis=1)
    feed_meta = jnp.pad(feed_meta, ((0, 0), (0, 5), (0, 0)))
    gain_mixer, gain_feed = shared_all[:, 0], shared_all[:, 1]
    router_mixer, router_feed = shared_all[:, 2 : 2 + NEXP], shared_all[:, 2 + NEXP :]

    def routers(part):
        return jnp.pad(part.astype(BF16), ((0, 0), (0, LANES - NEXP)))

    own_tokens = tokens[:, 0].astype(F32)
    home_places = ex * TOK_MB + jnp.arange(TOK_MB, dtype=jnp.int32)
    own_valid = (home_places[None, :] < lengths[:, :1]).astype(F32)
    own_cotangent = cotangent[:, 0].astype(F32) * own_valid[..., None]

    normed_mixer, inverse_mixer = norm_forward(own_tokens, gain_mixer)
    fixed = constants(slots)
    tables = mixer_tables(slots)
    (
        mixer_all, mixer_part, rows_mixer, keys, values, queries, mixture, mixture_gated, info,
        gates_mixer, cot_all, *input_parts,
    ) = mixer_forward(
        tokens_all, mixer_meta, row_lengths, gain_mixer[None], routers(router_mixer), query_full,
        key_value_full, output_weight, (*fixed, *tables),
        Riders(chips, owners, input_jobs[0][:1], gather=(cotangent[:, 0], False)), 2,
    )
    cot_all = cot_all.reshape(groups, group_slots, D)
    mixer_sum, *more_parts = scatter_sum(
        mixer_part.reshape(mb, devices, TOK_MB, D), chips, owners, True, 10, input_jobs[0][1:]
    )
    input_parts += more_parts

    second = own_tokens + mixer_sum
    normed_feed, inverse_feed = norm_forward(second, gain_feed)
    feed_all, *more_parts = gather_all(
        [normed_feed.astype(BF16)], [False], chips, owners, 3,
        input_jobs[1][:1] if count > 1 else [],
    )
    input_parts += more_parts
    feed_all = feed_all.reshape(groups, group_slots, D)
    feed_fixed = constants(group_slots)
    before, back_jobs, actives, cots, gate_terms_feed = [], [], [], [], 0.0
    for l in range(count):
        carried = [job for jobs in input_jobs[l + 1 : l + 2] for job in jobs[l == 0 :]]
        carried += back_jobs[:1]
        (
            feed_part, grad_feed_part, rows_feed, cot_rows, active_gated, grad_gate, grad_up,
            terms, gates_feed, *more_parts,
        ) = feed(
            feed_all, cot_all, feed_meta, routers(router_feed), input_parts[2 * l], input_parts[2 * l + 1],
            down_full[l], feed_fixed, offset, offsets, l, count, before, Riders(chips, owners, carried),
            60 + l,
        )
        before += [feed_part, grad_feed_part]
        grad_input_parts = more_parts[len(carried) - len(back_jobs[:1]) :]
        input_parts += more_parts[: len(carried) - len(back_jobs[:1])]
        for grad in (grad_gate, grad_up):
            back_jobs.append(back_job(product("rd,rf->df", rows_feed, grad).astype(BF16)))
        actives.append(active_gated[:, :share])
        cots.append(cot_rows)
        gate_terms_feed = gate_terms_feed + terms
    if count > 1:
        back_jobs = back_jobs[1:]
    grad_down = product("lrf,lrd->lfd", jnp.stack(actives), jnp.stack(cots))

    def home_parts(terms, by_row):
        terms = terms[..., :2]
        if by_row:
            terms = jnp.swapaxes(terms.reshape(mb, devices, TOK_MB * 2), 0, 1)
        terms = terms.reshape(devices, -1, LANES)
        return jnp.pad(terms, ((0, 0), (0, -terms.shape[1] % 8), (0, 0)))

    def at_home(parts):
        return jnp.sum(parts, axis=0).reshape(-1)[: mb * TOK_MB * 2].reshape(mb, TOK_MB, 2)

    def own_of(gates, by_row):
        gates = gates[..., :2]
        if by_row:
            return lax.dynamic_index_in_dim(
                gates.reshape(mb, devices, TOK_MB, 2), me, 1, keepdims=False
            )
        return lax.dynamic_index_in_dim(
            gates.reshape(devices, mb, TOK_MB, 2), me, 0, keepdims=False
        )

    grad_normed_feed, *more_parts, terms = scatter_sum(
        grad_feed_part.reshape(devices, mb, TOK_MB, D), chips, owners, False, 20, back_jobs[:1],
        [home_parts(gate_terms_feed, False)],
    )
    grad_input_parts += more_parts
    grad_logits_feed = gate_grads(
        own_of(gates_feed, False), at_home(terms), feedforward_routes[:, 0]
    )
    grad_normed_feed = grad_normed_feed + product("mte,de->mtd", grad_logits_feed, router_feed)
    grad_second, grad_gain_feed = norm_backward(second, inverse_feed, gain_feed, grad_normed_feed)
    grad_second = grad_second + own_cotangent

    grad_all, *more_parts = gather_all(
        [grad_second.astype(BF16)], [True], chips, owners, 5, back_jobs[1:2]
    )
    grad_input_parts += more_parts
    grad_all = grad_all.reshape(seqs, slots, D)
    feed_part = feed_part.reshape(devices, mb, TOK_MB, D)
    beside = scatter_parts(chips, owners, TOK_MB, D) == 1
    (
        grad_mixer_part, grad_rows, gate_terms_mixer, grad_query_pre, grad_key_value, *more_parts
    ) = mixer_backward(
        grad_all, mixer_meta, row_lengths, query_full, key_value_full, output_weight,
        (*fixed, *tables), (keys, values, queries, mixture, info),
        Riders(chips, owners, back_jobs[2:], scatter=(feed_part, False) if beside else None), 6,
    )
    if not beside:
        more_parts = scatter_sum(feed_part, chips, owners, False, 30) + more_parts
    feed_sum, *more_parts = more_parts
    grad_input_parts += more_parts
    result = (second + feed_sum).astype(BF16)[:, None]
    grad_output = product("lrc,lrd->lcd", mixture_gated, grad_rows)
    grad_query = [
        product("rd,rc->dc", rows_mixer[l], grad_query_pre[l]).astype(BF16) for l in range(count)
    ]
    grad_key_value_w = product("std,stc->dc", mixer_all, grad_key_value).astype(BF16)
    grad_normed_mixer, *more_parts = scatter_sum(
        grad_mixer_part.reshape(mb, devices, TOK_MB, D), chips, owners, True, 40,
        [back_job(grad) for grad in grad_query],
        [
            home_parts(gate_terms_mixer, True),
            grad_key_value_w.reshape(devices, slice_rows, 2 * hc),
        ],
    )
    *more_parts, terms, grad_key_value_w = more_parts
    grad_query, grad_key_value_w = rejoin(more_parts, grad_key_value_w, owners)
    grad_logits_mixer = gate_grads(
        own_of(gates_mixer, True), at_home(terms), attention_routes[:, 0]
    )
    grad_normed_mixer = grad_normed_mixer + product("mte,de->mtd", grad_logits_mixer, router_mixer)
    grad_tokens, grad_gain_mixer = norm_backward(
        own_tokens, inverse_mixer, gain_mixer, grad_normed_mixer
    )
    grad_tokens = (grad_tokens + grad_second).astype(BF16)[:, None]

    router_terms = [
        product("mtd,mte->de", normed.astype(BF16), logits.astype(BF16))
        for normed, logits in ((normed_mixer, grad_logits_mixer), (normed_feed, grad_logits_feed))
    ]
    last = jnp.concatenate([grad_gain_mixer[:, None], grad_gain_feed[:, None], *router_terms], axis=1)
    last = last.reshape(devices, slice_rows * 18)
    last = jnp.pad(last, ((0, 0), (0, -last.shape[1] % (8 * LANES)))).reshape(devices, -1, LANES)
    last = jnp.sum(exchange(last, chips, owners, 8), axis=0).reshape(-1)
    last = last[: slice_rows * 18].reshape(slice_rows, 18)
    grad_gains, grad_router = last[:, :2], last[:, 2:]

    grad_input = put_together(grad_input_parts, count, starts, tiles)
    return (
        result, grad_tokens, grad_gains, grad_router, grad_key_value_w, grad_query,
        grad_output, grad_input, grad_down,
    )


def solution(mesh):
    shared = P(("dp", "expert"), None)
    slots = P(None, "dp", "expert", None)
    owned = P("expert", "dp", None)
    return jax.shard_map(
        shards,
        mesh=mesh,
        in_specs=(slots, P(None, "dp"), slots, slots, shared, shared, shared) + (owned,) * 4 + (slots,),
        out_specs=(slots, slots, shared, shared, shared) + (owned,) * 4,
        check_vma=False,
    )
```

```python
import functools

import jax
import jax.numpy as jnp
import numpy as np
from jax import lax
from jax.experimental import pallas as pl
from jax.experimental.pallas import tpu as pltpu
from jax.sharding import PartitionSpec as P

MESH = pl.DeviceIdType.MESH
BF16 = jnp.bfloat16
F32 = jnp.float32
ANY = pl.BlockSpec(memory_space=pl.ANY)


def expert_factors(owners):
    return (2, owners // 2) if owners % 2 == 0 and owners > 2 else (1, owners)


class Place:
    def __init__(self, chips, first, second):
        dp = lax.axis_index("dp")
        ex = lax.axis_index("expert")
        self.chips, self.first, self.second = chips, first, second
        self.owners, self.n_dp = first * second, chips * 2
        self.dp, self.ex = dp, ex
        self.z, self.k = dp // 2, dp % 2
        self.a, self.b = ex // second, ex % second

    def at(self, z=None, k=None, a=None, b=None):
        z = self.z if z is None else z
        k = self.k if k is None else k
        a = self.a if a is None else a
        b = self.b if b is None else b
        return (z * 2 + k, a * self.second + b)

    def other(self, i):
        number = (self.dp * self.owners + self.ex + i) % (self.n_dp * self.owners)
        return number, (number // self.owners, number % self.owners)

    def greet(self, reach):
        barrier = pltpu.get_barrier_semaphore()

        def hello(target):
            pl.semaphore_signal(barrier, inc=1, device_id=target, device_id_type=MESH)

        if reach == "all":
            count = self.n_dp * self.owners - 1

            def one(i, carried):
                hello(self.other(i)[1])
                return carried

            lax.fori_loop(1, count + 1, one, 0)
            pl.semaphore_wait(barrier, count)
            return
        if reach in ("column", "dp"):
            for i in range(1, self.n_dp):
                hello(((self.dp + i) % self.n_dp, self.ex))
        if reach == "column":
            pl.semaphore_wait(barrier, self.n_dp - 1)
            return
        for i in range(1, self.first):
            hello(self.at(a=(self.a + i) % self.first))
        for i in range(1, self.second):
            hello(self.at(b=(self.b + i) % self.second))
        if reach == "dp":
            pl.semaphore_wait(barrier, self.first + self.second + self.n_dp - 3)
            return
        hello(self.at(k=1 - self.k))
        pl.when(self.z > 0)(lambda: hello(self.at(z=self.z - 1)))
        pl.when(self.z < self.chips - 1)(lambda: hello(self.at(z=self.z + 1)))
        along = (self.z > 0).astype(jnp.int32) + (self.z < self.chips - 1).astype(jnp.int32)
        pl.semaphore_wait(barrier, self.first + self.second - 1 + along)


def remote(src, dst, send, recv, target):
    return pltpu.make_async_remote_copy(
        src_ref=src, dst_ref=dst, send_sem=send, recv_sem=recv, device_id=target, device_id_type=MESH
    )


class Job:
    def __init__(self, src, out_shape, pick, put):
        self.src, self.out_shape, self.pick, self.put = src, out_shape, pick, put


class Load:
    def __init__(self, jobs, me, srcs, outs, sems):
        self.jobs, self.me, self.srcs, self.outs = jobs, me, srcs, outs
        self.own, self.send, self.recv = sems if jobs else (None,) * 3

    def peers(self):
        return [(i, (self.me.dp + i) % self.me.n_dp) for i in range(1, self.me.n_dp)]

    def copy(self, j, i, d):
        me, job = self.me, self.jobs[j]
        return remote(
            job.pick(self.srcs[j], d), job.put(self.outs[j], me.dp),
            self.send.at[j, i], self.recv.at[j, me.dp], (d, me.ex),
        )

    def stay(self, j):
        job, dp = self.jobs[j], self.me.dp
        return pltpu.make_async_copy(
            job.pick(self.srcs[j], dp), job.put(self.outs[j], dp), self.own.at[j]
        )

    def start(self, chosen=None):
        for j in range(len(self.jobs)) if chosen is None else chosen:
            for i, d in self.peers():
                self.copy(j, i, d).start()
            self.stay(j).start()

    def landed(self, j):
        self.stay(j).wait()
        for i, d in self.peers():
            dst = self.jobs[j].put(self.outs[j], d)
            remote(dst, dst, self.send.at[j, i], self.recv.at[j, d], (d, self.me.ex)).wait_recv()

    def finish(self, skip=()):
        for j in range(len(self.jobs)):
            if j not in skip:
                self.landed(j)
            for i, d in self.peers():
                self.copy(j, i, d).wait_send()

    @staticmethod
    def scratch(jobs, n_dp):
        if not jobs:
            return []
        sem = pltpu.SemaphoreType.DMA
        return [sem((len(jobs),)), sem((len(jobs), n_dp)), sem((len(jobs), n_dp))]


class Work:
    def __init__(self, a, b, dtype, l=None, keep=None, slot=None):
        self.ins, self.l, self.keep, self.slot = (a, b), l, keep, slot
        (self.k, self.m), self.n = a.shape[-2:], b.shape[-1]
        shape = (keep or self.m, self.n)
        self.shape = jax.ShapeDtypeStruct(shape if slot is None else (slot[1],) + shape, dtype)

    def run(self, a_ref, b_ref, out_ref):
        if self.l is not None:
            a_ref = a_ref.at[self.l] if len(a_ref.shape) == 3 else a_ref
            b_ref = b_ref.at[self.l] if len(b_ref.shape) == 3 else b_ref
        k, m, n, keep = self.k, self.m, self.n, self.keep

        def body(a, b, out):
            value = lax.dot_general(
                a[...], b[...], (((0,), (0,)), ((), ())), preferred_element_type=F32
            )
            out[...] = value[: out.shape[0]].astype(out.dtype)

        if keep is None:
            blk = 256 if k <= 8192 else 128
            specs = [pl.BlockSpec((k, blk), lambda i: (0, i)), pl.BlockSpec((k, n), lambda i: (0, 0))]
            out = pl.BlockSpec((blk, n), lambda i: (i, 0))
            grid = m // blk
        else:
            blk = 512
            specs = [pl.BlockSpec((k, m), lambda i: (0, 0)), pl.BlockSpec((k, blk), lambda i: (0, i))]
            out = pl.BlockSpec((keep, blk), lambda i: (0, i))
            grid = n // blk
        pltpu.emit_pipeline(body, grid=(grid,), in_specs=specs, out_specs=[out])(
            a_ref, b_ref, out_ref
        )


class Works:
    def __init__(self, works, ins, outs):
        self.works, self.ins, self.outs = works, ins, outs

    def run(self, i):
        if i < len(self.works):
            slot = self.works[i].slot
            out = self.outs[i] if slot is None else self.outs[i - slot[0]].at[slot[0]]
            self.works[i].run(*self.ins[2 * i : 2 * i + 2], out)

    @staticmethod
    def shapes(works):
        return [work.shape for work in works if work.slot is None or work.slot[0] == 0]

    @staticmethod
    def taken(works, refs):
        return [
            refs.pop(0) if work.slot is None or work.slot[0] == 0 else None for work in works
        ]

    @staticmethod
    def arrays(works):
        return [a for work in works for a in work.ins]


class Fold:
    def __init__(self, me, x_ref, out_ref, refs):
        self.me, self.x_ref, self.out_ref = me, x_ref, out_ref
        self.here, self.got, self.sem, self.send, self.recv, self.send_dp, self.recv_dp = refs

    @staticmethod
    def scratch(n_dp, owners, rows, columns):
        sem = pltpu.SemaphoreType.DMA
        return [
            pltpu.VMEM((n_dp, rows, columns), BF16),
            pltpu.VMEM((max(owners - 1, 1), n_dp, rows, columns), BF16),
            sem((2,)), sem((owners,)), sem((owners,)), sem((n_dp,)), sem((n_dp,)),
        ]

    def first(self, i):
        me = self.me
        e = (me.ex + i) % me.owners
        slot = me.owners - 1 - i
        return remote(
            self.x_ref.at[:, e], self.got.at[slot], self.send.at[i], self.recv.at[slot], (me.dp, e)
        )

    def second(self, i):
        me = self.me
        d = (me.dp + i) % me.n_dp
        return remote(
            self.here.at[d], self.out_ref.at[me.dp], self.send_dp.at[i], self.recv_dp.at[me.dp],
            (d, me.ex),
        )

    def load(self):
        return pltpu.make_async_copy(self.x_ref.at[:, self.me.ex], self.here, self.sem.at[0])

    def stay(self):
        dp = self.me.dp
        return pltpu.make_async_copy(self.here.at[dp], self.out_ref.at[dp], self.sem.at[1])

    def begin(self):
        self.load().start()
        for i in range(1, self.me.owners):
            self.first(i).start()

    def turn(self):
        self.load().wait()
        total = self.here[...].astype(F32)
        for slot in range(self.me.owners - 1):
            there = self.got.at[slot]
            remote(
                there, there, self.send.at[0], self.recv.at[slot], (self.me.dp, self.me.ex)
            ).wait_recv()
            total = total + self.got[slot].astype(F32)
        self.here[...] = total.astype(BF16)
        self.stay().start()
        for i in range(1, self.me.n_dp):
            self.second(i).start()

    def finish(self):
        me = self.me
        self.stay().wait()
        for i in range(1, me.owners):
            self.first(i).wait_send()
        for i in range(1, me.n_dp):
            d = (me.dp + i) % me.n_dp
            there = self.out_ref.at[d]
            remote(there, there, self.send_dp.at[i], self.recv_dp.at[d], (d, me.ex)).wait_recv()
            self.second(i).wait_send()


class Mail:
    def __init__(self, arrays, me, srcs, outs, sems):
        self.arrays, self.me, self.srcs, self.outs = arrays, me, srcs, outs
        self.devices = me.n_dp * me.owners
        self.number = me.dp * me.owners + me.ex
        self.own, self.send, self.recv = sems if arrays else (None,) * 3

    def part(self, j, n):
        return self.srcs[j].at[0 if self.arrays[j].shape[0] == 1 else n]

    def copy(self, j, i):
        n, where = self.me.other(i)
        return remote(
            self.part(j, n), self.outs[j].at[self.number], self.send.at[j, i],
            self.recv.at[j, self.number], where,
        )

    def stay(self, j):
        return pltpu.make_async_copy(
            self.part(j, self.number), self.outs[j].at[self.number], self.own.at[j]
        )

    def start(self):
        for j in range(len(self.arrays)):

            def one(i, carried, j=j):
                self.copy(j, i).start()
                return carried

            self.stay(j).start()
            lax.fori_loop(1, self.devices, one, 0)

    def finish(self):
        for j in range(len(self.arrays)):

            def one(i, carried, j=j):
                n, where = self.me.other(i)
                there = self.outs[j].at[n]
                remote(there, there, self.send.at[j, i], self.recv.at[j, n], where).wait_recv()
                self.copy(j, i).wait_send()
                return carried

            self.stay(j).wait()
            lax.fori_loop(1, self.devices, one, 0)

    @staticmethod
    def scratch(arrays, devices):
        if not arrays:
            return []
        sem = pltpu.SemaphoreType.DMA
        return [sem((len(arrays),)), sem((len(arrays), devices)), sem((len(arrays), devices))]

    @staticmethod
    def shapes(arrays, devices):
        return [jax.ShapeDtypeStruct((devices,) + a.shape[1:], a.dtype) for a in arrays]


class Gather:
    def __init__(self, me, by_row, x_ref, out_ref, sems):
        self.me, self.by_row, self.x_ref, self.out_ref = me, by_row, x_ref, out_ref
        self.own_sem, self.recv, self.sends = sems
        self.pending = []
        self.own = self.index(me.z, me.a, me.b)

    @staticmethod
    def scratch(chips, first, second):
        sem = pltpu.SemaphoreType.DMA
        sends = 4 + (2 * chips - 1) * (
            2 + 2 * (first + second - 1) + 2 * (second - 1) * first + 2 * (first - 1) * second
        )
        return [sem((2,)), sem((chips * 2 * first * second, 2)), sem((sends,))]

    def index(self, z, a, b):
        return (z * 2 + self.me.k) * self.me.owners + a * self.me.second + b

    def piece(self, blk, h):
        return self.out_ref.at[h, blk] if self.by_row else self.out_ref.at[blk, h]

    def push(self, src, blk, h, target, when=None):
        copy = remote(
            src, self.piece(blk, h), self.sends.at[len(self.pending)], self.recv.at[blk, h], target
        )
        self.pending.append(when)
        copy.start() if when is None else pl.when(when())(copy.start)

    def landed(self, blk, h, when=None):
        there = self.piece(blk, h)
        copy = remote(there, there, self.sends.at[0], self.recv.at[blk, h], self.me.at())
        copy.wait_recv() if when is None else pl.when(when())(copy.wait_recv)

    def there(self, shift):
        if shift == 0:
            return None
        me = self.me
        return lambda: (me.z + shift >= 0) if shift < 0 else (me.z + shift < me.chips)

    def spread(self, blk, source, when=None):
        me = self.me
        for h in range(2):
            for i in range(1, me.second):
                self.push(source(h), blk, h, me.at(b=(me.b + i) % me.second), when)
            for i in range(1, me.first):
                self.push(source(h), blk, h, me.at(a=(me.a + i) % me.first), when)
        for h in range(2):
            self.push(source(h), blk, h, me.at(k=1 - me.k), when)

    def relay(self, shift):
        me, when = self.me, self.there(shift)
        z = me.z + shift
        for h in range(2):
            if h == 0:
                froms = [(me.a, (me.b + i) % me.second) for i in range(1, me.second)]
                onward = [dict(a=(me.a + i) % me.first) for i in range(1, me.first)]
            else:
                froms = [((me.a + i) % me.first, me.b) for i in range(1, me.first)]
                onward = [dict(b=(me.b + i) % me.second) for i in range(1, me.second)]
            for a, b in froms:
                blk = self.index(z, a, b)
                self.landed(blk, h, when)
                for target in onward:
                    self.push(self.piece(blk, h), blk, h, me.at(**target), when)
                self.push(self.piece(blk, h), blk, h, me.at(k=1 - me.k), when)

    def settle(self, shift):
        me, when = self.me, self.there(shift)
        z = me.z + shift
        for h in range(2):
            for i in range(1, me.second if h else me.first):
                for j in range(me.first if h else me.second):
                    if h == 0:
                        a, b = (me.a + i) % me.first, (me.b + j) % me.second
                    else:
                        a, b = (me.a + j) % me.first, (me.b + i) % me.second
                    blk = self.index(z, a, b)
                    self.landed(blk, h, when)
                    self.push(self.piece(blk, h), blk, h, me.at(k=1 - me.k), when)

    def stay(self, h):
        return pltpu.make_async_copy(
            self.x_ref.at[h], self.piece(self.own, h), self.own_sem.at[h]
        )

    def begin(self):
        me, x_ref, own = self.me, self.x_ref, self.own
        for h in range(2):
            self.stay(h).start()
        for h in range(2):
            self.push(x_ref.at[h], own, h, me.at(z=me.z + 1), self.there(1))
            self.push(x_ref.at[h], own, h, me.at(z=me.z - 1), self.there(-1))
        self.spread(own, lambda h: x_ref.at[h])

    def stage(self, t):
        me = self.me
        for shift in (-t, t):
            there, onward = self.there(shift), self.there(1 if shift < 0 else -1)
            blk = self.index(me.z + shift, me.a, me.b)
            for h in range(2):
                self.landed(blk, h, there)
                self.push(
                    self.piece(blk, h), blk, h, me.at(z=me.z + (1 if shift < 0 else -1)),
                    lambda there=there, onward=onward: there() & onward(),
                )
            self.spread(blk, lambda h, blk=blk: self.piece(blk, h), there)

    def drain(self, t):
        shifts = (-t, t) if t else (0,)
        for shift in shifts:
            self.relay(shift)
        for shift in shifts:
            self.settle(shift)

    def along(self):
        return [functools.partial(self.stage, t) for t in range(1, self.me.chips)]

    def across(self):
        return [functools.partial(self.drain, t) for t in range(self.me.chips)]

    def finish(self):
        me = self.me
        for h in range(2):
            self.stay(h).wait()
        for z in range(me.chips):
            for e in range(me.owners):
                for h in range(2):
                    self.landed((z * 2 + 1 - me.k) * me.owners + e, h)
        for i, when in enumerate(self.pending):
            copy = remote(
                self.x_ref.at[0], self.x_ref.at[0], self.sends.at[i], self.recv.at[0, 0], me.at()
            )
            copy.wait_send() if when is None else pl.when(when())(copy.wait_send)


def taken(refs, number):
    return [refs.pop(0) for _ in range(number)]


def gather_kernel(chips, first, second, orders, jobs, mails, works, *refs):
    me = Place(chips, first, second)
    refs = list(refs)
    x_refs = taken(refs, len(orders))
    mail_srcs = taken(refs, len(mails))
    srcs = taken(refs, len(jobs))
    work_ins = taken(refs, 2 * len(works))
    out_refs = taken(refs, len(orders))
    mail_outs = taken(refs, len(mails))
    outs = taken(refs, len(jobs))
    works = Works(works, work_ins, Works.taken(works, refs))
    gathers = [
        Gather(me, by_row, x_ref, out_ref, taken(refs, 3))
        for by_row, x_ref, out_ref in zip(orders, x_refs, out_refs)
    ]
    if mails:
        spread_send, spread_recv = taken(refs, 2)
        mail = Mail(mails, me, mail_srcs, mail_outs, taken(refs, 3))
    load = Load(jobs, me, srcs, outs, refs)
    me.greet("all" if mails else "dp" if jobs else "near")
    for gather in gathers:
        gather.begin()
    if mails:
        mail.start()
    along = [stage for stages in zip(*[gather.along() for gather in gathers]) for stage in stages]
    for i, stage in enumerate(along):
        if i == len(along) - 1:
            load.start()
        stage()
    rest = [stage for stages in zip(*[gather.across() for gather in gathers]) for stage in stages]
    for stage in rest[:2]:
        stage()
    works.run(0)
    if mails:
        j = 0
        load.landed(j)
        column = outs[j].at[:, me.ex]
        spreads = [
            remote(
                column, column, spread_send.at[i], spread_recv.at[me.ex],
                (me.dp, (me.ex + i) % me.owners),
            )
            for i in range(1, me.owners)
        ]
        for copy in spreads:
            copy.start()
    for i, stage in enumerate(rest[2:]):
        stage()
        works.run(1 + i)
    if mails:
        mail.finish()
        for i in range(1, me.owners):
            e = (me.ex + i) % me.owners
            there = outs[j].at[:, e]
            remote(there, there, spread_send.at[i], spread_recv.at[e], (me.dp, e)).wait_recv()
        for copy in spreads:
            copy.wait_send()
    for gather in gathers:
        gather.finish()
    load.finish(skip=(0,) if mails else ())


def gather_all(xs, orders, chips, owners, collective_id, jobs=(), mails=(), works=()):
    first, second = expert_factors(owners)
    blocks = chips * 2 * owners
    sem = pltpu.SemaphoreType.DMA
    shapes = []
    for x, by_row in zip(xs, orders):
        rest = x.shape[1:]
        shape = (2, blocks) + rest if by_row else (blocks, 2) + rest
        shapes.append(jax.ShapeDtypeStruct(shape, x.dtype))
    shapes += Mail.shapes(mails, blocks) + [job.out_shape for job in jobs]
    shapes += Works.shapes(works)
    ins = list(xs) + list(mails) + [job.src for job in jobs] + Works.arrays(works)
    scratch = Gather.scratch(chips, first, second) * len(xs)
    if mails:
        scratch += [sem((owners,)), sem((owners,))] + Mail.scratch(mails, blocks)
    return pl.pallas_call(
        functools.partial(
            gather_kernel, chips, first, second, orders, jobs,
            [jax.ShapeDtypeStruct(a.shape, a.dtype) for a in mails], works,
        ),
        out_shape=shapes,
        in_specs=[ANY] * len(ins),
        out_specs=[ANY] * len(shapes),
        scratch_shapes=scratch + Load.scratch(jobs, chips * 2),
        compiler_params=pltpu.CompilerParams(
            collective_id=collective_id, has_side_effects=True, vmem_limit_bytes=60 * 2**20
        ),
    )(*ins)


class Scatter:
    def __init__(self, me, by_row, column, width, p_ref, out_ref, refs):
        self.me, self.by_row, self.cut = me, by_row, pl.ds(column, width)
        self.p_ref, self.out_ref = p_ref, out_ref
        self.mine, self.fromk, self.a0, self.b0, self.b1, self.a1, self.fromz = refs[:7]
        self.load_sem, self.ks, self.a0s, self.b0s, self.b1s, self.a1s, self.zs, self.sends = refs[7:]
        self.pending = []

    @staticmethod
    def scratch(chips, first, second, half, width):
        sem, owners = pltpu.SemaphoreType.DMA, first * second
        one = max(first - 1, 1), max(second - 1, 1)
        sends = chips * (owners + 2 + 2 * (first - 1) * second + 2 * (second - 1) * first)
        return [
            pltpu.VMEM((chips, owners, 2, half, width), BF16),
            pltpu.VMEM((chips, owners, 2, half, width), BF16),
            pltpu.VMEM((chips, one[0], second, half, width), BF16),
            pltpu.VMEM((chips, one[1], half, width), BF16),
            pltpu.VMEM((chips, one[1], first, half, width), BF16),
            pltpu.VMEM((chips, one[0], half, width), BF16),
            pltpu.VMEM((chips + 1, 2, half, width), BF16),
            sem((chips, owners)),
            sem((chips, owners)),
            sem((chips, one[0], second)),
            sem((chips, one[1])),
            sem((chips, one[1], first)),
            sem((chips, one[0])),
            sem((chips + 1,)),
            sem((sends + chips * (first + second),)),
        ]

    def push(self, src, dst, sem, target, part, when=None):
        copy = remote(src, dst, self.sends.at[len(self.pending)], sem, target)
        self.pending.append((part, when))
        copy.start() if when is None else pl.when(when())(copy.start)

    def landed(self, dst, sem):
        remote(dst, dst, self.sends.at[0], sem, self.me.at()).wait_recv()

    def line(self, t):
        z, chips = self.me.z, self.me.chips
        return jnp.where(
            z < chips // 2,
            jnp.where(t < chips - 1 - z, chips - 1 - t, t - (chips - 1 - z)),
            jnp.where(t < z, t, chips - 1 - (t - z)),
        )

    def block(self, z, k, e):
        blk = (z * 2 + k) * self.me.owners + e
        if self.by_row:
            return self.p_ref.at[:, blk, :, self.cut]
        return self.p_ref.at[blk, :, :, self.cut]

    def begin(self):
        me = self.me
        for t in range(me.chips):
            z = self.line(t)
            for e in range(me.owners):
                pltpu.make_async_copy(
                    self.block(z, me.k, e), self.mine.at[t, e], self.load_sem.at[t, e]
                ).start()
                self.push(
                    self.block(z, 1 - me.k, e), self.fromk.at[t, e], self.ks.at[t, e],
                    me.at(k=1 - me.k), "block",
                )

    @staticmethod
    def add(*terms):
        value = terms[0].astype(F32)
        for term in terms[1:]:
            value = value + term.astype(F32)
        return value

    def step_one(self, t):
        me, mine = self.me, self.mine
        first, second = me.first, me.second
        for i in range(first):
            for j in range(second):
                a, b = (me.a + 1 + i) % first, (me.b + 1 + j) % second
                e = a * second + b
                pltpu.make_async_copy(mine.at[t, e], mine.at[t, e], self.load_sem.at[t, e]).wait()
                self.landed(self.fromk.at[t, e], self.ks.at[t, e])
                mine[t, e] = self.add(mine[t, e], self.fromk[t, e]).astype(BF16)
                if i < first - 1:
                    slot = first - 2 - i
                    self.push(
                        mine.at[t, e, 0], self.a0.at[t, slot, b], self.a0s.at[t, slot, b],
                        me.at(a=a), "half",
                    )
                if j < second - 1:
                    slot = second - 2 - j
                    self.push(
                        mine.at[t, e, 1], self.b1.at[t, slot, a], self.b1s.at[t, slot, a],
                        me.at(b=b), "half",
                    )

    def step_two(self, t):
        me, mine = self.me, self.mine
        first, second = me.first, me.second
        for j in range(second - 1):
            b = (me.b + 1 + j) % second
            e = me.a * second + b
            for i in range(first - 1):
                self.landed(self.a0.at[t, i, b], self.a0s.at[t, i, b])
            mine[t, e, 0] = self.add(
                mine[t, e, 0], *[self.a0[t, i, b] for i in range(first - 1)]
            ).astype(BF16)
            slot = second - 2 - j
            self.push(
                mine.at[t, e, 0], self.b0.at[t, slot], self.b0s.at[t, slot], me.at(b=b), "half"
            )
        for i in range(first - 1):
            a = (me.a + 1 + i) % first
            e = a * second + me.b
            for j in range(second - 1):
                self.landed(self.b1.at[t, j, a], self.b1s.at[t, j, a])
            mine[t, e, 1] = self.add(
                mine[t, e, 1], *[self.b1[t, j, a] for j in range(second - 1)]
            ).astype(BF16)
            slot = first - 2 - i
            self.push(
                mine.at[t, e, 1], self.a1.at[t, slot], self.a1s.at[t, slot], me.at(a=a), "half"
            )

    def step_three(self, t):
        me, mine, total, fromz, zs = self.me, self.mine, self.out_ref, self.fromz, self.zs
        first, second, chips = me.first, me.second, me.chips
        z, e = self.line(t), me.ex
        for i in range(first - 1):
            self.landed(self.a0.at[t, i, me.b], self.a0s.at[t, i, me.b])
            self.landed(self.a1.at[t, i], self.a1s.at[t, i])
        for j in range(second - 1):
            self.landed(self.b1.at[t, j, me.a], self.b1s.at[t, j, me.a])
            self.landed(self.b0.at[t, j], self.b0s.at[t, j])
        total[0] = self.add(
            mine[t, e, 0], *[self.a0[t, i, me.b] for i in range(first - 1)],
            *[self.b0[t, j] for j in range(second - 1)],
        )
        total[1] = self.add(
            mine[t, e, 1], *[self.b1[t, j, me.a] for j in range(second - 1)],
            *[self.a1[t, i] for i in range(first - 1)],
        )

        def also(when, slot):
            @pl.when(when)
            def _():
                self.landed(fromz.at[slot], zs.at[slot])
                total[...] = total[...] + fromz[slot].astype(F32)

        if t < chips - 1:
            up = z > me.z
            also(jnp.where(up, me.z > 0, me.z < chips - 1), z)
            mine[t, e] = total[...].astype(BF16)
            self.push(
                mine.at[t, e], fromz.at[z], zs.at[z], me.at(z=me.z + 1), "block",
                lambda: self.line(t) > me.z,
            )
            slot = jnp.where(z == me.z - 1, chips, z)
            self.push(
                mine.at[t, e], fromz.at[slot], zs.at[slot], me.at(z=me.z - 1), "block",
                lambda: self.line(t) < me.z,
            )
        else:
            also(me.z > 0, me.z)
            also(me.z < chips - 1, chips)

    def stage(self, t):
        if t < self.me.chips:
            self.step_one(t)
        if 0 <= t - 1 < self.me.chips:
            self.step_two(t - 1)
        if 0 <= t - 2 < self.me.chips:
            self.step_three(t - 2)

    def stages(self):
        return [functools.partial(self.stage, t) for t in range(self.me.chips + 2)]

    def finish(self):
        for i, (part, when) in enumerate(self.pending):
            ref = self.mine.at[0, 0] if part == "block" else self.mine.at[0, 0, 0]
            copy = remote(ref, ref, self.sends.at[i], self.zs.at[0], self.me.at())
            copy.wait_send() if when is None else pl.when(when())(copy.wait_send)


def scatter_parts(chips, owners, half, full):
    parts = 1
    while chips * owners * half * (full // parts) * 8 > 16 * 2**20:
        parts *= 2
    return parts


def scatter_kernel(chips, first, second, by_row, column, width, jobs, mails, works, fold, *refs):
    me = Place(chips, first, second)
    refs = list(refs)
    (p_ref,) = taken(refs, 1)
    ready = [j for j, job in enumerate(jobs) if not isinstance(job.src, int)]
    given, mail_srcs = taken(refs, len(ready)), taken(refs, len(mails))
    work_ins = taken(refs, 2 * len(works))
    (out_ref,) = taken(refs, 1)
    outs, mail_outs = taken(refs, len(jobs)), taken(refs, len(mails))
    work_outs = Works.taken(works, refs)
    folded = taken(refs, 0 if fold is None else 1)
    scatter = Scatter(me, by_row, column, width, p_ref, out_ref, taken(refs, 15))
    mail = Mail(mails, me, mail_srcs, mail_outs, taken(refs, 3) if mails else ())
    if fold is not None:
        x_ref = work_outs[fold].reshape(
            me.n_dp, me.owners, folded[0].shape[1], folded[0].shape[2]
        )
        folding = Fold(me, x_ref, folded[0], taken(refs, 7))
    srcs = [given.pop(0) if j in ready else work_outs[job.src] for j, job in enumerate(jobs)]
    load = Load(jobs, me, srcs, outs, refs)
    doing = Works(works, work_ins, work_outs)
    me.greet("all" if mails else "dp" if jobs else "near")
    scatter.begin()
    mail.start()
    load.start(ready)
    stages = scatter.stages()
    for i in range(max(len(stages), len(works))):
        if i < len(stages):
            stages[i]()
        if fold is not None and i == fold + 1:
            folding.turn()
        doing.run(i)
        load.start([j for j, job in enumerate(jobs) if j not in ready and job.src == i])
        if i == fold:
            folding.begin()
    mail.finish()
    load.finish()
    if fold is not None:
        folding.finish()
    scatter.finish()


def scatter_sum(p, chips, owners, by_row, collective_id, jobs=(), mails=(), works=(), fold=None):
    first, second = expert_factors(owners)
    half, full = p.shape[2:]
    parts = scatter_parts(chips, owners, half, full)
    width = full // parts
    n_dp = chips * 2

    def call(part, jobs, mails, works, fold):
        extra_shapes, extra_scratch = [], []
        if fold is not None:
            rows, columns = works[fold].shape.shape
            cut = (n_dp, rows // (n_dp * owners), columns)
            extra_shapes = [jax.ShapeDtypeStruct(cut, BF16)]
            extra_scratch = Fold.scratch(n_dp, owners, cut[1], columns)
        shapes = [jax.ShapeDtypeStruct((2, half, width), F32)]
        shapes += [job.out_shape for job in jobs] + Mail.shapes(mails, n_dp * owners)
        shapes += Works.shapes(works) + extra_shapes
        ins = [p] + [job.src for job in jobs if not isinstance(job.src, int)]
        ins += list(mails) + Works.arrays(works)
        return pl.pallas_call(
            functools.partial(
                scatter_kernel, chips, first, second, by_row, part * width, width, jobs,
                [jax.ShapeDtypeStruct(a.shape, a.dtype) for a in mails], works, fold,
            ),
            out_shape=shapes,
            in_specs=[ANY] * len(ins),
            out_specs=[pl.BlockSpec(memory_space=pltpu.VMEM)] + [ANY] * (len(shapes) - 1),
            scratch_shapes=Scatter.scratch(chips, first, second, half, width)
            + Mail.scratch(mails, n_dp * owners)
            + extra_scratch
            + Load.scratch(jobs, n_dp),
            compiler_params=pltpu.CompilerParams(
                collective_id=collective_id + part, has_side_effects=True,
                vmem_limit_bytes=60 * 2**20,
            ),
        )(*ins)

    calls = [call(0, jobs, mails, works, fold)]
    calls += [call(part, (), (), (), None) for part in range(1, parts)]
    whole = calls[0][0] if parts == 1 else jnp.concatenate([c[0] for c in calls], axis=-1)
    return [whole] + list(calls[0][1:])


class Riders:
    def __init__(self, chips, owners, jobs=(), gather=None, scatter=None):
        self.chips, self.owners, self.jobs = chips, owners, jobs
        self.factors = expert_factors(owners)
        self.orders = [order for pair in (gather, scatter) if pair for order in pair[1:]]
        self.has = gather is not None, scatter is not None
        self.ins = [pair[0] for pair in (gather, scatter) if pair] + [job.src for job in jobs]
        self.out_shapes, self.out_specs, self.scratch = [], [], []
        blocks = chips * 2 * owners
        if gather:
            x, by_row = gather
            rest = x.shape[1:]
            shape = (2, blocks) + rest if by_row else (blocks, 2) + rest
            self.out_shapes.append(jax.ShapeDtypeStruct(shape, x.dtype))
            self.out_specs.append(ANY)
            self.scratch += Gather.scratch(chips, *self.factors)
        if scatter:
            half, full = scatter[0].shape[2:]
            shape = jax.ShapeDtypeStruct((2, half, full), F32)
            self.out_shapes.append(shape)
            self.out_specs.append(pl.BlockSpec(shape.shape, lambda i: (0, 0, 0)))
            self.scratch += Scatter.scratch(chips, *self.factors, half, full)
            self.full = full
        self.out_shapes += [job.out_shape for job in jobs]
        self.out_specs += [ANY] * len(jobs)
        self.scratch += Load.scratch(jobs, chips * 2)
        self.ins_specs = [ANY] * len(self.ins)
        self.count = len(self.ins)

    def params(self, collective_id):
        if not self.count:
            return dict(vmem_limit_bytes=60 * 2**20)
        return dict(
            vmem_limit_bytes=60 * 2**20, collective_id=collective_id, has_side_effects=True
        )

    def board(self, refs, ins, outs, scratch=0):
        refs = list(refs)
        own = taken(refs, ins)
        given = taken(refs, self.count)
        own += taken(refs, outs)
        results = taken(refs, self.count)
        own += taken(refs, scratch)
        if not self.count:
            return own
        self.me = me = Place(self.chips, *self.factors)
        orders, staged, self.stages = list(self.orders), [], []
        if self.has[0]:
            rider = Gather(me, orders.pop(0), given.pop(0), results.pop(0), taken(refs, 3))
            staged.append(rider)
        if self.has[1]:
            rider = Scatter(
                me, orders.pop(0), 0, self.full, given.pop(0), results.pop(0), taken(refs, 15)
            )
            staged.append(rider)
        load = Load(self.jobs, me, given, results, refs)
        step, steps = pl.program_id(0), pl.num_programs(0)

        @pl.when(step == 0)
        def _():
            me.greet("column" if not staged else "dp" if self.jobs else "near")
            for rider in staged:
                rider.begin()
            if not self.has[0]:
                load.start()

        plan = []
        for rider in staged:
            if isinstance(rider, Gather):
                along, across = rider.along(), rider.across()
                along.insert(len(along) - 1, load.start)
                unit = max(1, (self.steps - 4) // self.chips)
                spots = [unit * (i + 1) for i in range(self.chips - 1)]
                spots.insert(len(spots) - 1, spots[max(0, len(spots) - 2)])
                spots += [unit * (i + 1) + 2 for i in range(self.chips)]
                plan += list(zip(spots, along + across))
            else:
                stages = rider.stages()
                plan += [
                    (1 + i * (self.steps - 2) // (len(stages) - 1), stage)
                    for i, stage in enumerate(stages)
                ]
        for at, stage in plan:
            pl.when(step == at)(stage)

        def finish():
            @pl.when(step == steps - 1)
            def _():
                for rider in staged:
                    rider.finish()
                load.finish()

        self.alight = finish
        return own

    def alight(self):
        pass


def exchange_kernel(chips, first, second, array, x_ref, out_ref, *sems):
    me = Place(chips, first, second)
    mail = Mail([array], me, [x_ref], [out_ref], sems)
    me.greet("all")
    mail.start()
    mail.finish()


def exchange(x, chips, owners, collective_id):
    first, second = expert_factors(owners)
    devices = chips * 2 * owners
    shape = jax.ShapeDtypeStruct(x.shape, x.dtype)
    return pl.pallas_call(
        functools.partial(exchange_kernel, chips, first, second, shape),
        out_shape=shape,
        in_specs=[ANY],
        out_specs=ANY,
        scratch_shapes=Mail.scratch([shape], devices),
        compiler_params=pltpu.CompilerParams(collective_id=collective_id, has_side_effects=True),
    )(x)


D = 2048
KVH = 16
HD = 128
FF = 5632
NEXP = 8
TOK_MB = 64
CAP = 24
LANES = 128
EPSILON = 1e-06


def dot(a, b):
    return jnp.dot(a, b, preferred_element_type=F32)


def dot_nt(a, b):
    return lax.dot_general(a, b, (((1,), (1,)), ((), ())), preferred_element_type=F32)


def dot_tn(a, b):
    return lax.dot_general(a, b, (((0,), (0,)), ((), ())), preferred_element_type=F32)


def counted(shape, axis):
    return lax.broadcasted_iota(jnp.int32, shape, axis).astype(F32)


def two_parts(value):
    upper = value.astype(BF16)
    return upper, (value - upper.astype(F32)).astype(BF16)


class Seats:
    def __init__(self, meta, first_expert, count, tri, eye):
        slots = meta.shape[1]
        per = slots // TOK_MB * CAP
        self.count, self.per, self.slots, self.first = count, per, slots, first_expert
        line = counted(meta.shape, 0)
        expert = first_expert + line
        hit = (meta[0:1] == expert) | (meta[1:2] == expert)
        hit = hit & (line < count)
        rank = dot(jnp.where(hit, 1.0, 0.0).astype(BF16), tri)
        block = lax.broadcasted_iota(jnp.int32, meta.shape, 1) // TOK_MB
        seat = jnp.where(hit, block.astype(F32) * CAP + rank + line * per, -1.0)
        self.routes = dot_nt(eye, meta.astype(BF16))
        column = dot_nt(eye, seat.astype(BF16))
        total = count * per
        row = counted((total, slots), 0)
        lane = counted((slots, total), 1)
        here, there = row == seat[0:1], lane == column[:, 0:1]
        for l in range(1, count):
            here = here | (row == seat[l : l + 1])
            there = there | (lane == column[:, l : l + 1])
        self.take = jnp.where(here, 1.0, 0.0).astype(BF16)
        self.put = jnp.where(there, 1.0, 0.0).astype(BF16)

    def gates(self, logits):
        lane = counted(logits.shape, 1)
        one = jnp.sum(jnp.where(lane == self.routes[:, 0:1], logits, 0.0), axis=1, keepdims=True)
        two = jnp.sum(jnp.where(lane == self.routes[:, 1:2], logits, 0.0), axis=1, keepdims=True)
        highest = jnp.maximum(one, two)
        one, two = jnp.exp(one - highest), jnp.exp(two - highest)
        total = one + two
        return one / total, two / total

    def seat_values(self, pairs, plain):
        lane = counted((self.slots, LANES), 1)
        per_expert = []
        for l in range(self.count):
            expert = self.first + l
            values = [
                jnp.where(self.routes[:, 0:1] == expert, a, 0.0)
                + jnp.where(self.routes[:, 1:2] == expert, b, 0.0)
                for a, b in pairs
            ] + list(plain)
            packed = jnp.zeros((self.slots, LANES), F32)
            for i, value in enumerate(values):
                upper, lower = two_parts(value)
                packed = jnp.where(lane == 2 * i, upper.astype(F32), packed)
                packed = jnp.where(lane == 2 * i + 1, lower.astype(F32), packed)
            part = dot(self.take[l * self.per : (l + 1) * self.per], packed.astype(BF16))
            per_expert.append(
                [part[:, 2 * i : 2 * i + 1] + part[:, 2 * i + 1 : 2 * i + 2] for i in range(len(values))]
            )
        return [
            jnp.concatenate(parts, axis=0) if self.count > 1 else parts[0]
            for parts in zip(*per_expert)
        ]

    def slot_values(self, value):
        total = self.count * self.per
        lane = counted((total, LANES), 1)
        row = counted((total, LANES), 0)
        upper, lower = two_parts(value)
        packed = jnp.zeros((total, LANES), F32)
        for l in range(self.count):
            mine = (row >= l * self.per) & (row < (l + 1) * self.per)
            packed = jnp.where(mine & (lane == 2 * l), upper.astype(F32), packed)
            packed = jnp.where(mine & (lane == 2 * l + 1), lower.astype(F32), packed)
        back = dot(self.put, packed.astype(BF16))
        out = jnp.zeros((self.slots, 8), F32)
        lane = counted((self.slots, 8), 1)
        for l in range(self.count):
            value = back[:, 2 * l : 2 * l + 1] + back[:, 2 * l + 1 : 2 * l + 2]
            for k in range(2):
                chosen = (self.routes[:, k : k + 1] == self.first + l) & (lane == k)
                out = jnp.where(chosen, value, out)
        return out


def first_expert(count):
    return (lax.axis_index("expert") * count).astype(F32)


def turned(values, cosine, sine):
    heads = []
    for h in range(values.shape[1] // HD):
        head = values[:, h * HD : (h + 1) * HD]
        heads.append(head * cosine + pltpu.roll(head, HD // 2, 1) * sine)
    return heads[0] if len(heads) == 1 else jnp.concatenate(heads, axis=1)


def mixer_forward_kernel(count, riders, *refs):
    (
        length_ref, x_ref, meta_ref, gain_ref, router_ref, *wq_refs, wkv_ref, wo_ref,
        tri_ref, eye_ref, upper_ref, lower_ref,
        normed_ref, part_ref, rows_ref, key_ref, value_ref, query_ref, mix_ref, gated_ref, info_ref, gates_ref,
    ) = riders.board(refs, 11 + count, 10)
    hc = key_ref.shape[2]
    x = x_ref[0].astype(F32)
    inverse = lax.rsqrt(jnp.mean(x * x, axis=1, keepdims=True) + EPSILON)
    normed = (x * inverse * gain_ref[...]).astype(BF16)
    normed_ref[0] = normed
    seats = Seats(meta_ref[0], first_expert(count), count, tri_ref[...], eye_ref[...])
    one, two = seats.gates(dot(normed, router_ref[...]))
    lane = counted((seats.slots, 8), 1)
    gates_ref[0] = jnp.where(lane == 0, one, jnp.where(lane == 1, two, 0.0))
    gate, place = seats.seat_values([(one, two)], [counted((seats.slots, 1), 0)])
    lane = counted((gate.shape[0], 8), 1)
    info_ref[0] = jnp.where(lane == 0, gate, jnp.where(lane == 1, place, 0.0))

    key_value = dot(normed, wkv_ref[...])
    upper, lower = upper_ref[...], lower_ref[...]
    table = upper.astype(F32) + lower.astype(F32)
    key = turned(key_value[:, :hc], table[:, :HD], table[:, HD:]).astype(BF16)
    value = key_value[:, hc:].astype(BF16)
    key_ref[0], value_ref[0] = key, value

    rows = dot(seats.take, normed).astype(BF16)
    per = seats.per
    for l in range(count):
        rows_ref[l] = rows[l * per : (l + 1) * per]
    table = dot(seats.take, upper) + dot(seats.take, lower)
    query = [dot(rows[l * per : (l + 1) * per], wq_refs[l][...]) for l in range(count)]
    query = query[0] if count == 1 else jnp.concatenate(query, axis=0)
    query = (turned(query, table[:, :HD], table[:, HD:]) * HD ** (-0.5)).astype(BF16)
    query_ref[0] = query

    at = counted((seats.take.shape), 1)
    length = length_ref[pl.program_id(0)].astype(F32)
    allowed = (at <= place) & (at < length)
    mix = []
    for h in range(hc // HD):
        cut = slice(h * HD, (h + 1) * HD)
        scores = jnp.where(allowed, dot_nt(query[:, cut], key[:, cut]), -1e30)
        exponent = jnp.exp(scores - jnp.max(scores, axis=1, keepdims=True))
        probs = (exponent / jnp.sum(exponent, axis=1, keepdims=True)).astype(BF16)
        mix.append(dot(probs, value[:, cut]))
    mix = mix[0] if len(mix) == 1 else jnp.concatenate(mix, axis=1)
    mix_ref[0] = mix
    gated = (mix * gate).astype(BF16)
    for l in range(count):
        gated_ref[l] = gated[l * per : (l + 1) * per]
    out = [dot(gated[l * per : (l + 1) * per], wo_ref[l]).astype(BF16) for l in range(count)]
    out = out[0] if count == 1 else jnp.concatenate(out, axis=0)
    part_ref[0] = dot(seats.put, out).astype(BF16)
    riders.alight()


def mixer_backward_kernel(count, riders, *refs):
    (
        length_ref, grad_ref, meta_ref, *wq_refs, wkv_ref, wo_ref, tri_ref, eye_ref,
        upper_ref, lower_ref, key_ref, value_ref, query_ref, mix_ref, info_ref,
        part_ref, rows_ref, terms_ref, grad_query_ref, grad_key_value_ref,
    ) = riders.board(refs, 14 + count, 5)
    hc = key_ref.shape[2]
    seats = Seats(meta_ref[0], first_expert(count), count, tri_ref[...], eye_ref[...])
    per = seats.per
    rows = dot(seats.take, grad_ref[0]).astype(BF16)
    for l in range(count):
        rows_ref[l] = rows[l * per : (l + 1) * per]
    grad_mix = [dot_nt(rows[l * per : (l + 1) * per], wo_ref[l]) for l in range(count)]
    grad_mix = grad_mix[0] if count == 1 else jnp.concatenate(grad_mix, axis=0)
    gate, place = info_ref[0, :, 0:1], info_ref[0, :, 1:2]
    terms_ref[0] = seats.slot_values(jnp.sum(grad_mix * mix_ref[0], axis=1, keepdims=True))
    grad_mix = (grad_mix * gate).astype(BF16)

    at = counted(seats.take.shape, 1)
    length = length_ref[pl.program_id(0)].astype(F32)
    allowed = (at <= place) & (at < length)
    key, value, query = key_ref[0], value_ref[0], query_ref[0]
    grad_query, grad_key, grad_value = [], [], []
    for h in range(hc // HD):
        cut = slice(h * HD, (h + 1) * HD)
        scores = jnp.where(allowed, dot_nt(query[:, cut], key[:, cut]), -1e30)
        exponent = jnp.exp(scores - jnp.max(scores, axis=1, keepdims=True))
        probs = exponent / jnp.sum(exponent, axis=1, keepdims=True)
        grad_probs = dot_nt(grad_mix[:, cut], value[:, cut])
        grad_value.append(dot_tn(probs.astype(BF16), grad_mix[:, cut]))
        row_dot = jnp.sum(probs * grad_probs, axis=1, keepdims=True)
        grad_scores = (probs * (grad_probs - row_dot)).astype(BF16)
        grad_query.append(dot(grad_scores, key[:, cut]))
        grad_key.append(dot_tn(grad_scores, query[:, cut]))

    def joined(parts):
        return parts[0] if len(parts) == 1 else jnp.concatenate(parts, axis=1)

    upper, lower = upper_ref[...], lower_ref[...]
    table = dot(seats.take, upper) + dot(seats.take, lower)
    grad_query = turned(joined(grad_query), table[:, :HD], -table[:, HD:]) * HD ** (-0.5)
    grad_query = grad_query.astype(BF16)
    for l in range(count):
        grad_query_ref[l] = grad_query[l * per : (l + 1) * per]
    table = upper.astype(F32) + lower.astype(F32)
    grad_key = turned(joined(grad_key), table[:, :HD], -table[:, HD:])
    grad_key_value = jnp.concatenate([grad_key, joined(grad_value)], axis=1).astype(BF16)
    grad_key_value_ref[0] = grad_key_value
    back = [
        dot_nt(grad_query[l * per : (l + 1) * per], wq_refs[l][...]).astype(BF16)
        for l in range(count)
    ]
    back = back[0] if count == 1 else jnp.concatenate(back, axis=0)
    part_ref[0] = (dot(seats.put, back) + dot_nt(grad_key_value, wkv_ref[...])).astype(BF16)
    riders.alight()


def feed_kernel(count, l, last, groups, turns, riders, *refs):
    prior = 2 * l if last else 0
    refs = riders.board(refs, 10 + prior, 9 if last else 9, 4 if last else 2)
    (
        offset_ref, x_ref, cot_ref, meta_ref, router_ref, wg_ref, wu_ref, wd_ref, tri_ref, eye_ref,
    ) = refs[:10]
    before, refs = refs[10 : 10 + prior], refs[10 + prior :]
    part_ref, back_ref, rows_ref, cot_rows_ref, active_ref, grad_gate_ref, grad_up_ref, terms_ref, gates_ref = refs[:9]
    gate_ref, term_ref = refs[9:11]
    kept = []
    for g in range(groups):
        seats = Seats(meta_ref[g], first_expert(count), count, tri_ref[...], eye_ref[...])
        kept.append(seats)
        per = seats.per
        mine = slice(l * per, (l + 1) * per)
        one, two = seats.gates(dot(x_ref[g], router_ref[...]))
        lane = counted((seats.slots, 8), 1)
        gates_ref[g] = jnp.where(lane == 0, one, jnp.where(lane == 1, two, 0.0))
        (gate,) = seats.seat_values([(one, two)], [])
        take = seats.take[mine]
        valid = meta_ref[g][2:3] > 0.0
        here = slice(g * per, (g + 1) * per)
        rows_ref[here] = dot(take, x_ref[g]).astype(BF16)
        cot_rows_ref[here] = dot(jnp.where(valid, take, 0.0).astype(BF16), cot_ref[g]).astype(BF16)
        gate_ref[here] = jnp.broadcast_to(gate[mine], (per, LANES))
    wide = wd_ref.shape[1]
    rows, cot_rows, gate = rows_ref[...], cot_rows_ref[...], gate_ref[...][:, 0:1]
    gate_part = dot(rows, wg_ref[...])
    up_part = dot(rows, wu_ref[...])
    grad_plain = dot_nt(cot_rows, wd_ref[0])
    sigmoid = 1.0 / (1.0 + jnp.exp(-gate_part))
    silu = gate_part * sigmoid
    active = silu * up_part
    gated = active * gate
    front = gated
    for off in turns:
        front = jnp.where(offset_ref[0] == off, pltpu.roll(gated, wide - off, 1), front)
    active_ref[...] = front.astype(BF16)
    gated = gated.astype(BF16)
    term = jnp.sum(active * grad_plain, axis=1, keepdims=True)
    term_ref[...] = jnp.broadcast_to(term, term_ref.shape)
    grad_active = grad_plain * gate
    grad_up = (grad_active * silu).astype(BF16)
    grad_gate = (
        grad_active * up_part * sigmoid * (1.0 + gate_part * (1.0 - sigmoid))
    ).astype(BF16)
    grad_gate_ref[...], grad_up_ref[...] = grad_gate, grad_up
    out = dot(gated, wd_ref[0]).astype(BF16)
    back = (dot_nt(grad_gate, wg_ref[...]) + dot_nt(grad_up, wu_ref[...])).astype(BF16)
    if last:
        out_ref, dx_ref = refs[11:]
        for g in range(groups):
            here = slice(g * per, (g + 1) * per)
            for e in range(l):
                out_ref[g, e * per : (e + 1) * per] = before[2 * e][here]
                dx_ref[g, e * per : (e + 1) * per] = before[2 * e + 1][here]
            out_ref[g, mine] = out[here]
            dx_ref[g, mine] = back[here]
        for g in range(groups):
            part_ref[g] = dot(kept[g].put, out_ref[g]).astype(BF16)
            back_ref[g] = dot(kept[g].put, dx_ref[g]).astype(BF16)
    else:
        part_ref[...], back_ref[...] = out, back
    for g in range(groups):
        value = term_ref[g * per : (g + 1) * per][:, 0:1]
        parts = [value if e == l else jnp.zeros_like(value) for e in range(count)]
        value = parts[0] if count == 1 else jnp.concatenate(parts, axis=0)
        terms_ref[g] = kept[g].slot_values(value)
    riders.alight()


def whole_block(array):
    return pl.BlockSpec(array.shape, lambda i: (0,) * array.ndim)


def step_block(shape, first=1):
    return pl.BlockSpec((first,) + tuple(shape[1:]), lambda i: (i,) + (0,) * (len(shape) - 1))


SMEM = pl.BlockSpec(memory_space=pltpu.SMEM)


def constants(slots):
    at = np.arange(slots)
    earlier = (at[:, None] < at[None, :]) & (at[:, None] // TOK_MB == at[None, :] // TOK_MB)
    return jnp.asarray(earlier, BF16), jnp.asarray(np.eye(slots), BF16)


def mixer_tables(slots):
    frequency = 10000.0 ** (-(jnp.arange(HD // 2, dtype=F32) * (2.0 / HD)))
    angles = jnp.arange(slots, dtype=F32)[:, None] * frequency
    cosine, sine = jnp.cos(angles), jnp.sin(angles)
    table = jnp.concatenate([cosine, cosine, -sine, sine], axis=1)
    upper = lax.reduce_precision(table, 8, 7)
    return upper.astype(BF16), (table - upper).astype(BF16)


def mixer_forward(x, meta, lengths, gain, router, wq, wkv, wo, fixed, riders, collective_id):
    seqs, slots, _ = x.shape
    riders.steps = seqs
    count, hc = len(wq), wq[0].shape[1]
    seats = slots // TOK_MB * CAP * count
    per = seats // count

    def by_expert(width):
        shape = (count, seqs * per, width)
        return shape, BF16, pl.BlockSpec((count, per, width), lambda i: (0, i, 0))

    def by_row(rows, width, dtype=BF16):
        shape = (seqs, rows, width)
        return shape, dtype, step_block(shape)

    outs = [
        by_row(slots, D), by_row(slots, D), by_expert(D), by_row(slots, hc), by_row(slots, hc),
        by_row(seats, hc), by_row(seats, hc, F32), by_expert(hc), by_row(seats, 8, F32), by_row(slots, 8, F32),
    ]
    fixed_in = [gain, router, *wq, wkv, wo, *fixed]
    return pl.pallas_call(
        functools.partial(mixer_forward_kernel, count, riders),
        grid=(seqs,),
        out_shape=[jax.ShapeDtypeStruct(shape, dtype) for shape, dtype, _ in outs]
        + riders.out_shapes,
        in_specs=[SMEM, step_block(x.shape), step_block(meta.shape)]
        + [whole_block(a) for a in fixed_in]
        + riders.ins_specs,
        out_specs=[spec for _, _, spec in outs] + riders.out_specs,
        scratch_shapes=riders.scratch,
        compiler_params=pltpu.CompilerParams(**riders.params(collective_id)),
    )(lengths, x, meta, *fixed_in, *riders.ins)


def mixer_backward(
    grad, meta, lengths, wq, wkv, wo, fixed, saved, riders, collective_id
):
    seqs, slots, _ = grad.shape
    riders.steps = seqs
    count, hc = len(wq), wq[0].shape[1]
    seats = slots // TOK_MB * CAP * count
    per = seats // count

    def by_expert(width):
        shape = (count, seqs * per, width)
        return shape, BF16, pl.BlockSpec((count, per, width), lambda i: (0, i, 0))

    def by_row(rows, width, dtype=BF16):
        shape = (seqs, rows, width)
        return shape, dtype, step_block(shape)

    outs = [
        by_row(slots, D), by_expert(D), by_row(slots, 8, F32), by_expert(hc), by_row(slots, 2 * hc)
    ]
    fixed_in = [*wq, wkv, wo, *fixed]
    return pl.pallas_call(
        functools.partial(mixer_backward_kernel, count, riders),
        grid=(seqs,),
        out_shape=[jax.ShapeDtypeStruct(shape, dtype) for shape, dtype, _ in outs]
        + riders.out_shapes,
        in_specs=[SMEM, step_block(grad.shape), step_block(meta.shape)]
        + [whole_block(a) for a in fixed_in]
        + [step_block(a.shape) for a in saved]
        + riders.ins_specs,
        out_specs=[spec for _, _, spec in outs] + riders.out_specs,
        scratch_shapes=riders.scratch,
        compiler_params=pltpu.CompilerParams(**riders.params(collective_id)),
    )(lengths, grad, meta, *fixed_in, *saved, *riders.ins)


def feed(x, cot, meta, router, wg, wu, wd, fixed, offset, offsets, l, count, before, riders, collective_id):
    groups, slots, _ = x.shape
    _, wide, _ = wd.shape
    per = slots // TOK_MB * CAP
    last = l == count - 1
    at_once = 2 if last else 4
    riders.steps = groups // at_once
    seats = groups * per

    def of_rows(width):
        return ((seats, width), BF16), pl.BlockSpec((at_once * per, width), lambda i: (i, 0))

    def of_slots(width, dtype):
        return ((groups, slots, width), dtype), step_block((groups, slots, width), at_once)

    outs = [of_slots(D, BF16) if last else of_rows(D)] * 2
    outs += [of_rows(width) for width in (D, D, wide, wide, wide)] + [of_slots(8, F32)] * 2
    fixed_in = [router, wg, wu, wd, *fixed]
    turns = sorted({o for o in offsets if o})
    scratch = [pltpu.VMEM((at_once * per, LANES), F32)] * 2
    if last:
        scratch += [pltpu.VMEM((at_once, count * per, D), BF16)] * 2
    return pl.pallas_call(
        functools.partial(feed_kernel, count, l, last, at_once, turns, riders),
        grid=(groups // at_once,),
        out_shape=[jax.ShapeDtypeStruct(*shape) for shape, _ in outs] + riders.out_shapes,
        in_specs=[SMEM]
        + [step_block(a.shape, at_once) for a in (x, cot, meta)]
        + [
            pl.BlockSpec((1, wide, D), lambda i: (l, 0, 0), pipeline_mode=pl.Buffered(1))
            if a is wd
            else pl.BlockSpec(a.shape, lambda i, n=a.ndim: (0,) * n, pipeline_mode=pl.Buffered(1))
            for a in fixed_in
        ]
        + [of_rows(D)[1]] * len(before)
        + riders.ins_specs,
        out_specs=[spec for _, spec in outs] + riders.out_specs,
        scratch_shapes=scratch + riders.scratch,
        compiler_params=pltpu.CompilerParams(**riders.params(collective_id)),
    )(offset.reshape(1), x, cot, meta, *fixed_in, *before, *riders.ins)


def rejoin_kernel(*refs):
    *parts, key_value, query_out, key_value_out = refs
    for l, part in enumerate(parts):
        n_dp, _, hc = part.shape
        for d in range(n_dp):
            query_out[l, :, d * hc : (d + 1) * hc] = part[d].astype(F32)
    for d in range(n_dp):
        for half in range(2):
            at = (half * n_dp + d) * hc
            key_value_out[:, at : at + hc] = key_value[d, :, half * hc : (half + 1) * hc].astype(F32)


def rejoin(parts, key_value):
    n_dp, depth, hc = parts[0].shape
    rows = key_value.shape[1]
    return pl.pallas_call(
        rejoin_kernel,
        out_shape=[
            jax.ShapeDtypeStruct((len(parts), depth, n_dp * hc), F32),
            jax.ShapeDtypeStruct((rows, 2 * n_dp * hc), F32),
        ],
        compiler_params=pltpu.CompilerParams(vmem_limit_bytes=48 * 2**20),
    )(*parts, key_value)


def norm_forward(values, norm_gain):
    inverse = lax.rsqrt(jnp.mean(values * values, axis=-1, keepdims=True) + EPSILON)
    return (values * inverse * norm_gain, inverse)


def norm_backward(values, inverse, norm_gain, grad_normed):
    scaled = grad_normed * norm_gain
    grad_gain = jnp.sum(grad_normed * values * inverse, axis=(0, 1))
    grad_values = inverse * scaled - values * inverse**3 * jnp.mean(
        scaled * values, axis=-1, keepdims=True
    )
    return (grad_values, grad_gain)


def gate_grads(gate_probs, grad_gate_probs, routes):
    weighted = jnp.sum(gate_probs * grad_gate_probs, axis=-1, keepdims=True)
    grad_picked = gate_probs * (grad_gate_probs - weighted)
    choose = (routes[..., None] == jnp.arange(NEXP, dtype=jnp.int32)).astype(F32)
    return jnp.sum(grad_picked[..., None] * choose, axis=-2)


def tile_starts(shards):
    share = FF // shards
    most = max(share * d % LANES for d in range(shards))
    tiles = -(-(share + most) // LANES)
    starts = [min(share * d // LANES, FF // LANES - tiles) for d in range(shards)]
    return tiles, starts, [share * d - LANES * starts[d] for d in range(shards)]


def put_together_kernel(count, starts, tiles, *refs):
    out_ref = refs[-1]
    edges = sorted(set(starts) | {s + tiles for s in starts})
    for l in range(count):
        for g in range(2):
            part = refs[l * 2 + g]
            for low, high in zip(edges[:-1], edges[1:]):
                cover = [d for d in range(len(starts)) if starts[d] <= low and high <= starts[d] + tiles]
                value = None
                for d in cover:
                    cut = slice((low - starts[d]) * LANES, (high - starts[d]) * LANES)
                    term = part[d, :, cut].astype(F32)
                    value = term if value is None else value + term
                out_ref[l, :, g * FF + low * LANES : g * FF + high * LANES] = value


def put_together(parts, count, starts, tiles):
    n_dp, depth, wide = parts[0].shape
    rows = 32
    return pl.pallas_call(
        functools.partial(put_together_kernel, count, starts, tiles),
        grid=(depth // rows,),
        out_shape=jax.ShapeDtypeStruct((count, depth, 2 * FF), F32),
        in_specs=[pl.BlockSpec((n_dp, rows, wide), lambda i: (0, i, 0))] * len(parts),
        out_specs=pl.BlockSpec((count, rows, 2 * FF), lambda i: (0, i, 0)),
        compiler_params=pltpu.CompilerParams(vmem_limit_bytes=48 * 2**20),
    )(*parts)


def product(pattern, operand, factor):
    return jnp.einsum(pattern, operand, factor, preferred_element_type=F32)


def shards(
    tokens, lengths, attention_routes, feedforward_routes, norm_gains, router_weight,
    key_value_weight, query_weight, output_weight, input_weight, down_weight, cotangent,
):
    n_dp = lax.axis_size("dp")
    owners = lax.axis_size("expert")
    chips = n_dp // 2
    devices = n_dp * owners
    dp = lax.axis_index("dp")
    ex = lax.axis_index("expert")
    me = dp * owners + ex
    mb = tokens.shape[0]
    count = NEXP // owners
    seqs = mb * n_dp
    slots = owners * TOK_MB
    hc = KVH // n_dp * HD
    att = KVH * HD
    depth = D // n_dp
    slice_rows = D // devices
    tiles, starts, offsets = tile_starts(n_dp)
    share, wide = FF // n_dp, tiles * LANES
    offset = jnp.array(offsets, jnp.int32)[dp]

    def query_job(l):
        return Job(
            query_weight,
            jax.ShapeDtypeStruct((D, hc), BF16),
            lambda src, d: src.at[l, :, pl.ds(pl.multiple_of(d * hc, LANES), hc)],
            lambda out, d: out.at[pl.ds(pl.multiple_of(d * depth, depth), depth)],
        )

    key_value_job = Job(
        jnp.swapaxes(key_value_weight.reshape(slice_rows, 2, att), 0, 1),
        jax.ShapeDtypeStruct((n_dp, owners, 2, slice_rows, hc), BF16),
        lambda src, d: src.at[:, :, pl.ds(pl.multiple_of(d * hc, LANES), hc)],
        lambda out, d: out.at[d, lax.axis_index("expert")],
    )

    def start_of(d):
        start = (share * d) // LANES
        if max(share * i // LANES - starts[i] for i in range(n_dp)):
            start = jnp.minimum(start, FF // LANES - tiles)
        return start

    def input_job(l, g):
        return Job(
            input_weight,
            jax.ShapeDtypeStruct((D, wide), BF16),
            lambda src, d: src.at[
                l, :, pl.ds(pl.multiple_of(g * FF + start_of(d) * LANES, LANES), wide)
            ],
            lambda out, d: out.at[pl.ds(pl.multiple_of(d * depth, depth), depth)],
        )

    def back_job(grad, columns):
        return Job(
            grad,
            jax.ShapeDtypeStruct((n_dp, depth, columns), BF16),
            lambda src, d: src.at[pl.ds(pl.multiple_of(d * depth, depth), depth)],
            lambda out, d: out.at[d],
        )

    input_jobs = [[input_job(l, g) for g in range(2)] for l in range(count)]
    down_full = lax.dynamic_update_slice(
        jnp.zeros((count, wide, D), BF16), down_weight, (0, offset, 0)
    )

    def route_lines(routes):
        return jnp.swapaxes(routes[:, 0], 1, 2).reshape(-1, LANES).astype(F32)

    shared = jnp.concatenate([norm_gains, router_weight], axis=1).astype(F32)
    tail = jnp.concatenate([shared.reshape(-1), lengths.reshape(-1).astype(F32)])
    tail = jnp.pad(tail, (0, -tail.shape[0] % LANES)).reshape(-1, LANES)
    small = jnp.concatenate(
        [route_lines(attention_routes), route_lines(feedforward_routes), tail]
    )
    small = jnp.pad(small, ((0, -small.shape[0] % 8), (0, 0)))[None]
    tokens_all, small, *resharded = gather_all(
        [tokens.reshape(mb, TOK_MB, D)], [True], chips, owners, 1,
        [key_value_job] + [query_job(l) for l in range(count)], [small],
    )
    tokens_all = tokens_all.reshape(seqs, slots, D)
    query_full = resharded[1:]
    key_value_full = jnp.transpose(resharded[0], (0, 1, 3, 2, 4)).reshape(D, 2 * hc)
    group_slots = mb * TOK_MB * 2
    groups = devices // 2
    lines = mb * 2 * TOK_MB // LANES
    mixer_routes = small[:, :lines].reshape(n_dp, owners, mb, 2, TOK_MB)
    mixer_meta = jnp.transpose(mixer_routes, (2, 0, 3, 1, 4)).reshape(seqs, 2, slots)
    mixer_meta = jnp.pad(mixer_meta, ((0, 0), (0, 6), (0, 0)))
    feed_routes = small[:, lines : 2 * lines].reshape(groups, 2, mb, 2, TOK_MB)
    feed_meta = jnp.transpose(feed_routes, (0, 3, 1, 2, 4)).reshape(groups, 2, group_slots)
    tail = small[:, 2 * lines :].reshape(devices, -1)
    shared_all = tail[:, : slice_rows * 18].reshape(D, 18)
    all_lengths = tail[:, slice_rows * 18 : slice_rows * 18 + mb].reshape(n_dp, owners, mb)
    row_lengths = all_lengths[:, 0].T.reshape(seqs).astype(jnp.int32)
    places = (jnp.arange(owners)[:, None, None] * TOK_MB + jnp.arange(TOK_MB)).astype(F32)
    valid = (places[None] < all_lengths[..., None]).astype(F32).reshape(groups, 1, group_slots)
    feed_meta = jnp.concatenate([feed_meta, valid], axis=1)
    feed_meta = jnp.pad(feed_meta, ((0, 0), (0, 5), (0, 0)))
    gain_mixer, gain_feed = shared_all[:, 0], shared_all[:, 1]
    router_mixer, router_feed = shared_all[:, 2 : 2 + NEXP], shared_all[:, 2 + NEXP :]

    def routers(part):
        return jnp.pad(part.astype(BF16), ((0, 0), (0, LANES - NEXP)))

    own_tokens = tokens[:, 0].astype(F32)
    home_places = ex * TOK_MB + jnp.arange(TOK_MB, dtype=jnp.int32)
    own_valid = (home_places[None, :] < lengths[:, :1]).astype(F32)
    own_cotangent = cotangent[:, 0].astype(F32) * own_valid[..., None]

    normed_mixer, inverse_mixer = norm_forward(own_tokens, gain_mixer)
    fixed = constants(slots)
    tables = mixer_tables(slots)
    (
        mixer_all, mixer_part, rows_mixer, keys, values, queries, mixture, mixture_gated, info,
        gates_mixer, cot_all, *input_parts,
    ) = mixer_forward(
        tokens_all, mixer_meta, row_lengths, gain_mixer[None], routers(router_mixer), query_full,
        key_value_full, output_weight, (*fixed, *tables),
        Riders(chips, owners, input_jobs[0][:1], gather=(cotangent.reshape(mb, TOK_MB, D), False)), 2,
    )
    cot_all = cot_all.reshape(groups, group_slots, D)
    mixer_sum, *more_parts = scatter_sum(
        mixer_part.reshape(mb, devices, TOK_MB, D), chips, owners, True, 10, input_jobs[0][1:]
    )
    input_parts += more_parts

    second = own_tokens + mixer_sum
    normed_feed, inverse_feed = norm_forward(second, gain_feed)
    feed_all, *more_parts = gather_all(
        [normed_feed.astype(BF16)], [False], chips, owners, 3,
        input_jobs[1][:1] if count > 1 else [],
    )
    input_parts += more_parts
    feed_all = feed_all.reshape(groups, group_slots, D)
    feed_fixed = constants(group_slots)
    before, back_jobs, works, actives, cots, gate_terms_feed = [], [], [], [], [], 0.0
    for l in range(count):
        carried = [job for jobs in input_jobs[l + 1 : l + 2] for job in jobs[l == 0 :]]
        carried += back_jobs[:1]
        (
            feed_part, grad_feed_part, rows_feed, cot_rows, active_gated, grad_gate, grad_up,
            terms, gates_feed, *more_parts,
        ) = feed(
            feed_all, cot_all, feed_meta, routers(router_feed), input_parts[2 * l], input_parts[2 * l + 1],
            down_full, feed_fixed, offset, offsets, l, count, before, Riders(chips, owners, carried),
            60 + l,
        )
        before += [feed_part, grad_feed_part]
        grad_input_parts = more_parts[len(carried) - len(back_jobs[:1]) :]
        input_parts += more_parts[: len(carried) - len(back_jobs[:1])]
        works += [Work(rows_feed, grad, BF16) for grad in (grad_gate, grad_up)]
        if l < count - 1:
            first_grad = product("rd,rf->df", rows_feed, grad_gate).astype(BF16)
            back_jobs.append(back_job(first_grad, wide))
            works.pop(-2)
        actives.append(active_gated[:, :share])
        cots.append(cot_rows)
        gate_terms_feed = gate_terms_feed + terms

    def home_parts(terms, by_row):
        terms = terms[..., :2]
        if by_row:
            terms = jnp.swapaxes(terms.reshape(mb, devices, TOK_MB * 2), 0, 1)
        terms = terms.reshape(devices, -1, LANES)
        return jnp.pad(terms, ((0, 0), (0, -terms.shape[1] % 8), (0, 0)))

    def at_home(parts):
        return jnp.sum(parts, axis=0).reshape(-1)[: mb * TOK_MB * 2].reshape(mb, TOK_MB, 2)

    def own_of(gates, by_row):
        gates = gates[..., :2]
        if by_row:
            return lax.dynamic_index_in_dim(
                gates.reshape(mb, devices, TOK_MB, 2), me, 1, keepdims=False
            )
        return lax.dynamic_index_in_dim(
            gates.reshape(devices, mb, TOK_MB, 2), me, 0, keepdims=False
        )

    grad_normed_feed, first_part, terms, _, *later = scatter_sum(
        grad_feed_part.reshape(devices, mb, TOK_MB, D), chips, owners, False, 20,
        [back_job(0, wide)], [home_parts(gate_terms_feed, False)], works,
    )
    grad_input_parts.append(first_part)
    later = [back_job(grad, wide) for grad in later]
    grad_logits_feed = gate_grads(
        own_of(gates_feed, False), at_home(terms), feedforward_routes[:, 0]
    )
    grad_normed_feed = grad_normed_feed + product("mte,de->mtd", grad_logits_feed, router_feed)
    grad_second, grad_gain_feed = norm_backward(second, inverse_feed, gain_feed, grad_normed_feed)
    grad_second = grad_second + own_cotangent

    grad_all, *more_parts = gather_all(
        [grad_second.astype(BF16)], [True], chips, owners, 5, later[:1]
    )
    grad_down = product("lrf,lrd->lfd", jnp.stack(actives), jnp.stack(cots))
    grad_input_parts += more_parts[:1]
    grad_all = grad_all.reshape(seqs, slots, D)
    feed_part = feed_part.reshape(devices, mb, TOK_MB, D)
    beside = scatter_parts(chips, owners, TOK_MB, D) == 1
    (
        grad_mixer_part, grad_rows, gate_terms_mixer, grad_query_pre, grad_key_value, *more_parts
    ) = mixer_backward(
        grad_all, mixer_meta, row_lengths, query_full, key_value_full, output_weight,
        (*fixed, *tables), (keys, values, queries, mixture, info),
        Riders(chips, owners, later[1:], scatter=(feed_part, False) if beside else None), 6,
    )
    if not beside:
        more_parts = scatter_sum(feed_part, chips, owners, False, 30) + more_parts
    feed_sum, *more_parts = more_parts
    grad_input_parts += more_parts
    result = (second + feed_sum).astype(BF16)[:, None]
    grad_normed_mixer, *more_parts = scatter_sum(
        grad_mixer_part.reshape(mb, devices, TOK_MB, D), chips, owners, True, 40,
        [back_job(l, hc) for l in range(count)],
        [home_parts(gate_terms_mixer, True)],
        [Work(rows_mixer, grad_query_pre, BF16, l=l) for l in range(count)]
        + [
            Work(mixer_all.reshape(seqs * slots, D), grad_key_value.reshape(seqs * slots, 2 * hc), BF16)
        ]
        + [
            Work(mixture_gated, grad_rows, F32, l=l, keep=hc, slot=(l, count)) for l in range(count)
        ],
        fold=count,
    )
    query_parts, terms = more_parts[:count], more_parts[count]
    grad_output = more_parts[-2]
    grad_key_value_w = more_parts[-1]
    grad_query, grad_key_value_w = rejoin(query_parts, grad_key_value_w)
    grad_logits_mixer = gate_grads(
        own_of(gates_mixer, True), at_home(terms), attention_routes[:, 0]
    )
    grad_normed_mixer = grad_normed_mixer + product("mte,de->mtd", grad_logits_mixer, router_mixer)
    grad_tokens, grad_gain_mixer = norm_backward(
        own_tokens, inverse_mixer, gain_mixer, grad_normed_mixer
    )
    grad_tokens = (grad_tokens + grad_second).astype(BF16)[:, None]

    router_terms = [
        product("mtd,mte->de", normed.astype(BF16), logits.astype(BF16))
        for normed, logits in ((normed_mixer, grad_logits_mixer), (normed_feed, grad_logits_feed))
    ]
    last = jnp.concatenate([grad_gain_mixer[:, None], grad_gain_feed[:, None], *router_terms], axis=1)
    last = last.reshape(devices, slice_rows * 18)
    last = jnp.pad(last, ((0, 0), (0, -last.shape[1] % (8 * LANES)))).reshape(devices, -1, LANES)
    last = jnp.sum(exchange(last, chips, owners, 8), axis=0).reshape(-1)
    last = last[: slice_rows * 18].reshape(slice_rows, 18)
    grad_gains, grad_router = last[:, :2], last[:, 2:]

    grad_input = put_together(grad_input_parts, count, starts, tiles)
    return (
        result, grad_tokens, grad_gains, grad_router, grad_key_value_w, grad_query,
        grad_output, grad_input, grad_down,
    )


def solution(mesh):
    shared = P(("dp", "expert"), None)
    slots = P(None, "dp", "expert", None)
    owned = P("expert", "dp", None)
    return jax.shard_map(
        shards,
        mesh=mesh,
        in_specs=(slots, P(None, "dp"), slots, slots, shared, shared, shared) + (owned,) * 4 + (slots,),
        out_specs=(slots, slots, shared, shared, shared) + (owned,) * 4,
        check_vma=False,
    )
```

```python
import functools

import jax
import jax.numpy as jnp
import numpy as np
from jax import lax
from jax.experimental import pallas as pl
from jax.experimental.pallas import tpu as pltpu
from jax.sharding import PartitionSpec as P

MESH = pl.DeviceIdType.MESH
BF16 = jnp.bfloat16
F32 = jnp.float32
ANY = pl.BlockSpec(memory_space=pl.ANY)


def expert_factors(owners):
    return (2, owners // 2) if owners % 2 == 0 and owners > 2 else (1, owners)


class Place:
    def __init__(self, chips, first, second):
        dp = lax.axis_index("dp")
        ex = lax.axis_index("expert")
        self.chips, self.first, self.second = chips, first, second
        self.owners, self.n_dp = first * second, chips * 2
        self.dp, self.ex = dp, ex
        self.z, self.k = dp // 2, dp % 2
        self.a, self.b = ex // second, ex % second

    def at(self, z=None, k=None, a=None, b=None):
        z = self.z if z is None else z
        k = self.k if k is None else k
        a = self.a if a is None else a
        b = self.b if b is None else b
        return (z * 2 + k, a * self.second + b)

    def other(self, i):
        number = (self.dp * self.owners + self.ex + i) % (self.n_dp * self.owners)
        return number, (number // self.owners, number % self.owners)

    def greet(self, reach):
        barrier = pltpu.get_barrier_semaphore()

        def hello(target):
            pl.semaphore_signal(barrier, inc=1, device_id=target, device_id_type=MESH)

        if reach == "all":
            count = self.n_dp * self.owners - 1

            def one(i, carried):
                hello(self.other(i)[1])
                return carried

            lax.fori_loop(1, count + 1, one, 0)
            pl.semaphore_wait(barrier, count)
            return
        if reach in ("column", "dp"):
            for i in range(1, self.n_dp):
                hello(((self.dp + i) % self.n_dp, self.ex))
        if reach == "column":
            pl.semaphore_wait(barrier, self.n_dp - 1)
            return
        for i in range(1, self.first):
            hello(self.at(a=(self.a + i) % self.first))
        for i in range(1, self.second):
            hello(self.at(b=(self.b + i) % self.second))
        if reach == "dp":
            pl.semaphore_wait(barrier, self.first + self.second + self.n_dp - 3)
            return
        hello(self.at(k=1 - self.k))
        pl.when(self.z > 0)(lambda: hello(self.at(z=self.z - 1)))
        pl.when(self.z < self.chips - 1)(lambda: hello(self.at(z=self.z + 1)))
        along = (self.z > 0).astype(jnp.int32) + (self.z < self.chips - 1).astype(jnp.int32)
        pl.semaphore_wait(barrier, self.first + self.second - 1 + along)


def remote(src, dst, send, recv, target):
    return pltpu.make_async_remote_copy(
        src_ref=src, dst_ref=dst, send_sem=send, recv_sem=recv, device_id=target, device_id_type=MESH
    )


class Job:
    def __init__(self, src, out_shape, pick, put):
        self.src, self.out_shape, self.pick, self.put = src, out_shape, pick, put


class Load:
    def __init__(self, jobs, me, srcs, outs, sems):
        self.jobs, self.me, self.srcs, self.outs = jobs, me, srcs, outs
        self.own, self.send, self.recv = sems if jobs else (None,) * 3

    def peers(self):
        return [(i, (self.me.dp + i) % self.me.n_dp) for i in range(1, self.me.n_dp)]

    def copy(self, j, i, d):
        me, job = self.me, self.jobs[j]
        return remote(
            job.pick(self.srcs[j], d), job.put(self.outs[j], me.dp),
            self.send.at[j, i], self.recv.at[j, me.dp], (d, me.ex),
        )

    def stay(self, j):
        job, dp = self.jobs[j], self.me.dp
        return pltpu.make_async_copy(
            job.pick(self.srcs[j], dp), job.put(self.outs[j], dp), self.own.at[j]
        )

    def start(self, chosen=None):
        for j in range(len(self.jobs)) if chosen is None else chosen:
            for i, d in self.peers():
                self.copy(j, i, d).start()
            self.stay(j).start()

    def landed(self, j):
        self.stay(j).wait()
        for i, d in self.peers():
            dst = self.jobs[j].put(self.outs[j], d)
            remote(dst, dst, self.send.at[j, i], self.recv.at[j, d], (d, self.me.ex)).wait_recv()

    def finish(self, skip=()):
        for j in range(len(self.jobs)):
            if j not in skip:
                self.landed(j)
            for i, d in self.peers():
                self.copy(j, i, d).wait_send()

    @staticmethod
    def scratch(jobs, n_dp):
        if not jobs:
            return []
        sem = pltpu.SemaphoreType.DMA
        return [sem((len(jobs),)), sem((len(jobs), n_dp)), sem((len(jobs), n_dp))]


class Work:
    def __init__(self, a, b, dtype, l=None, keep=None, slot=None):
        self.ins, self.l, self.keep, self.slot = (a, b), l, keep, slot
        (self.k, self.m), self.n = a.shape[-2:], b.shape[-1]
        shape = (keep or self.m, self.n)
        self.shape = jax.ShapeDtypeStruct(shape if slot is None else (slot[1],) + shape, dtype)

    def run(self, a_ref, b_ref, out_ref):
        if self.l is not None:
            a_ref = a_ref.at[self.l] if len(a_ref.shape) == 3 else a_ref
            b_ref = b_ref.at[self.l] if len(b_ref.shape) == 3 else b_ref
        k, m, n, keep = self.k, self.m, self.n, self.keep

        def body(a, b, out):
            value = lax.dot_general(
                a[...], b[...], (((0,), (0,)), ((), ())), preferred_element_type=F32
            )
            out[...] = value[: out.shape[0]].astype(out.dtype)

        if keep is None:
            blk = 256 if k <= 8192 else 128
            specs = [pl.BlockSpec((k, blk), lambda i: (0, i)), pl.BlockSpec((k, n), lambda i: (0, 0))]
            out = pl.BlockSpec((blk, n), lambda i: (i, 0))
            grid = m // blk
        else:
            blk = 512
            specs = [pl.BlockSpec((k, m), lambda i: (0, 0)), pl.BlockSpec((k, blk), lambda i: (0, i))]
            out = pl.BlockSpec((keep, blk), lambda i: (0, i))
            grid = n // blk
        pltpu.emit_pipeline(body, grid=(grid,), in_specs=specs, out_specs=[out])(
            a_ref, b_ref, out_ref
        )


class Works:
    def __init__(self, works, ins, outs):
        self.works, self.ins, self.outs = works, ins, outs

    def run(self, i):
        if i < len(self.works):
            slot = self.works[i].slot
            out = self.outs[i] if slot is None else self.outs[i - slot[0]].at[slot[0]]
            self.works[i].run(*self.ins[2 * i : 2 * i + 2], out)

    @staticmethod
    def shapes(works):
        return [work.shape for work in works if work.slot is None or work.slot[0] == 0]

    @staticmethod
    def taken(works, refs):
        return [
            refs.pop(0) if work.slot is None or work.slot[0] == 0 else None for work in works
        ]

    @staticmethod
    def arrays(works):
        return [a for work in works for a in work.ins]


class Fold:
    def __init__(self, me, x_ref, out_ref, refs):
        self.me, self.x_ref, self.out_ref = me, x_ref, out_ref
        self.here, self.got, self.sem, self.send, self.recv, self.send_dp, self.recv_dp = refs

    @staticmethod
    def scratch(n_dp, owners, rows, columns):
        sem = pltpu.SemaphoreType.DMA
        return [
            pltpu.VMEM((n_dp, rows, columns), BF16),
            pltpu.VMEM((max(owners - 1, 1), n_dp, rows, columns), BF16),
            sem((2,)), sem((owners,)), sem((owners,)), sem((n_dp,)), sem((n_dp,)),
        ]

    def first(self, i):
        me = self.me
        e = (me.ex + i) % me.owners
        slot = me.owners - 1 - i
        return remote(
            self.x_ref.at[:, e], self.got.at[slot], self.send.at[i], self.recv.at[slot], (me.dp, e)
        )

    def second(self, i):
        me = self.me
        d = (me.dp + i) % me.n_dp
        return remote(
            self.here.at[d], self.out_ref.at[me.dp], self.send_dp.at[i], self.recv_dp.at[me.dp],
            (d, me.ex),
        )

    def load(self):
        return pltpu.make_async_copy(self.x_ref.at[:, self.me.ex], self.here, self.sem.at[0])

    def stay(self):
        dp = self.me.dp
        return pltpu.make_async_copy(self.here.at[dp], self.out_ref.at[dp], self.sem.at[1])

    def begin(self):
        self.load().start()
        for i in range(1, self.me.owners):
            self.first(i).start()

    def turn(self):
        self.load().wait()
        total = self.here[...].astype(F32)
        for slot in range(self.me.owners - 1):
            there = self.got.at[slot]
            remote(
                there, there, self.send.at[0], self.recv.at[slot], (self.me.dp, self.me.ex)
            ).wait_recv()
            total = total + self.got[slot].astype(F32)
        self.here[...] = total.astype(BF16)
        self.stay().start()
        for i in range(1, self.me.n_dp):
            self.second(i).start()

    def finish(self):
        me = self.me
        self.stay().wait()
        for i in range(1, me.owners):
            self.first(i).wait_send()
        for i in range(1, me.n_dp):
            d = (me.dp + i) % me.n_dp
            there = self.out_ref.at[d]
            remote(there, there, self.send_dp.at[i], self.recv_dp.at[d], (d, me.ex)).wait_recv()
            self.second(i).wait_send()


class Mail:
    def __init__(self, arrays, me, srcs, outs, sems):
        self.arrays, self.me, self.srcs, self.outs = arrays, me, srcs, outs
        self.devices = me.n_dp * me.owners
        self.number = me.dp * me.owners + me.ex
        self.own, self.send, self.recv = sems if arrays else (None,) * 3

    def part(self, j, n):
        return self.srcs[j].at[0 if self.arrays[j].shape[0] == 1 else n]

    def copy(self, j, i):
        n, where = self.me.other(i)
        return remote(
            self.part(j, n), self.outs[j].at[self.number], self.send.at[j, i],
            self.recv.at[j, self.number], where,
        )

    def stay(self, j):
        return pltpu.make_async_copy(
            self.part(j, self.number), self.outs[j].at[self.number], self.own.at[j]
        )

    def start(self):
        for j in range(len(self.arrays)):

            def one(i, carried, j=j):
                self.copy(j, i).start()
                return carried

            self.stay(j).start()
            lax.fori_loop(1, self.devices, one, 0)

    def finish(self):
        for j in range(len(self.arrays)):

            def one(i, carried, j=j):
                n, where = self.me.other(i)
                there = self.outs[j].at[n]
                remote(there, there, self.send.at[j, i], self.recv.at[j, n], where).wait_recv()
                self.copy(j, i).wait_send()
                return carried

            self.stay(j).wait()
            lax.fori_loop(1, self.devices, one, 0)

    @staticmethod
    def scratch(arrays, devices):
        if not arrays:
            return []
        sem = pltpu.SemaphoreType.DMA
        return [sem((len(arrays),)), sem((len(arrays), devices)), sem((len(arrays), devices))]

    @staticmethod
    def shapes(arrays, devices):
        return [jax.ShapeDtypeStruct((devices,) + a.shape[1:], a.dtype) for a in arrays]


class Gather:
    def __init__(self, me, by_row, x_ref, out_ref, sems):
        self.me, self.by_row, self.x_ref, self.out_ref = me, by_row, x_ref, out_ref
        self.own_sem, self.recv, self.sends = sems
        self.pending = []
        self.own = self.index(me.z, me.a, me.b)

    @staticmethod
    def scratch(chips, first, second):
        sem = pltpu.SemaphoreType.DMA
        sends = 4 + (2 * chips - 1) * (
            2 + 2 * (first + second - 1) + 2 * (second - 1) * first + 2 * (first - 1) * second
        )
        return [sem((2,)), sem((chips * 2 * first * second, 2)), sem((sends,))]

    def index(self, z, a, b):
        return (z * 2 + self.me.k) * self.me.owners + a * self.me.second + b

    def piece(self, blk, h):
        return self.out_ref.at[h, blk] if self.by_row else self.out_ref.at[blk, h]

    def push(self, src, blk, h, target, when=None):
        copy = remote(
            src, self.piece(blk, h), self.sends.at[len(self.pending)], self.recv.at[blk, h], target
        )
        self.pending.append(when)
        copy.start() if when is None else pl.when(when())(copy.start)

    def landed(self, blk, h, when=None):
        there = self.piece(blk, h)
        copy = remote(there, there, self.sends.at[0], self.recv.at[blk, h], self.me.at())
        copy.wait_recv() if when is None else pl.when(when())(copy.wait_recv)

    def there(self, shift):
        if shift == 0:
            return None
        me = self.me
        return lambda: (me.z + shift >= 0) if shift < 0 else (me.z + shift < me.chips)

    def spread(self, blk, source, when=None):
        me = self.me
        for h in range(2):
            for i in range(1, me.second):
                self.push(source(h), blk, h, me.at(b=(me.b + i) % me.second), when)
            for i in range(1, me.first):
                self.push(source(h), blk, h, me.at(a=(me.a + i) % me.first), when)
        for h in range(2):
            self.push(source(h), blk, h, me.at(k=1 - me.k), when)

    def relay(self, shift):
        me, when = self.me, self.there(shift)
        z = me.z + shift
        for h in range(2):
            if h == 0:
                froms = [(me.a, (me.b + i) % me.second) for i in range(1, me.second)]
                onward = [dict(a=(me.a + i) % me.first) for i in range(1, me.first)]
            else:
                froms = [((me.a + i) % me.first, me.b) for i in range(1, me.first)]
                onward = [dict(b=(me.b + i) % me.second) for i in range(1, me.second)]
            for a, b in froms:
                blk = self.index(z, a, b)
                self.landed(blk, h, when)
                for target in onward:
                    self.push(self.piece(blk, h), blk, h, me.at(**target), when)
                self.push(self.piece(blk, h), blk, h, me.at(k=1 - me.k), when)

    def settle(self, shift):
        me, when = self.me, self.there(shift)
        z = me.z + shift
        for h in range(2):
            for i in range(1, me.second if h else me.first):
                for j in range(me.first if h else me.second):
                    if h == 0:
                        a, b = (me.a + i) % me.first, (me.b + j) % me.second
                    else:
                        a, b = (me.a + j) % me.first, (me.b + i) % me.second
                    blk = self.index(z, a, b)
                    self.landed(blk, h, when)
                    self.push(self.piece(blk, h), blk, h, me.at(k=1 - me.k), when)

    def stay(self, h):
        return pltpu.make_async_copy(
            self.x_ref.at[h], self.piece(self.own, h), self.own_sem.at[h]
        )

    def begin(self):
        me, x_ref, own = self.me, self.x_ref, self.own
        for h in range(2):
            self.stay(h).start()
        for h in range(2):
            self.push(x_ref.at[h], own, h, me.at(z=me.z + 1), self.there(1))
            self.push(x_ref.at[h], own, h, me.at(z=me.z - 1), self.there(-1))
        self.spread(own, lambda h: x_ref.at[h])

    def stage(self, t):
        me = self.me
        for shift in (-t, t):
            there, onward = self.there(shift), self.there(1 if shift < 0 else -1)
            blk = self.index(me.z + shift, me.a, me.b)
            for h in range(2):
                self.landed(blk, h, there)
                self.push(
                    self.piece(blk, h), blk, h, me.at(z=me.z + (1 if shift < 0 else -1)),
                    lambda there=there, onward=onward: there() & onward(),
                )
            self.spread(blk, lambda h, blk=blk: self.piece(blk, h), there)

    def drain(self, t):
        shifts = (-t, t) if t else (0,)
        for shift in shifts:
            self.relay(shift)
        for shift in shifts:
            self.settle(shift)

    def along(self):
        return [functools.partial(self.stage, t) for t in range(1, self.me.chips)]

    def across(self):
        return [functools.partial(self.drain, t) for t in range(self.me.chips)]

    def finish(self):
        me = self.me
        for h in range(2):
            self.stay(h).wait()
        for z in range(me.chips):
            for e in range(me.owners):
                for h in range(2):
                    self.landed((z * 2 + 1 - me.k) * me.owners + e, h)
        for i, when in enumerate(self.pending):
            copy = remote(
                self.x_ref.at[0], self.x_ref.at[0], self.sends.at[i], self.recv.at[0, 0], me.at()
            )
            copy.wait_send() if when is None else pl.when(when())(copy.wait_send)


def taken(refs, number):
    return [refs.pop(0) for _ in range(number)]


def gather_kernel(chips, first, second, orders, jobs, mails, works, *refs):
    me = Place(chips, first, second)
    refs = list(refs)
    x_refs = taken(refs, len(orders))
    mail_srcs = taken(refs, len(mails))
    srcs = taken(refs, len(jobs))
    work_ins = taken(refs, 2 * len(works))
    out_refs = taken(refs, len(orders))
    mail_outs = taken(refs, len(mails))
    outs = taken(refs, len(jobs))
    works = Works(works, work_ins, Works.taken(works, refs))
    gathers = [
        Gather(me, by_row, x_ref, out_ref, taken(refs, 3))
        for by_row, x_ref, out_ref in zip(orders, x_refs, out_refs)
    ]
    if mails:
        spread_send, spread_recv = taken(refs, 2)
        mail = Mail(mails, me, mail_srcs, mail_outs, taken(refs, 3))
    load = Load(jobs, me, srcs, outs, refs)
    me.greet("all" if mails else "dp" if jobs else "near")
    for gather in gathers:
        gather.begin()
    if mails:
        mail.start()
    along = [stage for stages in zip(*[gather.along() for gather in gathers]) for stage in stages]
    for i, stage in enumerate(along):
        if i == len(along) - 1:
            load.start()
        stage()
    rest = [stage for stages in zip(*[gather.across() for gather in gathers]) for stage in stages]
    for stage in rest[:2]:
        stage()
    works.run(0)
    if mails:
        j = 0
        load.landed(j)
        column = outs[j].at[:, me.ex]
        spreads = [
            remote(
                column, column, spread_send.at[i], spread_recv.at[me.ex],
                (me.dp, (me.ex + i) % me.owners),
            )
            for i in range(1, me.owners)
        ]
        for copy in spreads:
            copy.start()
    for i, stage in enumerate(rest[2:]):
        stage()
        works.run(1 + i)
    if mails:
        mail.finish()
        for i in range(1, me.owners):
            e = (me.ex + i) % me.owners
            there = outs[j].at[:, e]
            remote(there, there, spread_send.at[i], spread_recv.at[e], (me.dp, e)).wait_recv()
        for copy in spreads:
            copy.wait_send()
    for gather in gathers:
        gather.finish()
    load.finish(skip=(0,) if mails else ())


def gather_all(xs, orders, chips, owners, collective_id, jobs=(), mails=(), works=()):
    first, second = expert_factors(owners)
    blocks = chips * 2 * owners
    sem = pltpu.SemaphoreType.DMA
    shapes = []
    for x, by_row in zip(xs, orders):
        rest = x.shape[1:]
        shape = (2, blocks) + rest if by_row else (blocks, 2) + rest
        shapes.append(jax.ShapeDtypeStruct(shape, x.dtype))
    shapes += Mail.shapes(mails, blocks) + [job.out_shape for job in jobs]
    shapes += Works.shapes(works)
    ins = list(xs) + list(mails) + [job.src for job in jobs] + Works.arrays(works)
    scratch = Gather.scratch(chips, first, second) * len(xs)
    if mails:
        scratch += [sem((owners,)), sem((owners,))] + Mail.scratch(mails, blocks)
    return pl.pallas_call(
        functools.partial(
            gather_kernel, chips, first, second, orders, jobs,
            [jax.ShapeDtypeStruct(a.shape, a.dtype) for a in mails], works,
        ),
        out_shape=shapes,
        in_specs=[ANY] * len(ins),
        out_specs=[ANY] * len(shapes),
        scratch_shapes=scratch + Load.scratch(jobs, chips * 2),
        compiler_params=pltpu.CompilerParams(
            collective_id=collective_id, has_side_effects=True, vmem_limit_bytes=60 * 2**20
        ),
    )(*ins)


class Scatter:
    def __init__(self, me, by_row, column, width, p_ref, out_ref, refs):
        self.me, self.by_row, self.cut = me, by_row, pl.ds(column, width)
        self.p_ref, self.out_ref = p_ref, out_ref
        self.mine, self.fromk, self.a0, self.b0, self.b1, self.a1, self.fromz = refs[:7]
        self.load_sem, self.ks, self.a0s, self.b0s, self.b1s, self.a1s, self.zs, self.sends = refs[7:]
        self.pending = []

    @staticmethod
    def scratch(chips, first, second, half, width):
        sem, owners = pltpu.SemaphoreType.DMA, first * second
        one = max(first - 1, 1), max(second - 1, 1)
        sends = chips * (owners + 2 + 2 * (first - 1) * second + 2 * (second - 1) * first)
        return [
            pltpu.VMEM((chips, owners, 2, half, width), BF16),
            pltpu.VMEM((chips, owners, 2, half, width), BF16),
            pltpu.VMEM((chips, one[0], second, half, width), BF16),
            pltpu.VMEM((chips, one[1], half, width), BF16),
            pltpu.VMEM((chips, one[1], first, half, width), BF16),
            pltpu.VMEM((chips, one[0], half, width), BF16),
            pltpu.VMEM((chips + 1, 2, half, width), BF16),
            sem((chips, owners)),
            sem((chips, owners)),
            sem((chips, one[0], second)),
            sem((chips, one[1])),
            sem((chips, one[1], first)),
            sem((chips, one[0])),
            sem((chips + 1,)),
            sem((sends + chips * (first + second),)),
        ]

    def push(self, src, dst, sem, target, part, when=None):
        copy = remote(src, dst, self.sends.at[len(self.pending)], sem, target)
        self.pending.append((part, when))
        copy.start() if when is None else pl.when(when())(copy.start)

    def landed(self, dst, sem):
        remote(dst, dst, self.sends.at[0], sem, self.me.at()).wait_recv()

    def line(self, t):
        z, chips = self.me.z, self.me.chips
        return jnp.where(
            z < chips // 2,
            jnp.where(t < chips - 1 - z, chips - 1 - t, t - (chips - 1 - z)),
            jnp.where(t < z, t, chips - 1 - (t - z)),
        )

    def block(self, z, k, e):
        blk = (z * 2 + k) * self.me.owners + e
        if self.by_row:
            return self.p_ref.at[:, blk, :, self.cut]
        return self.p_ref.at[blk, :, :, self.cut]

    def begin(self):
        me = self.me
        for t in range(me.chips):
            z = self.line(t)
            for e in range(me.owners):
                pltpu.make_async_copy(
                    self.block(z, me.k, e), self.mine.at[t, e], self.load_sem.at[t, e]
                ).start()
                self.push(
                    self.block(z, 1 - me.k, e), self.fromk.at[t, e], self.ks.at[t, e],
                    me.at(k=1 - me.k), "block",
                )

    @staticmethod
    def add(*terms):
        value = terms[0].astype(F32)
        for term in terms[1:]:
            value = value + term.astype(F32)
        return value

    def step_one(self, t):
        me, mine = self.me, self.mine
        first, second = me.first, me.second
        for i in range(first):
            for j in range(second):
                a, b = (me.a + 1 + i) % first, (me.b + 1 + j) % second
                e = a * second + b
                pltpu.make_async_copy(mine.at[t, e], mine.at[t, e], self.load_sem.at[t, e]).wait()
                self.landed(self.fromk.at[t, e], self.ks.at[t, e])
                mine[t, e] = self.add(mine[t, e], self.fromk[t, e]).astype(BF16)
                if i < first - 1:
                    slot = first - 2 - i
                    self.push(
                        mine.at[t, e, 0], self.a0.at[t, slot, b], self.a0s.at[t, slot, b],
                        me.at(a=a), "half",
                    )
                if j < second - 1:
                    slot = second - 2 - j
                    self.push(
                        mine.at[t, e, 1], self.b1.at[t, slot, a], self.b1s.at[t, slot, a],
                        me.at(b=b), "half",
                    )

    def step_two(self, t):
        me, mine = self.me, self.mine
        first, second = me.first, me.second
        for j in range(second - 1):
            b = (me.b + 1 + j) % second
            e = me.a * second + b
            for i in range(first - 1):
                self.landed(self.a0.at[t, i, b], self.a0s.at[t, i, b])
            mine[t, e, 0] = self.add(
                mine[t, e, 0], *[self.a0[t, i, b] for i in range(first - 1)]
            ).astype(BF16)
            slot = second - 2 - j
            self.push(
                mine.at[t, e, 0], self.b0.at[t, slot], self.b0s.at[t, slot], me.at(b=b), "half"
            )
        for i in range(first - 1):
            a = (me.a + 1 + i) % first
            e = a * second + me.b
            for j in range(second - 1):
                self.landed(self.b1.at[t, j, a], self.b1s.at[t, j, a])
            mine[t, e, 1] = self.add(
                mine[t, e, 1], *[self.b1[t, j, a] for j in range(second - 1)]
            ).astype(BF16)
            slot = first - 2 - i
            self.push(
                mine.at[t, e, 1], self.a1.at[t, slot], self.a1s.at[t, slot], me.at(a=a), "half"
            )

    def step_three(self, t):
        me, mine, total, fromz, zs = self.me, self.mine, self.out_ref, self.fromz, self.zs
        first, second, chips = me.first, me.second, me.chips
        z, e = self.line(t), me.ex
        for i in range(first - 1):
            self.landed(self.a0.at[t, i, me.b], self.a0s.at[t, i, me.b])
            self.landed(self.a1.at[t, i], self.a1s.at[t, i])
        for j in range(second - 1):
            self.landed(self.b1.at[t, j, me.a], self.b1s.at[t, j, me.a])
            self.landed(self.b0.at[t, j], self.b0s.at[t, j])
        total[0] = self.add(
            mine[t, e, 0], *[self.a0[t, i, me.b] for i in range(first - 1)],
            *[self.b0[t, j] for j in range(second - 1)],
        )
        total[1] = self.add(
            mine[t, e, 1], *[self.b1[t, j, me.a] for j in range(second - 1)],
            *[self.a1[t, i] for i in range(first - 1)],
        )

        def also(when, slot):
            @pl.when(when)
            def _():
                self.landed(fromz.at[slot], zs.at[slot])
                total[...] = total[...] + fromz[slot].astype(F32)

        if t < chips - 1:
            up = z > me.z
            also(jnp.where(up, me.z > 0, me.z < chips - 1), z)
            mine[t, e] = total[...].astype(BF16)
            self.push(
                mine.at[t, e], fromz.at[z], zs.at[z], me.at(z=me.z + 1), "block",
                lambda: self.line(t) > me.z,
            )
            slot = jnp.where(z == me.z - 1, chips, z)
            self.push(
                mine.at[t, e], fromz.at[slot], zs.at[slot], me.at(z=me.z - 1), "block",
                lambda: self.line(t) < me.z,
            )
        else:
            also(me.z > 0, me.z)
            also(me.z < chips - 1, chips)

    def stage(self, t):
        if t < self.me.chips:
            self.step_one(t)
        if 0 <= t - 1 < self.me.chips:
            self.step_two(t - 1)
        if 0 <= t - 2 < self.me.chips:
            self.step_three(t - 2)

    def stages(self):
        return [functools.partial(self.stage, t) for t in range(self.me.chips + 2)]

    def finish(self):
        for i, (part, when) in enumerate(self.pending):
            ref = self.mine.at[0, 0] if part == "block" else self.mine.at[0, 0, 0]
            copy = remote(ref, ref, self.sends.at[i], self.zs.at[0], self.me.at())
            copy.wait_send() if when is None else pl.when(when())(copy.wait_send)


def scatter_parts(chips, owners, half, full):
    parts = 1
    while chips * owners * half * (full // parts) * 8 > 16 * 2**20:
        parts *= 2
    return parts


def scatter_kernel(chips, first, second, by_row, column, width, jobs, mails, works, fold, *refs):
    me = Place(chips, first, second)
    refs = list(refs)
    (p_ref,) = taken(refs, 1)
    ready = [j for j, job in enumerate(jobs) if not isinstance(job.src, int)]
    given, mail_srcs = taken(refs, len(ready)), taken(refs, len(mails))
    work_ins = taken(refs, 2 * len(works))
    (out_ref,) = taken(refs, 1)
    outs, mail_outs = taken(refs, len(jobs)), taken(refs, len(mails))
    work_outs = Works.taken(works, refs)
    folded = taken(refs, 0 if fold is None else 1)
    scatter = Scatter(me, by_row, column, width, p_ref, out_ref, taken(refs, 15))
    mail = Mail(mails, me, mail_srcs, mail_outs, taken(refs, 3) if mails else ())
    if fold is not None:
        x_ref = work_outs[fold].reshape(
            me.n_dp, me.owners, folded[0].shape[1], folded[0].shape[2]
        )
        folding = Fold(me, x_ref, folded[0], taken(refs, 7))
    srcs = [given.pop(0) if j in ready else work_outs[job.src] for j, job in enumerate(jobs)]
    load = Load(jobs, me, srcs, outs, refs)
    doing = Works(works, work_ins, work_outs)
    me.greet("all" if mails else "dp" if jobs else "near")
    scatter.begin()
    mail.start()
    load.start(ready)
    stages = scatter.stages()
    for i in range(max(len(stages), len(works))):
        if i < len(stages):
            stages[i]()
        if fold is not None and i == fold + 1:
            folding.turn()
        doing.run(i)
        load.start([j for j, job in enumerate(jobs) if j not in ready and job.src == i])
        if i == fold:
            folding.begin()
    mail.finish()
    load.finish()
    if fold is not None:
        folding.finish()
    scatter.finish()


def scatter_sum(p, chips, owners, by_row, collective_id, jobs=(), mails=(), works=(), fold=None):
    first, second = expert_factors(owners)
    half, full = p.shape[2:]
    parts = scatter_parts(chips, owners, half, full)
    width = full // parts
    n_dp = chips * 2

    def call(part, jobs, mails, works, fold):
        extra_shapes, extra_scratch = [], []
        if fold is not None:
            rows, columns = works[fold].shape.shape
            cut = (n_dp, rows // (n_dp * owners), columns)
            extra_shapes = [jax.ShapeDtypeStruct(cut, BF16)]
            extra_scratch = Fold.scratch(n_dp, owners, cut[1], columns)
        shapes = [jax.ShapeDtypeStruct((2, half, width), F32)]
        shapes += [job.out_shape for job in jobs] + Mail.shapes(mails, n_dp * owners)
        shapes += Works.shapes(works) + extra_shapes
        ins = [p] + [job.src for job in jobs if not isinstance(job.src, int)]
        ins += list(mails) + Works.arrays(works)
        return pl.pallas_call(
            functools.partial(
                scatter_kernel, chips, first, second, by_row, part * width, width, jobs,
                [jax.ShapeDtypeStruct(a.shape, a.dtype) for a in mails], works, fold,
            ),
            out_shape=shapes,
            in_specs=[ANY] * len(ins),
            out_specs=[pl.BlockSpec(memory_space=pltpu.VMEM)] + [ANY] * (len(shapes) - 1),
            scratch_shapes=Scatter.scratch(chips, first, second, half, width)
            + Mail.scratch(mails, n_dp * owners)
            + extra_scratch
            + Load.scratch(jobs, n_dp),
            compiler_params=pltpu.CompilerParams(
                collective_id=collective_id + part, has_side_effects=True,
                vmem_limit_bytes=60 * 2**20,
            ),
        )(*ins)

    calls = [call(0, jobs, mails, works, fold)]
    calls += [call(part, (), (), (), None) for part in range(1, parts)]
    whole = calls[0][0] if parts == 1 else jnp.concatenate([c[0] for c in calls], axis=-1)
    return [whole] + list(calls[0][1:])


class Riders:
    def __init__(self, chips, owners, jobs=(), gather=None, scatter=None, works=()):
        self.chips, self.owners, self.jobs, self.works = chips, owners, jobs, works
        self.factors = expert_factors(owners)
        self.orders = [order for pair in (gather, scatter) if pair for order in pair[1:]]
        self.has = gather is not None, scatter is not None
        self.ins = [pair[0] for pair in (gather, scatter) if pair] + [job.src for job in jobs]
        self.ins += Works.arrays(works)
        self.out_shapes, self.out_specs, self.scratch = [], [], []
        blocks = chips * 2 * owners
        if gather:
            x, by_row = gather
            rest = x.shape[1:]
            shape = (2, blocks) + rest if by_row else (blocks, 2) + rest
            self.out_shapes.append(jax.ShapeDtypeStruct(shape, x.dtype))
            self.out_specs.append(ANY)
            self.scratch += Gather.scratch(chips, *self.factors)
        if scatter:
            half, full = scatter[0].shape[2:]
            shape = jax.ShapeDtypeStruct((2, half, full), F32)
            self.out_shapes.append(shape)
            self.out_specs.append(pl.BlockSpec(shape.shape, lambda i: (0, 0, 0)))
            self.scratch += Scatter.scratch(chips, *self.factors, half, full)
            self.full = full
        self.out_shapes += [job.out_shape for job in jobs] + Works.shapes(works)
        self.out_specs += [ANY] * (len(jobs) + len(works))
        self.scratch += Load.scratch(jobs, chips * 2)
        self.ins_specs = [ANY] * len(self.ins)
        self.count = len(self.ins)

    def params(self, collective_id):
        if not self.count:
            return dict(vmem_limit_bytes=60 * 2**20)
        return dict(
            vmem_limit_bytes=60 * 2**20, collective_id=collective_id, has_side_effects=True
        )

    def board(self, refs, ins, outs, scratch=0):
        refs = list(refs)
        own = taken(refs, ins)
        given = taken(refs, self.count)
        own += taken(refs, outs)
        results = taken(refs, len(self.out_shapes))
        own += taken(refs, scratch)
        if not self.count:
            return own
        self.me = me = Place(self.chips, *self.factors)
        orders, staged, self.stages = list(self.orders), [], []
        if self.has[0]:
            rider = Gather(me, orders.pop(0), given.pop(0), results.pop(0), taken(refs, 3))
            staged.append(rider)
        if self.has[1]:
            rider = Scatter(
                me, orders.pop(0), 0, self.full, given.pop(0), results.pop(0), taken(refs, 15)
            )
            staged.append(rider)
        n = len(self.jobs)
        load = Load(self.jobs, me, given[:n], results[:n], refs)
        works = Works(self.works, given[n:], results[n:])
        step, steps = pl.program_id(0), pl.num_programs(0)

        @pl.when(step == 0)
        def _():
            me.greet("column" if not staged else "dp" if self.jobs else "near")
            for rider in staged:
                rider.begin()
            if not self.has[0]:
                load.start()

        plan = []
        for rider in staged:
            if isinstance(rider, Gather):
                along, across = rider.along(), rider.across()
                along.insert(len(along) - 1, load.start)
                unit = max(1, (self.steps - 4) // self.chips)
                spots = [unit * (i + 1) for i in range(self.chips - 1)]
                spots.insert(len(spots) - 1, spots[max(0, len(spots) - 2)])
                spots += [unit * (i + 1) + 2 for i in range(self.chips)]
                plan += list(zip(spots, along + across))
            else:
                stages = rider.stages()
                plan += [
                    (1 + i * (self.steps - 2) // (len(stages) - 1), stage)
                    for i, stage in enumerate(stages)
                ]
        for at, stage in plan:
            pl.when(step == at)(stage)

        def finish():
            @pl.when(step == steps - 1)
            def _():
                for i in range(len(self.works)):
                    works.run(i)
                for rider in staged:
                    rider.finish()
                load.finish()

        self.alight = finish
        return own

    def alight(self):
        pass


def exchange_kernel(chips, first, second, array, x_ref, out_ref, *sems):
    me = Place(chips, first, second)
    mail = Mail([array], me, [x_ref], [out_ref], sems)
    me.greet("all")
    mail.start()
    mail.finish()


def exchange(x, chips, owners, collective_id):
    first, second = expert_factors(owners)
    devices = chips * 2 * owners
    shape = jax.ShapeDtypeStruct(x.shape, x.dtype)
    return pl.pallas_call(
        functools.partial(exchange_kernel, chips, first, second, shape),
        out_shape=shape,
        in_specs=[ANY],
        out_specs=ANY,
        scratch_shapes=Mail.scratch([shape], devices),
        compiler_params=pltpu.CompilerParams(collective_id=collective_id, has_side_effects=True),
    )(x)


D = 2048
KVH = 16
HD = 128
FF = 5632
NEXP = 8
TOK_MB = 64
CAP = 24
LANES = 128
EPSILON = 1e-06


def dot(a, b):
    return jnp.dot(a, b, preferred_element_type=F32)


def dot_nt(a, b):
    return lax.dot_general(a, b, (((1,), (1,)), ((), ())), preferred_element_type=F32)


def dot_tn(a, b):
    return lax.dot_general(a, b, (((0,), (0,)), ((), ())), preferred_element_type=F32)


def counted(shape, axis):
    return lax.broadcasted_iota(jnp.int32, shape, axis).astype(F32)


def two_parts(value):
    upper = value.astype(BF16)
    return upper, (value - upper.astype(F32)).astype(BF16)


class Seats:
    def __init__(self, meta, first_expert, count, tri, eye):
        slots = meta.shape[1]
        per = slots // TOK_MB * CAP
        self.count, self.per, self.slots, self.first = count, per, slots, first_expert
        line = counted(meta.shape, 0)
        expert = first_expert + line
        hit = (meta[0:1] == expert) | (meta[1:2] == expert)
        hit = hit & (line < count)
        rank = dot(jnp.where(hit, 1.0, 0.0).astype(BF16), tri)
        block = lax.broadcasted_iota(jnp.int32, meta.shape, 1) // TOK_MB
        seat = jnp.where(hit, block.astype(F32) * CAP + rank + line * per, -1.0)
        self.routes = dot_nt(eye, meta.astype(BF16))
        column = dot_nt(eye, seat.astype(BF16))
        total = count * per
        row = counted((total, slots), 0)
        lane = counted((slots, total), 1)
        here, there = row == seat[0:1], lane == column[:, 0:1]
        for l in range(1, count):
            here = here | (row == seat[l : l + 1])
            there = there | (lane == column[:, l : l + 1])
        self.take = jnp.where(here, 1.0, 0.0).astype(BF16)
        self.put = jnp.where(there, 1.0, 0.0).astype(BF16)

    def gates(self, logits):
        lane = counted(logits.shape, 1)
        one = jnp.sum(jnp.where(lane == self.routes[:, 0:1], logits, 0.0), axis=1, keepdims=True)
        two = jnp.sum(jnp.where(lane == self.routes[:, 1:2], logits, 0.0), axis=1, keepdims=True)
        highest = jnp.maximum(one, two)
        one, two = jnp.exp(one - highest), jnp.exp(two - highest)
        total = one + two
        return one / total, two / total

    def seat_values(self, pairs, plain):
        lane = counted((self.slots, LANES), 1)
        per_expert = []
        for l in range(self.count):
            expert = self.first + l
            values = [
                jnp.where(self.routes[:, 0:1] == expert, a, 0.0)
                + jnp.where(self.routes[:, 1:2] == expert, b, 0.0)
                for a, b in pairs
            ] + list(plain)
            packed = jnp.zeros((self.slots, LANES), F32)
            for i, value in enumerate(values):
                upper, lower = two_parts(value)
                packed = jnp.where(lane == 2 * i, upper.astype(F32), packed)
                packed = jnp.where(lane == 2 * i + 1, lower.astype(F32), packed)
            part = dot(self.take[l * self.per : (l + 1) * self.per], packed.astype(BF16))
            per_expert.append(
                [part[:, 2 * i : 2 * i + 1] + part[:, 2 * i + 1 : 2 * i + 2] for i in range(len(values))]
            )
        return [
            jnp.concatenate(parts, axis=0) if self.count > 1 else parts[0]
            for parts in zip(*per_expert)
        ]

    def slot_values(self, value):
        total = self.count * self.per
        lane = counted((total, LANES), 1)
        row = counted((total, LANES), 0)
        upper, lower = two_parts(value)
        packed = jnp.zeros((total, LANES), F32)
        for l in range(self.count):
            mine = (row >= l * self.per) & (row < (l + 1) * self.per)
            packed = jnp.where(mine & (lane == 2 * l), upper.astype(F32), packed)
            packed = jnp.where(mine & (lane == 2 * l + 1), lower.astype(F32), packed)
        back = dot(self.put, packed.astype(BF16))
        out = jnp.zeros((self.slots, 8), F32)
        lane = counted((self.slots, 8), 1)
        for l in range(self.count):
            value = back[:, 2 * l : 2 * l + 1] + back[:, 2 * l + 1 : 2 * l + 2]
            for k in range(2):
                chosen = (self.routes[:, k : k + 1] == self.first + l) & (lane == k)
                out = jnp.where(chosen, value, out)
        return out


def first_expert(count):
    return (lax.axis_index("expert") * count).astype(F32)


def turned(values, cosine, sine):
    heads = []
    for h in range(values.shape[1] // HD):
        head = values[:, h * HD : (h + 1) * HD]
        heads.append(head * cosine + pltpu.roll(head, HD // 2, 1) * sine)
    return heads[0] if len(heads) == 1 else jnp.concatenate(heads, axis=1)


def mixer_forward_kernel(count, riders, *refs):
    (
        length_ref, x_ref, meta_ref, gain_ref, router_ref, *wq_refs, wkv_ref, wo_ref,
        tri_ref, eye_ref, upper_ref, lower_ref,
        normed_ref, part_ref, rows_ref, key_ref, value_ref, query_ref, mix_ref, gated_ref, info_ref, gates_ref,
    ) = riders.board(refs, 11 + count, 10)
    hc = key_ref.shape[2]
    x = x_ref[0].astype(F32)
    inverse = lax.rsqrt(jnp.mean(x * x, axis=1, keepdims=True) + EPSILON)
    normed = (x * inverse * gain_ref[...]).astype(BF16)
    normed_ref[0] = normed
    seats = Seats(meta_ref[0], first_expert(count), count, tri_ref[...], eye_ref[...])
    one, two = seats.gates(dot(normed, router_ref[...]))
    lane = counted((seats.slots, 8), 1)
    gates_ref[0] = jnp.where(lane == 0, one, jnp.where(lane == 1, two, 0.0))
    gate, place = seats.seat_values([(one, two)], [counted((seats.slots, 1), 0)])
    lane = counted((gate.shape[0], 8), 1)
    info_ref[0] = jnp.where(lane == 0, gate, jnp.where(lane == 1, place, 0.0))

    key_value = dot(normed, wkv_ref[...])
    upper, lower = upper_ref[...], lower_ref[...]
    table = upper.astype(F32) + lower.astype(F32)
    key = turned(key_value[:, :hc], table[:, :HD], table[:, HD:]).astype(BF16)
    value = key_value[:, hc:].astype(BF16)
    key_ref[0], value_ref[0] = key, value

    rows = dot(seats.take, normed).astype(BF16)
    per = seats.per
    for l in range(count):
        rows_ref[l] = rows[l * per : (l + 1) * per]
    table = dot(seats.take, upper) + dot(seats.take, lower)
    query = [dot(rows[l * per : (l + 1) * per], wq_refs[l][...]) for l in range(count)]
    query = query[0] if count == 1 else jnp.concatenate(query, axis=0)
    query = (turned(query, table[:, :HD], table[:, HD:]) * HD ** (-0.5)).astype(BF16)
    query_ref[0] = query

    at = counted((seats.take.shape), 1)
    length = length_ref[pl.program_id(0)].astype(F32)
    allowed = (at <= place) & (at < length)
    mix = []
    for h in range(hc // HD):
        cut = slice(h * HD, (h + 1) * HD)
        scores = jnp.where(allowed, dot_nt(query[:, cut], key[:, cut]), -1e30)
        exponent = jnp.exp(scores - jnp.max(scores, axis=1, keepdims=True))
        probs = (exponent / jnp.sum(exponent, axis=1, keepdims=True)).astype(BF16)
        mix.append(dot(probs, value[:, cut]))
    mix = mix[0] if len(mix) == 1 else jnp.concatenate(mix, axis=1)
    mix_ref[0] = mix
    gated = (mix * gate).astype(BF16)
    for l in range(count):
        gated_ref[l] = gated[l * per : (l + 1) * per]
    out = [dot(gated[l * per : (l + 1) * per], wo_ref[l]).astype(BF16) for l in range(count)]
    out = out[0] if count == 1 else jnp.concatenate(out, axis=0)
    part_ref[0] = dot(seats.put, out).astype(BF16)
    riders.alight()


def mixer_backward_kernel(count, riders, *refs):
    (
        length_ref, grad_ref, meta_ref, *wq_refs, wkv_ref, wo_ref, tri_ref, eye_ref,
        upper_ref, lower_ref, key_ref, value_ref, query_ref, mix_ref, info_ref,
        part_ref, rows_ref, terms_ref, grad_query_ref, grad_key_value_ref,
    ) = riders.board(refs, 14 + count, 5)
    hc = key_ref.shape[2]
    seats = Seats(meta_ref[0], first_expert(count), count, tri_ref[...], eye_ref[...])
    per = seats.per
    rows = dot(seats.take, grad_ref[0]).astype(BF16)
    for l in range(count):
        rows_ref[l] = rows[l * per : (l + 1) * per]
    grad_mix = [dot_nt(rows[l * per : (l + 1) * per], wo_ref[l]) for l in range(count)]
    grad_mix = grad_mix[0] if count == 1 else jnp.concatenate(grad_mix, axis=0)
    gate, place = info_ref[0, :, 0:1], info_ref[0, :, 1:2]
    terms_ref[0] = seats.slot_values(jnp.sum(grad_mix * mix_ref[0], axis=1, keepdims=True))
    grad_mix = (grad_mix * gate).astype(BF16)

    at = counted(seats.take.shape, 1)
    length = length_ref[pl.program_id(0)].astype(F32)
    allowed = (at <= place) & (at < length)
    key, value, query = key_ref[0], value_ref[0], query_ref[0]
    grad_query, grad_key, grad_value = [], [], []
    for h in range(hc // HD):
        cut = slice(h * HD, (h + 1) * HD)
        scores = jnp.where(allowed, dot_nt(query[:, cut], key[:, cut]), -1e30)
        exponent = jnp.exp(scores - jnp.max(scores, axis=1, keepdims=True))
        probs = exponent / jnp.sum(exponent, axis=1, keepdims=True)
        grad_probs = dot_nt(grad_mix[:, cut], value[:, cut])
        grad_value.append(dot_tn(probs.astype(BF16), grad_mix[:, cut]))
        row_dot = jnp.sum(probs * grad_probs, axis=1, keepdims=True)
        grad_scores = (probs * (grad_probs - row_dot)).astype(BF16)
        grad_query.append(dot(grad_scores, key[:, cut]))
        grad_key.append(dot_tn(grad_scores, query[:, cut]))

    def joined(parts):
        return parts[0] if len(parts) == 1 else jnp.concatenate(parts, axis=1)

    upper, lower = upper_ref[...], lower_ref[...]
    table = dot(seats.take, upper) + dot(seats.take, lower)
    grad_query = turned(joined(grad_query), table[:, :HD], -table[:, HD:]) * HD ** (-0.5)
    grad_query = grad_query.astype(BF16)
    for l in range(count):
        grad_query_ref[l] = grad_query[l * per : (l + 1) * per]
    table = upper.astype(F32) + lower.astype(F32)
    grad_key = turned(joined(grad_key), table[:, :HD], -table[:, HD:])
    grad_key_value = jnp.concatenate([grad_key, joined(grad_value)], axis=1).astype(BF16)
    grad_key_value_ref[0] = grad_key_value
    back = [
        dot_nt(grad_query[l * per : (l + 1) * per], wq_refs[l][...]).astype(BF16)
        for l in range(count)
    ]
    back = back[0] if count == 1 else jnp.concatenate(back, axis=0)
    part_ref[0] = (dot(seats.put, back) + dot_nt(grad_key_value, wkv_ref[...])).astype(BF16)
    riders.alight()


def feed_kernel(count, l, last, groups, turns, riders, *refs):
    prior = 2 * l if last else 0
    refs = riders.board(refs, 10 + prior, 9 if last else 9, 4 if last else 2)
    (
        offset_ref, x_ref, cot_ref, meta_ref, router_ref, wg_ref, wu_ref, wd_ref, tri_ref, eye_ref,
    ) = refs[:10]
    before, refs = refs[10 : 10 + prior], refs[10 + prior :]
    part_ref, back_ref, rows_ref, cot_rows_ref, active_ref, grad_gate_ref, grad_up_ref, terms_ref, gates_ref = refs[:9]
    gate_ref, term_ref = refs[9:11]
    kept = []
    for g in range(groups):
        seats = Seats(meta_ref[g], first_expert(count), count, tri_ref[...], eye_ref[...])
        kept.append(seats)
        per = seats.per
        mine = slice(l * per, (l + 1) * per)
        one, two = seats.gates(dot(x_ref[g], router_ref[...]))
        lane = counted((seats.slots, 8), 1)
        gates_ref[g] = jnp.where(lane == 0, one, jnp.where(lane == 1, two, 0.0))
        (gate,) = seats.seat_values([(one, two)], [])
        take = seats.take[mine]
        valid = meta_ref[g][2:3] > 0.0
        here = slice(g * per, (g + 1) * per)
        rows_ref[here] = dot(take, x_ref[g]).astype(BF16)
        cot_rows_ref[here] = dot(jnp.where(valid, take, 0.0).astype(BF16), cot_ref[g]).astype(BF16)
        gate_ref[here] = jnp.broadcast_to(gate[mine], (per, LANES))
    wide = wd_ref.shape[1]
    rows, cot_rows, gate = rows_ref[...], cot_rows_ref[...], gate_ref[...][:, 0:1]
    gate_part = dot(rows, wg_ref[...])
    up_part = dot(rows, wu_ref[...])
    grad_plain = dot_nt(cot_rows, wd_ref[0])
    sigmoid = 1.0 / (1.0 + jnp.exp(-gate_part))
    silu = gate_part * sigmoid
    active = silu * up_part
    gated = active * gate
    front = gated
    for off in turns:
        front = jnp.where(offset_ref[0] == off, pltpu.roll(gated, wide - off, 1), front)
    active_ref[...] = front.astype(BF16)
    gated = gated.astype(BF16)
    term = jnp.sum(active * grad_plain, axis=1, keepdims=True)
    term_ref[...] = jnp.broadcast_to(term, term_ref.shape)
    grad_active = grad_plain * gate
    grad_up = (grad_active * silu).astype(BF16)
    grad_gate = (
        grad_active * up_part * sigmoid * (1.0 + gate_part * (1.0 - sigmoid))
    ).astype(BF16)
    grad_gate_ref[...], grad_up_ref[...] = grad_gate, grad_up
    out = dot(gated, wd_ref[0]).astype(BF16)
    back = (dot_nt(grad_gate, wg_ref[...]) + dot_nt(grad_up, wu_ref[...])).astype(BF16)
    if last:
        out_ref, dx_ref = refs[11:]
        for g in range(groups):
            here = slice(g * per, (g + 1) * per)
            for e in range(l):
                out_ref[g, e * per : (e + 1) * per] = before[2 * e][here]
                dx_ref[g, e * per : (e + 1) * per] = before[2 * e + 1][here]
            out_ref[g, mine] = out[here]
            dx_ref[g, mine] = back[here]
        for g in range(groups):
            part_ref[g] = dot(kept[g].put, out_ref[g]).astype(BF16)
            back_ref[g] = dot(kept[g].put, dx_ref[g]).astype(BF16)
    else:
        part_ref[...], back_ref[...] = out, back
    for g in range(groups):
        value = term_ref[g * per : (g + 1) * per][:, 0:1]
        parts = [value if e == l else jnp.zeros_like(value) for e in range(count)]
        value = parts[0] if count == 1 else jnp.concatenate(parts, axis=0)
        terms_ref[g] = kept[g].slot_values(value)
    riders.alight()


def whole_block(array):
    return pl.BlockSpec(array.shape, lambda i: (0,) * array.ndim)


def step_block(shape, first=1):
    return pl.BlockSpec((first,) + tuple(shape[1:]), lambda i: (i,) + (0,) * (len(shape) - 1))


SMEM = pl.BlockSpec(memory_space=pltpu.SMEM)


def constants(slots):
    at = np.arange(slots)
    earlier = (at[:, None] < at[None, :]) & (at[:, None] // TOK_MB == at[None, :] // TOK_MB)
    return jnp.asarray(earlier, BF16), jnp.asarray(np.eye(slots), BF16)


def mixer_tables(slots):
    frequency = 10000.0 ** (-(jnp.arange(HD // 2, dtype=F32) * (2.0 / HD)))
    angles = jnp.arange(slots, dtype=F32)[:, None] * frequency
    cosine, sine = jnp.cos(angles), jnp.sin(angles)
    table = jnp.concatenate([cosine, cosine, -sine, sine], axis=1)
    upper = lax.reduce_precision(table, 8, 7)
    return upper.astype(BF16), (table - upper).astype(BF16)


def mixer_forward(x, meta, lengths, gain, router, wq, wkv, wo, fixed, riders, collective_id):
    seqs, slots, _ = x.shape
    riders.steps = seqs
    count, hc = len(wq), wq[0].shape[1]
    seats = slots // TOK_MB * CAP * count
    per = seats // count

    def by_expert(width):
        shape = (count, seqs * per, width)
        return shape, BF16, pl.BlockSpec((count, per, width), lambda i: (0, i, 0))

    def by_row(rows, width, dtype=BF16):
        shape = (seqs, rows, width)
        return shape, dtype, step_block(shape)

    outs = [
        by_row(slots, D), by_row(slots, D), by_expert(D), by_row(slots, hc), by_row(slots, hc),
        by_row(seats, hc), by_row(seats, hc, F32), by_expert(hc), by_row(seats, 8, F32), by_row(slots, 8, F32),
    ]
    fixed_in = [gain, router, *wq, wkv, wo, *fixed]
    return pl.pallas_call(
        functools.partial(mixer_forward_kernel, count, riders),
        grid=(seqs,),
        out_shape=[jax.ShapeDtypeStruct(shape, dtype) for shape, dtype, _ in outs]
        + riders.out_shapes,
        in_specs=[SMEM, step_block(x.shape), step_block(meta.shape)]
        + [whole_block(a) for a in fixed_in]
        + riders.ins_specs,
        out_specs=[spec for _, _, spec in outs] + riders.out_specs,
        scratch_shapes=riders.scratch,
        compiler_params=pltpu.CompilerParams(**riders.params(collective_id)),
    )(lengths, x, meta, *fixed_in, *riders.ins)


def mixer_backward(
    grad, meta, lengths, wq, wkv, wo, fixed, saved, riders, collective_id
):
    seqs, slots, _ = grad.shape
    riders.steps = seqs
    count, hc = len(wq), wq[0].shape[1]
    seats = slots // TOK_MB * CAP * count
    per = seats // count

    def by_expert(width):
        shape = (count, seqs * per, width)
        return shape, BF16, pl.BlockSpec((count, per, width), lambda i: (0, i, 0))

    def by_row(rows, width, dtype=BF16):
        shape = (seqs, rows, width)
        return shape, dtype, step_block(shape)

    outs = [
        by_row(slots, D), by_expert(D), by_row(slots, 8, F32), by_expert(hc), by_row(slots, 2 * hc)
    ]
    fixed_in = [*wq, wkv, wo, *fixed]
    return pl.pallas_call(
        functools.partial(mixer_backward_kernel, count, riders),
        grid=(seqs,),
        out_shape=[jax.ShapeDtypeStruct(shape, dtype) for shape, dtype, _ in outs]
        + riders.out_shapes,
        in_specs=[SMEM, step_block(grad.shape), step_block(meta.shape)]
        + [whole_block(a) for a in fixed_in]
        + [step_block(a.shape) for a in saved]
        + riders.ins_specs,
        out_specs=[spec for _, _, spec in outs] + riders.out_specs,
        scratch_shapes=riders.scratch,
        compiler_params=pltpu.CompilerParams(**riders.params(collective_id)),
    )(lengths, grad, meta, *fixed_in, *saved, *riders.ins)


def feed(x, cot, meta, router, wg, wu, wd, fixed, offset, offsets, l, count, before, riders, collective_id):
    groups, slots, _ = x.shape
    _, wide, _ = wd.shape
    per = slots // TOK_MB * CAP
    last = l == count - 1
    at_once = 2 if last else 4
    riders.steps = groups // at_once
    seats = groups * per

    def of_rows(width):
        return ((seats, width), BF16), pl.BlockSpec((at_once * per, width), lambda i: (i, 0))

    def of_slots(width, dtype):
        return ((groups, slots, width), dtype), step_block((groups, slots, width), at_once)

    outs = [of_slots(D, BF16) if last else of_rows(D)] * 2
    outs += [of_rows(width) for width in (D, D, wide, wide, wide)] + [of_slots(8, F32)] * 2
    fixed_in = [router, wg, wu, wd, *fixed]
    turns = sorted({o for o in offsets if o})
    scratch = [pltpu.VMEM((at_once * per, LANES), F32)] * 2
    if last:
        scratch += [pltpu.VMEM((at_once, count * per, D), BF16)] * 2
    return pl.pallas_call(
        functools.partial(feed_kernel, count, l, last, at_once, turns, riders),
        grid=(groups // at_once,),
        out_shape=[jax.ShapeDtypeStruct(*shape) for shape, _ in outs] + riders.out_shapes,
        in_specs=[SMEM]
        + [step_block(a.shape, at_once) for a in (x, cot, meta)]
        + [
            pl.BlockSpec((1, wide, D), lambda i: (l, 0, 0), pipeline_mode=pl.Buffered(1))
            if a is wd
            else pl.BlockSpec(a.shape, lambda i, n=a.ndim: (0,) * n, pipeline_mode=pl.Buffered(1))
            for a in fixed_in
        ]
        + [of_rows(D)[1]] * len(before)
        + riders.ins_specs,
        out_specs=[spec for _, spec in outs] + riders.out_specs,
        scratch_shapes=scratch + riders.scratch,
        compiler_params=pltpu.CompilerParams(**riders.params(collective_id)),
    )(offset.reshape(1), x, cot, meta, *fixed_in, *before, *riders.ins)


def rejoin_kernel(*refs):
    *parts, key_value, query_out, key_value_out = refs
    for l, part in enumerate(parts):
        n_dp, _, hc = part.shape
        for d in range(n_dp):
            query_out[l, :, d * hc : (d + 1) * hc] = part[d].astype(F32)
    for d in range(n_dp):
        for half in range(2):
            at = (half * n_dp + d) * hc
            key_value_out[:, at : at + hc] = key_value[d, :, half * hc : (half + 1) * hc].astype(F32)


def rejoin(parts, key_value):
    n_dp, depth, hc = parts[0].shape
    rows = key_value.shape[1]
    return pl.pallas_call(
        rejoin_kernel,
        out_shape=[
            jax.ShapeDtypeStruct((len(parts), depth, n_dp * hc), F32),
            jax.ShapeDtypeStruct((rows, 2 * n_dp * hc), F32),
        ],
        compiler_params=pltpu.CompilerParams(vmem_limit_bytes=48 * 2**20),
    )(*parts, key_value)


def norm_forward(values, norm_gain):
    inverse = lax.rsqrt(jnp.mean(values * values, axis=-1, keepdims=True) + EPSILON)
    return (values * inverse * norm_gain, inverse)


def norm_backward(values, inverse, norm_gain, grad_normed):
    scaled = grad_normed * norm_gain
    grad_gain = jnp.sum(grad_normed * values * inverse, axis=(0, 1))
    grad_values = inverse * scaled - values * inverse**3 * jnp.mean(
        scaled * values, axis=-1, keepdims=True
    )
    return (grad_values, grad_gain)


def gate_grads(gate_probs, grad_gate_probs, routes):
    weighted = jnp.sum(gate_probs * grad_gate_probs, axis=-1, keepdims=True)
    grad_picked = gate_probs * (grad_gate_probs - weighted)
    choose = (routes[..., None] == jnp.arange(NEXP, dtype=jnp.int32)).astype(F32)
    return jnp.sum(grad_picked[..., None] * choose, axis=-2)


def tile_starts(shards):
    share = FF // shards
    most = max(share * d % LANES for d in range(shards))
    tiles = -(-(share + most) // LANES)
    starts = [min(share * d // LANES, FF // LANES - tiles) for d in range(shards)]
    return tiles, starts, [share * d - LANES * starts[d] for d in range(shards)]


def put_together_kernel(count, starts, tiles, *refs):
    out_ref = refs[-1]
    edges = sorted(set(starts) | {s + tiles for s in starts})
    for l in range(count):
        for g in range(2):
            part = refs[l * 2 + g]
            for low, high in zip(edges[:-1], edges[1:]):
                cover = [d for d in range(len(starts)) if starts[d] <= low and high <= starts[d] + tiles]
                value = None
                for d in cover:
                    cut = slice((low - starts[d]) * LANES, (high - starts[d]) * LANES)
                    term = part[d, :, cut].astype(F32)
                    value = term if value is None else value + term
                out_ref[l, :, g * FF + low * LANES : g * FF + high * LANES] = value


def put_together(parts, count, starts, tiles):
    n_dp, depth, wide = parts[0].shape
    rows = 32
    return pl.pallas_call(
        functools.partial(put_together_kernel, count, starts, tiles),
        grid=(depth // rows,),
        out_shape=jax.ShapeDtypeStruct((count, depth, 2 * FF), F32),
        in_specs=[pl.BlockSpec((n_dp, rows, wide), lambda i: (0, i, 0))] * len(parts),
        out_specs=pl.BlockSpec((count, rows, 2 * FF), lambda i: (0, i, 0)),
        compiler_params=pltpu.CompilerParams(vmem_limit_bytes=48 * 2**20),
    )(*parts)


def product(pattern, operand, factor):
    return jnp.einsum(pattern, operand, factor, preferred_element_type=F32)


def shards(
    tokens, lengths, attention_routes, feedforward_routes, norm_gains, router_weight,
    key_value_weight, query_weight, output_weight, input_weight, down_weight, cotangent,
):
    n_dp = lax.axis_size("dp")
    owners = lax.axis_size("expert")
    chips = n_dp // 2
    devices = n_dp * owners
    dp = lax.axis_index("dp")
    ex = lax.axis_index("expert")
    me = dp * owners + ex
    mb = tokens.shape[0]
    count = NEXP // owners
    seqs = mb * n_dp
    slots = owners * TOK_MB
    hc = KVH // n_dp * HD
    att = KVH * HD
    depth = D // n_dp
    slice_rows = D // devices
    tiles, starts, offsets = tile_starts(n_dp)
    share, wide = FF // n_dp, tiles * LANES
    offset = jnp.array(offsets, jnp.int32)[dp]

    def query_job(l):
        return Job(
            query_weight,
            jax.ShapeDtypeStruct((D, hc), BF16),
            lambda src, d: src.at[l, :, pl.ds(pl.multiple_of(d * hc, LANES), hc)],
            lambda out, d: out.at[pl.ds(pl.multiple_of(d * depth, depth), depth)],
        )

    key_value_job = Job(
        jnp.swapaxes(key_value_weight.reshape(slice_rows, 2, att), 0, 1),
        jax.ShapeDtypeStruct((n_dp, owners, 2, slice_rows, hc), BF16),
        lambda src, d: src.at[:, :, pl.ds(pl.multiple_of(d * hc, LANES), hc)],
        lambda out, d: out.at[d, lax.axis_index("expert")],
    )

    def start_of(d):
        start = (share * d) // LANES
        if max(share * i // LANES - starts[i] for i in range(n_dp)):
            start = jnp.minimum(start, FF // LANES - tiles)
        return start

    def input_job(l, g):
        return Job(
            input_weight,
            jax.ShapeDtypeStruct((D, wide), BF16),
            lambda src, d: src.at[
                l, :, pl.ds(pl.multiple_of(g * FF + start_of(d) * LANES, LANES), wide)
            ],
            lambda out, d: out.at[pl.ds(pl.multiple_of(d * depth, depth), depth)],
        )

    def back_job(grad, columns):
        return Job(
            grad,
            jax.ShapeDtypeStruct((n_dp, depth, columns), BF16),
            lambda src, d: src.at[pl.ds(pl.multiple_of(d * depth, depth), depth)],
            lambda out, d: out.at[d],
        )

    input_jobs = [[input_job(l, g) for g in range(2)] for l in range(count)]
    down_full = lax.dynamic_update_slice(
        jnp.zeros((count, wide, D), BF16), down_weight, (0, offset, 0)
    )

    def route_lines(routes):
        return jnp.swapaxes(routes[:, 0], 1, 2).reshape(-1, LANES).astype(F32)

    shared = jnp.concatenate([norm_gains, router_weight], axis=1).astype(F32)
    tail = jnp.concatenate([shared.reshape(-1), lengths.reshape(-1).astype(F32)])
    tail = jnp.pad(tail, (0, -tail.shape[0] % LANES)).reshape(-1, LANES)
    small = jnp.concatenate(
        [route_lines(attention_routes), route_lines(feedforward_routes), tail]
    )
    small = jnp.pad(small, ((0, -small.shape[0] % 8), (0, 0)))[None]
    tokens_all, small, *resharded = gather_all(
        [tokens.reshape(mb, TOK_MB, D)], [True], chips, owners, 1,
        [key_value_job] + [query_job(l) for l in range(count)], [small],
    )
    tokens_all = tokens_all.reshape(seqs, slots, D)
    query_full = resharded[1:]
    key_value_full = jnp.transpose(resharded[0], (0, 1, 3, 2, 4)).reshape(D, 2 * hc)
    group_slots = mb * TOK_MB * 2
    groups = devices // 2
    lines = mb * 2 * TOK_MB // LANES
    mixer_routes = small[:, :lines].reshape(n_dp, owners, mb, 2, TOK_MB)
    mixer_meta = jnp.transpose(mixer_routes, (2, 0, 3, 1, 4)).reshape(seqs, 2, slots)
    mixer_meta = jnp.pad(mixer_meta, ((0, 0), (0, 6), (0, 0)))
    feed_routes = small[:, lines : 2 * lines].reshape(groups, 2, mb, 2, TOK_MB)
    feed_meta = jnp.transpose(feed_routes, (0, 3, 1, 2, 4)).reshape(groups, 2, group_slots)
    tail = small[:, 2 * lines :].reshape(devices, -1)
    shared_all = tail[:, : slice_rows * 18].reshape(D, 18)
    all_lengths = tail[:, slice_rows * 18 : slice_rows * 18 + mb].reshape(n_dp, owners, mb)
    row_lengths = all_lengths[:, 0].T.reshape(seqs).astype(jnp.int32)
    places = (jnp.arange(owners)[:, None, None] * TOK_MB + jnp.arange(TOK_MB)).astype(F32)
    valid = (places[None] < all_lengths[..., None]).astype(F32).reshape(groups, 1, group_slots)
    feed_meta = jnp.concatenate([feed_meta, valid], axis=1)
    feed_meta = jnp.pad(feed_meta, ((0, 0), (0, 5), (0, 0)))
    gain_mixer, gain_feed = shared_all[:, 0], shared_all[:, 1]
    router_mixer, router_feed = shared_all[:, 2 : 2 + NEXP], shared_all[:, 2 + NEXP :]

    def routers(part):
        return jnp.pad(part.astype(BF16), ((0, 0), (0, LANES - NEXP)))

    own_tokens = tokens[:, 0].astype(F32)
    home_places = ex * TOK_MB + jnp.arange(TOK_MB, dtype=jnp.int32)
    own_valid = (home_places[None, :] < lengths[:, :1]).astype(F32)
    own_cotangent = cotangent[:, 0].astype(F32) * own_valid[..., None]

    normed_mixer, inverse_mixer = norm_forward(own_tokens, gain_mixer)
    fixed = constants(slots)
    tables = mixer_tables(slots)
    (
        mixer_all, mixer_part, rows_mixer, keys, values, queries, mixture, mixture_gated, info,
        gates_mixer, cot_all, *input_parts,
    ) = mixer_forward(
        tokens_all, mixer_meta, row_lengths, gain_mixer[None], routers(router_mixer), query_full,
        key_value_full, output_weight, (*fixed, *tables),
        Riders(chips, owners, input_jobs[0][:1], gather=(cotangent.reshape(mb, TOK_MB, D), False)), 2,
    )
    cot_all = cot_all.reshape(groups, group_slots, D)
    mixer_sum, *more_parts = scatter_sum(
        mixer_part.reshape(mb, devices, TOK_MB, D), chips, owners, True, 10, input_jobs[0][1:]
    )
    input_parts += more_parts

    second = own_tokens + mixer_sum
    normed_feed, inverse_feed = norm_forward(second, gain_feed)
    feed_all, *more_parts = gather_all(
        [normed_feed.astype(BF16)], [False], chips, owners, 3,
        input_jobs[1][:1] if count > 1 else [],
    )
    input_parts += more_parts
    feed_all = feed_all.reshape(groups, group_slots, D)
    feed_fixed = constants(group_slots)
    before, back_jobs, works, actives, cots, gate_terms_feed = [], [], [], [], [], 0.0
    for l in range(count):
        carried = [job for jobs in input_jobs[l + 1 : l + 2] for job in jobs[l == 0 :]]
        carried += back_jobs[:1]
        (
            feed_part, grad_feed_part, rows_feed, cot_rows, active_gated, grad_gate, grad_up,
            terms, gates_feed, *more_parts,
        ) = feed(
            feed_all, cot_all, feed_meta, routers(router_feed), input_parts[2 * l], input_parts[2 * l + 1],
            down_full, feed_fixed, offset, offsets, l, count, before,
            Riders(chips, owners, carried, works=works), 60 + l,
        )
        before += [feed_part, grad_feed_part]
        grad_input_parts = more_parts[len(carried) - len(back_jobs[:1]) :]
        input_parts += more_parts[: len(carried) - len(back_jobs[:1])]
        done = more_parts[len(carried) :]
        grad_input_parts = grad_input_parts[: len(back_jobs[:1])]
        works = []
        works += [Work(rows_feed, grad, BF16) for grad in (grad_gate, grad_up)]
        if l < count - 1:
            first_grad = product("rd,rf->df", rows_feed, grad_gate).astype(BF16)
            back_jobs.append(back_job(first_grad, wide))
            works.pop(-2)
        actives.append(active_gated[:, :share])
        cots.append(cot_rows)
        gate_terms_feed = gate_terms_feed + terms

    def home_parts(terms, by_row):
        terms = terms[..., :2]
        if by_row:
            terms = jnp.swapaxes(terms.reshape(mb, devices, TOK_MB * 2), 0, 1)
        terms = terms.reshape(devices, -1, LANES)
        return jnp.pad(terms, ((0, 0), (0, -terms.shape[1] % 8), (0, 0)))

    def at_home(parts):
        return jnp.sum(parts, axis=0).reshape(-1)[: mb * TOK_MB * 2].reshape(mb, TOK_MB, 2)

    def own_of(gates, by_row):
        gates = gates[..., :2]
        if by_row:
            return lax.dynamic_index_in_dim(
                gates.reshape(mb, devices, TOK_MB, 2), me, 1, keepdims=False
            )
        return lax.dynamic_index_in_dim(
            gates.reshape(devices, mb, TOK_MB, 2), me, 0, keepdims=False
        )

    grad_normed_feed, first_part, terms, *later = scatter_sum(
        grad_feed_part.reshape(devices, mb, TOK_MB, D), chips, owners, False, 20,
        [back_job(done[0] if done else 0, wide)], [home_parts(gate_terms_feed, False)], works,
    )
    grad_input_parts.append(first_part)
    later = [back_job(grad, wide) for grad in (later if done else later[1:])]
    grad_logits_feed = gate_grads(
        own_of(gates_feed, False), at_home(terms), feedforward_routes[:, 0]
    )
    grad_normed_feed = grad_normed_feed + product("mte,de->mtd", grad_logits_feed, router_feed)
    grad_second, grad_gain_feed = norm_backward(second, inverse_feed, gain_feed, grad_normed_feed)
    grad_second = grad_second + own_cotangent

    grad_all, *more_parts = gather_all(
        [grad_second.astype(BF16)], [True], chips, owners, 5, later[:1]
    )
    grad_down = product("lrf,lrd->lfd", jnp.stack(actives), jnp.stack(cots))
    grad_input_parts += more_parts[:1]
    grad_all = grad_all.reshape(seqs, slots, D)
    feed_part = feed_part.reshape(devices, mb, TOK_MB, D)
    beside = scatter_parts(chips, owners, TOK_MB, D) == 1
    (
        grad_mixer_part, grad_rows, gate_terms_mixer, grad_query_pre, grad_key_value, *more_parts
    ) = mixer_backward(
        grad_all, mixer_meta, row_lengths, query_full, key_value_full, output_weight,
        (*fixed, *tables), (keys, values, queries, mixture, info),
        Riders(chips, owners, later[1:], scatter=(feed_part, False) if beside else None), 6,
    )
    if not beside:
        more_parts = scatter_sum(feed_part, chips, owners, False, 30) + more_parts
    feed_sum, *more_parts = more_parts
    grad_input_parts += more_parts
    result = (second + feed_sum).astype(BF16)[:, None]
    grad_normed_mixer, *more_parts = scatter_sum(
        grad_mixer_part.reshape(mb, devices, TOK_MB, D), chips, owners, True, 40,
        [back_job(l, hc) for l in range(count)],
        [home_parts(gate_terms_mixer, True)],
        [Work(rows_mixer, grad_query_pre, BF16, l=l) for l in range(count)]
        + [
            Work(mixer_all.reshape(seqs * slots, D), grad_key_value.reshape(seqs * slots, 2 * hc), BF16)
        ]
        + [
            Work(mixture_gated, grad_rows, F32, l=l, keep=hc, slot=(l, count)) for l in range(count)
        ],
        fold=count,
    )
    query_parts, terms = more_parts[:count], more_parts[count]
    grad_output = more_parts[-2]
    grad_key_value_w = more_parts[-1]
    grad_query, grad_key_value_w = rejoin(query_parts, grad_key_value_w)
    grad_logits_mixer = gate_grads(
        own_of(gates_mixer, True), at_home(terms), attention_routes[:, 0]
    )
    grad_normed_mixer = grad_normed_mixer + product("mte,de->mtd", grad_logits_mixer, router_mixer)
    grad_tokens, grad_gain_mixer = norm_backward(
        own_tokens, inverse_mixer, gain_mixer, grad_normed_mixer
    )
    grad_tokens = (grad_tokens + grad_second).astype(BF16)[:, None]

    router_terms = [
        product("mtd,mte->de", normed.astype(BF16), logits.astype(BF16))
        for normed, logits in ((normed_mixer, grad_logits_mixer), (normed_feed, grad_logits_feed))
    ]
    last = jnp.concatenate([grad_gain_mixer[:, None], grad_gain_feed[:, None], *router_terms], axis=1)
    last = last.reshape(devices, slice_rows * 18)
    last = jnp.pad(last, ((0, 0), (0, -last.shape[1] % (8 * LANES)))).reshape(devices, -1, LANES)
    last = jnp.sum(exchange(last, chips, owners, 8), axis=0).reshape(-1)
    last = last[: slice_rows * 18].reshape(slice_rows, 18)
    grad_gains, grad_router = last[:, :2], last[:, 2:]

    grad_input = put_together(grad_input_parts, count, starts, tiles)
    return (
        result, grad_tokens, grad_gains, grad_router, grad_key_value_w, grad_query,
        grad_output, grad_input, grad_down,
    )


def solution(mesh):
    shared = P(("dp", "expert"), None)
    slots = P(None, "dp", "expert", None)
    owned = P("expert", "dp", None)
    return jax.shard_map(
        shards,
        mesh=mesh,
        in_specs=(slots, P(None, "dp"), slots, slots, shared, shared, shared) + (owned,) * 4 + (slots,),
        out_specs=(slots, slots, shared, shared, shared) + (owned,) * 4,
        check_vma=False,
    )
```
